256 devices in a mesh: seq: 64 (over x_lo, z, y), tensor: 4 (over x_hi, core).
Axes of the slice: x: 4 (x_hi: 2, x_lo: 2; x = x_hi * 2 + x_lo), y: 4, z: 8, core: 2. Of those that a mesh axis runs over, the one named last changes fastest.
Arguments:
- queries: bfloat16 [16384, 2048], P('seq', 'tensor'), may hold values from -120 to 120
- key_heads: bfloat16 [16384, 2, 128], P('seq'), may hold values from -6 to 6
- value_heads: bfloat16 [16384, 2, 128], P('seq'), may hold values from -6 to 6
- doc_lengths: int32 [8], replicated, may hold values from 1 to 8448, 16384 in all
- out_weight: bfloat16 [2048, 8192], P('tensor'), may hold values from -0.75 to 0.75
Outputs:
- projected: bfloat16 [16384, 8192], P('seq', 'tensor')
The draws below stay inside these ranges and needn't reach their ends.
Inputs may be any that keep to these rules, and one draw needn't show every extreme that they name: `doc_lengths`: they sum to 16384; the longest document has exactly 8448 tokens.
All inputs are finite; a program needn't handle non-finite values.
Results may differ from the reference program's by a relative error of at most 0.015.
Values may be sent and summed in bfloat16 or wider, within the bound.
No kernel may reach another device: no remote copies, remote signals or barrier semaphores. Data moves between devices by JAX's collectives and lax.ppermute only.
A program may use at most 192 MiB of HBM per device.

```python
import math
import jax
import jax.numpy as jnp
import numpy as np
from jax import lax

D = 8192
HD = 128
HQ = 16
KVH = 2
DOCS = 8
TOK_DEV = 256
TOKENS = 16384


def key_base(key):
    return jnp.clip(jax.random.normal(key, (TOKENS, KVH, HD), jnp.float32), -6.0, 6.0)


def draw_key_heads(key, part):
    base = key_base(key)
    return base.astype(jnp.bfloat16)


def draw_queries(key, part):
    key = jax.random.fold_in(key, 23)
    fresh = jnp.clip(jax.random.normal(key, (TOKENS, HQ, HD), jnp.float32), -6.0, 6.0)
    return fresh.reshape(TOKENS, HQ * HD).astype(jnp.bfloat16)


def strengthened(entries, own_key, source, target, parts, factor):
    def block_of(axis_at):
        return (jnp.arange(entries.shape[axis_at]) // (entries.shape[axis_at] // parts)).reshape((-1,) + (1,) * (entries.ndim - 1 - axis_at))

    first = jax.random.permutation(own_key, parts)[block_of(target)]
    far = (block_of(target) + parts // 2) % parts
    return jnp.where((block_of(source) == first) | (block_of(source) == far), factor * entries, entries)


def levels(rng, dims, pieces, least, top_value):
    def one(axis_at, shards_of):
        steps = jax.random.uniform(jax.random.fold_in(jax.random.fold_in(rng, 6), axis_at), (shards_of,), jnp.float32, least / len(pieces), top_value / len(pieces))
        return jnp.repeat(jnp.exp(steps), dims[axis_at] // shards_of).reshape((-1,) + (1,) * (len(dims) - axis_at - 1))

    level = one(*pieces[0])
    for cut in pieces[1:]:
        level = level * one(*cut)
    return level


def split_up(number_of, total, limit, lean):
    weights = [(1 << 20) // math.isqrt(standing ** lean) + 1 for standing in range(2, number_of + 1)]
    spare, holding = total - limit - (number_of - 1), [1] * (number_of - 1)
    while spare > 0:
        candidates = [i for i in range(number_of - 1) if holding[i] < limit]
        whole, left = sum([weights[i] for i in candidates]), spare
        for i in candidates:
            addition = min(limit - holding[i], max(1, left * weights[i] // whole), spare)
            holding[i] = holding[i] + addition
            spare = spare - addition
    return np.array([limit] + holding)


def ragged(key, number_of, total, reach, slope):
    if number_of == 2:
        one = jax.random.randint(key, (), max(1, total - reach), min(reach, total - 1) + 1)
        return jnp.stack([one, total - one])
    tallies = jnp.asarray(split_up(number_of, total, reach, slope), jnp.int32)
    twos = (number_of - 1) // 2
    donor, taker = tallies[1:1 + 2 * twos:2], tallies[2:2 + 2 * twos:2]
    margin = jnp.minimum(donor - 1, reach - taker)
    passed = jax.random.randint(jax.random.fold_in(key, 1), (twos,), 0, 1 << 20) % (margin + 1)
    tallies = tallies.at[1:1 + 2 * twos:2].set(donor - passed).at[2:2 + 2 * twos:2].set(taker + passed)
    return tallies[jax.random.permutation(jax.random.fold_in(key, 2), number_of)]


def scatter_about(own_key, dims, spread, most, cuts=(), kind=jnp.bfloat16):
    drawn = spread * jax.random.normal(own_key, dims, jnp.float32)
    if cuts:
        drawn = drawn * levels(own_key, dims, cuts, -0.22, 0.18)
    return jnp.clip(drawn, -most, most).astype(kind)


def bell_draw_with(rng, shape, scale, bound, pieces, heavy, kind=jnp.bfloat16):
    array = scale * jax.random.normal(rng, shape, jnp.float32)
    if pieces:
        array = array * levels(rng, shape, pieces, -0.22, 0.18)
    return jnp.clip(strengthened(array, jax.random.fold_in(rng, 3), *heavy), -bound, bound).astype(kind)


def setup_inputs(seed: int = 0) -> dict:
    keys = jax.random.split(jax.random.key(seed), 6)
    queries = draw_queries(jax.random.fold_in(keys[5], 71), 0)
    key_heads = draw_key_heads(jax.random.fold_in(keys[5], 71), 0)
    value_heads = scatter_about(keys[2], (TOKENS, KVH, HD), 1.0, 6.0, ((0, 64),))
    doc_lengths = ragged(keys[3], DOCS, TOKENS, TOKENS // 2 + TOK_DEV, 2).astype(jnp.int32)
    out_weight = bell_draw_with(keys[4], (HQ * HD, D), HD ** -0.5, 0.75, ((0, 4),), (0, 1, 4, 2.0))
    return dict(queries=queries, key_heads=key_heads, value_heads=value_heads, doc_lengths=doc_lengths, out_weight=out_weight)


theta_base = 500000.0
neg_large = -1.0e30


def rotate(values, positions):
    width = values.shape[-1]
    half_width = width // 2
    exponents = jnp.arange(half_width, dtype=jnp.float32) * (2.0 / width)
    inverse = jnp.power(jnp.float32(theta_base), -exponents)
    angles = positions[:, None] * inverse[None, :]
    cosine = jnp.cos(angles)[:, None, :]
    sine = jnp.sin(angles)[:, None, :]
    first_half = values[..., :half_width]
    second_half = values[..., half_width:]
    return jnp.concatenate([first_half * cosine - second_half * sine, second_half * cosine + first_half * sine], axis=-1)


def doc_index(positions, doc_ends):
    return jnp.sum((positions[:, None] >= doc_ends[None, :]).astype(jnp.int32), axis=1)


def reference(queries, key_heads, value_heads, doc_lengths, out_weight):
    group_size = HQ // KVH
    positions = jnp.arange(TOKENS, dtype=jnp.int32)
    pos_float = positions.astype(jnp.float32)
    doc_ends = jnp.cumsum(doc_lengths).astype(jnp.int32)
    q_rot = rotate(queries.astype(jnp.float32).reshape(TOKENS, HQ, HD), pos_float).astype(jnp.bfloat16)
    k_rot = rotate(key_heads.astype(jnp.float32), pos_float).astype(jnp.bfloat16)
    block_size = math.gcd(TOKENS, 256)
    window = min(TOKENS, TOKENS // 2 + TOK_DEV + block_size)
    score_scale = HD ** -0.5

    def one_block(block_index):
        row_start = (block_index * block_size).astype(jnp.int32)
        key_start = jnp.maximum(row_start + block_size - window, 0).astype(jnp.int32)
        q_block = lax.dynamic_slice_in_dim(q_rot, row_start, block_size, 0).astype(jnp.float32)
        key_block = lax.dynamic_slice_in_dim(k_rot, key_start, window, 0).astype(jnp.float32)
        val_block = lax.dynamic_slice_in_dim(value_heads, key_start, window, 0).astype(jnp.float32)
        query_pos = row_start + jnp.arange(block_size, dtype=jnp.int32)
        key_pos = key_start + jnp.arange(window, dtype=jnp.int32)
        live = (doc_index(key_pos, doc_ends)[None, :] == doc_index(query_pos, doc_ends)[:, None]) & (key_pos[None, :] <= query_pos[:, None])
        outputs = []
        for group_index in range(KVH):
            heads_q = q_block[:, group_index * group_size:(group_index + 1) * group_size]
            scores = jnp.einsum('qhd,kd->hqk', heads_q, key_block[:, group_index], precision=lax.Precision.HIGHEST) * score_scale
            scores = jnp.where(live[None], scores, neg_large)
            peak = jnp.max(scores, axis=-1, keepdims=True)
            weights = jnp.where(live[None], jnp.exp(scores - peak), 0.0)
            denom = jnp.sum(weights, axis=-1, keepdims=True)
            weights_bf = weights.astype(jnp.bfloat16).astype(jnp.float32)
            summed = jnp.einsum('hqk,kd->hqd', weights_bf, val_block[:, group_index], precision=lax.Precision.HIGHEST)
            outputs.append(summed / denom)
        heads_out = jnp.concatenate(outputs, axis=0)
        return jnp.transpose(heads_out, (1, 0, 2)).reshape(block_size, HQ * HD).astype(jnp.bfloat16)

    blocks = lax.map(one_block, jnp.arange(TOKENS // block_size, dtype=jnp.int32))
    attended = blocks.reshape(TOKENS, HQ * HD)
    return jnp.dot(attended, out_weight, preferred_element_type=jnp.float32).astype(jnp.bfloat16)
```

```python
import functools
import math

import jax
import jax.numpy as jnp
from jax import lax
from jax.experimental import pallas as pl
from jax.experimental.pallas import tpu as pltpu
from jax.sharding import PartitionSpec as P

HQ = 16
KVH = 2
HD = 128
SEQ = 64
TENSOR = 4
ROW = 4
THETA = 500000.0
EMPTY = -1e30
MASKED = -2e30
LOG2E = math.log2(math.e)
BLOCK = 256
ROW_TOKENS = ROW * BLOCK
HEADS = 8
LANES = HEADS * BLOCK
STATE = HD + 8
MIB = 1024 * 1024


def device_perm(move):
    pairs = []
    for s in range(SEQ):
        for hi in range(2):
            for core in range(2):
                to = move(s, hi, core)
                if to is not None:
                    pairs.append((s * TENSOR + hi * 2 + core, to[0] * TENSOR + to[1] * 2 + to[2]))
    return pairs


def permute(x, move):
    return lax.ppermute(x, ("seq", "tensor"), device_perm(move))


def in_row(shift):
    return lambda s, hi, core: (s - s % ROW + (s + shift) % ROW, hi, core)


def other_core(s, hi, core):
    return s, hi, 1 - core


def other_hi(s, hi, core):
    return s, 1 - hi, core


def far_block(s, hi, core):
    if core == 0 and s % ROW == ROW - 1 and s + 33 < SEQ:
        return s + 33, hi, core
    return None


def first_hop(s, hi, core):
    if core == 0:
        return (s + ROW, hi, core) if s + ROW < SEQ else None
    return (s + SEQ // 2) % SEQ, hi, core


def next_hop(s, hi, core):
    if core == 0:
        return (s + ROW, hi, core) if s + ROW < SEQ else None
    return (s - ROW) % SEQ, hi, core


def rope_tables(positions):
    half = HD // 2
    exponents = jnp.arange(half, dtype=jnp.float32) * (2.0 / HD)
    inverse = jnp.power(jnp.float32(THETA), -exponents)
    angles = positions.astype(jnp.float32)[:, None] * inverse[None, :]
    return jnp.cos(angles), jnp.sin(angles)


def rope(values, cosine, sine):
    half = HD // 2
    first, second = values[..., :half], values[..., half:]
    return jnp.concatenate(
        [first * cosine - second * sine, second * cosine + first * sine], axis=-1
    )


def attend_kernel(scalars, q_ref, bounds_ref, kv_ref, state_in, state):
    mode = scalars[5]
    scale = HD**-0.5 * LOG2E
    keys = kv_ref.shape[0]

    def head(h, masked):
        lanes = pl.ds(pl.multiple_of(h * BLOCK, BLOCK), BLOCK)
        s = jnp.dot(kv_ref[:, :HD], q_ref[:, lanes], preferred_element_type=jnp.float32) * scale
        if masked:
            low = bounds_ref[0:1, :]
            high = jnp.minimum(bounds_ref[1:2, :], scalars[4] - 1)
            parts = []
            for b in range(keys // BLOCK):
                at = lax.broadcasted_iota(jnp.int32, (BLOCK, BLOCK), 0) + scalars[b]
                part = s[b * BLOCK : (b + 1) * BLOCK]
                parts.append(jnp.where((at >= low) & (at <= high), part, MASKED))
            s = jnp.concatenate(parts, axis=0)
        old = state_in[HD : HD + 1, lanes]
        new = jnp.maximum(old, jnp.max(s, axis=0, keepdims=True))
        weights = jnp.exp2(s - new)
        alpha = jnp.exp2(old - new)
        summed = lax.dot_general(
            kv_ref[:, HD:],
            weights.astype(jnp.bfloat16),
            (((0,), (0,)), ((), ())),
            preferred_element_type=jnp.float32,
        )
        state[:HD, lanes] = state_in[:HD, lanes] * alpha + summed
        denom = state_in[HD + 1 : HD + 2, lanes] * alpha + jnp.sum(weights, axis=0, keepdims=True)
        state[HD : HD + 8, lanes] = jnp.concatenate(
            [new, denom, jnp.zeros((6, BLOCK), jnp.float32)], axis=0
        )

    @pl.when(mode == 0)
    def _():
        state[...] = state_in[...]

    @pl.when(mode == 1)
    def _():
        lax.fori_loop(0, HEADS // 2, lambda i, c: (head(2 * i, False), head(2 * i + 1, False), c)[2], 0)

    @pl.when(mode == 2)
    def _():
        lax.fori_loop(0, HEADS, lambda h, c: (head(h, True), c)[1], 0)


def attend(scalars, q_all, bounds, kv, state):
    return pl.pallas_call(
        attend_kernel,
        out_shape=jax.ShapeDtypeStruct((STATE, LANES), jnp.float32),
        in_specs=[pl.BlockSpec(memory_space=pltpu.SMEM)] + [pl.BlockSpec(memory_space=pltpu.VMEM)] * 4,
        out_specs=pl.BlockSpec(memory_space=pltpu.VMEM),
        input_output_aliases={4: 0},
        compiler_params=pltpu.CompilerParams(vmem_limit_bytes=24 * MIB),
        cost_estimate=pl.CostEstimate(
            flops=4 * LANES * ROW_TOKENS * HD,
            bytes_accessed=3 * MIB,
            transcendentals=LANES * ROW_TOKENS,
        ),
        name="attend",
    )(scalars, q_all, bounds, kv, state)


def merge_kernel(mine, theirs, out):
    for h in range(HEADS):
        a = slice(h * BLOCK, (h + 1) * BLOCK)
        g = (h + HEADS // 2) % HEADS
        b = slice(g * BLOCK, (g + 1) * BLOCK)
        peak_a, peak_b = mine[HD : HD + 1, a], theirs[HD : HD + 1, b]
        peak = jnp.maximum(peak_a, peak_b)
        scale_a, scale_b = jnp.exp2(peak_a - peak), jnp.exp2(peak_b - peak)
        denom = mine[HD + 1 : HD + 2, a] * scale_a + theirs[HD + 1 : HD + 2, b] * scale_b
        summed = mine[:HD, a] * scale_a + theirs[:HD, b] * scale_b
        out[:, h * HD : (h + 1) * HD] = (summed / denom).T.astype(jnp.bfloat16)


def merge(mine, theirs):
    return pl.pallas_call(
        merge_kernel,
        out_shape=jax.ShapeDtypeStruct((BLOCK, HEADS * HD), jnp.bfloat16),
        in_specs=[pl.BlockSpec(memory_space=pltpu.VMEM)] * 2,
        out_specs=pl.BlockSpec(memory_space=pltpu.VMEM),
        compiler_params=pltpu.CompilerParams(vmem_limit_bytes=24 * MIB),
        cost_estimate=pl.CostEstimate(flops=8 * LANES * HD, bytes_accessed=3 * MIB, transcendentals=0),
        name="merge",
    )(mine, theirs)


def project_kernel(with_received, start, attended, own_weight, other_weight, *rest):
    half = HEADS * HD // 2
    total = jnp.dot(attended[:, :half], own_weight[...], preferred_element_type=jnp.float32)
    total += jnp.dot(attended[:, half:], other_weight[...], preferred_element_type=jnp.float32)
    if with_received:
        total += rest[0][...].astype(jnp.float32)
    rest[-1][...] = total.astype(jnp.bfloat16)


def project(start, attended, own_weight, other_weight, columns, received=None, tile=512):
    half = HEADS * HD // 2
    in_specs = [
        pl.BlockSpec((BLOCK, 2 * half), lambda j, at: (0, 0)),
        pl.BlockSpec((half, tile), lambda j, at: (0, at[0] + j)),
        pl.BlockSpec((half, tile), lambda j, at: (0, at[0] + j)),
    ]
    operands = [attended, own_weight, other_weight]
    if received is not None:
        in_specs.append(pl.BlockSpec((BLOCK, tile), lambda j, at: (0, j)))
        operands.append(received)
    return pl.pallas_call(
        functools.partial(project_kernel, received is not None),
        out_shape=jax.ShapeDtypeStruct((BLOCK, columns), jnp.bfloat16),
        grid_spec=pltpu.PrefetchScalarGridSpec(
            num_scalar_prefetch=1,
            grid=(columns // tile,),
            in_specs=in_specs,
            out_specs=pl.BlockSpec((BLOCK, tile), lambda j, at: (0, j)),
        ),
        compiler_params=pltpu.CompilerParams(vmem_limit_bytes=24 * MIB),
        cost_estimate=pl.CostEstimate(
            flops=2 * BLOCK * 2 * half * columns,
            bytes_accessed=2 * half * 2 * columns + 2 * BLOCK * columns,
            transcendentals=0,
        ),
        name="project",
    )(start, *operands)


def body(queries, key_heads, value_heads, doc_lengths, out_weight):
    s = lax.axis_index("seq")
    t = lax.axis_index("tensor")
    hi, core = t // 2, t % 2
    row, col = s // ROW, s % ROW

    query_pos = s * BLOCK + jnp.arange(BLOCK, dtype=jnp.int32)
    cosine, sine = rope_tables(query_pos)
    own_key = lax.dynamic_index_in_dim(key_heads, hi, 1, keepdims=False).astype(jnp.float32)
    own_key = rope(own_key, cosine, sine).astype(jnp.bfloat16)
    own_value = lax.dynamic_index_in_dim(value_heads, hi, 1, keepdims=False)
    block = jnp.concatenate([own_key, own_value], axis=1)

    up, down, across = (permute(block, in_row(shift)) for shift in (1, -1, 2))
    far = permute(block, far_block)
    offsets = jnp.array([0, -1, 1, 2], jnp.int32)
    kv_row = jnp.concatenate([block, up, down, across], axis=0)

    heads = queries.shape[1] // HD
    q_rot = rope(
        queries.astype(jnp.float32).reshape(BLOCK, heads, HD), cosine[:, None], sine[:, None]
    ).astype(jnp.bfloat16)
    q_own = jnp.transpose(q_rot, (2, 1, 0)).reshape(HD, heads * BLOCK)
    q_all = jnp.concatenate([q_own, permute(q_own, other_core)], axis=1)
    other_weight = permute(out_weight, other_core)

    doc_ends = jnp.cumsum(doc_lengths)
    low = jnp.max(
        jnp.where(doc_ends[None, :] <= query_pos[:, None], doc_ends[None, :], 0), axis=1
    )
    low_first = jnp.max(jnp.where(doc_ends <= s * BLOCK, doc_ends, 0))
    low_last = jnp.max(jnp.where(doc_ends <= s * BLOCK + BLOCK - 1, doc_ends, 0))
    bounds = jnp.concatenate(
        [low[None], query_pos[None], jnp.zeros((6, BLOCK), jnp.int32)], axis=0
    )

    def scalars_of(bases, first, end):
        none = (low_first >= end) | (first > s * BLOCK + BLOCK - 1) | (end <= 0)
        whole = (low_last <= first) & (end <= s * BLOCK) & (end - first == ROW_TOKENS)
        mode = jnp.where(none, 0, jnp.where(whole, 1, 2))
        return jnp.concatenate([bases, jnp.stack([end, mode, 0, 0])]).astype(jnp.int32)

    def row_scalars(index):
        bases = (index * ROW + (col + offsets) % ROW) * BLOCK
        return scalars_of(bases, index * ROW_TOKENS, (index + 1) * ROW_TOKENS)

    far_first = (s - 33) * BLOCK
    far_end = jnp.where(col == 0, far_first + BLOCK, 0)
    far_scalars = scalars_of(
        far_first + jnp.arange(ROW, dtype=jnp.int32) * BLOCK, far_first, far_end
    )
    far_padded = jnp.concatenate([far, jnp.zeros((ROW_TOKENS - BLOCK, 2 * HD), far.dtype)], axis=0)

    empty = jnp.concatenate(
        [
            jnp.zeros((HD, LANES), jnp.float32),
            jnp.full((1, LANES), EMPTY, jnp.float32),
            jnp.zeros((7, LANES), jnp.float32),
        ],
        axis=0,
    )
    travelling = permute(kv_row, first_hop)
    state = attend(
        jnp.where(core == 0, far_scalars, row_scalars(row)),
        q_all,
        bounds,
        jnp.where(core == 0, far_padded, kv_row),
        empty,
    )
    for step in range(1, 5):
        held = travelling
        if step < 4:
            travelling = permute(held, next_hop)
        index = jnp.where(core == 0, row - step, row - 9 + step)
        state = attend(row_scalars(index), q_all, bounds, held, state)

    attended = merge(state, permute(state, other_core))

    columns = out_weight.shape[1] // TENSOR
    tile = 512
    part = columns // 2
    send_at = (2 * (1 - hi) + core) * (columns // tile)
    keep_at = (2 * hi + core) * (columns // tile)
    received = []
    for i in range(2):
        at = (send_at + i * (part // tile)).astype(jnp.int32).reshape(1)
        partial = project(at, attended, out_weight, other_weight, part)
        received.append(permute(partial, other_hi))
    out = []
    for i in range(2):
        at = (keep_at + i * (part // tile)).astype(jnp.int32).reshape(1)
        out.append(project(at, attended, out_weight, other_weight, part, received[i]))
    return jnp.concatenate(out, axis=1)


def solution(mesh):
    return jax.shard_map(
        body,
        mesh=mesh,
        in_specs=(
            P("seq", "tensor"),
            P("seq", None, None),
            P("seq", None, None),
            P(),
            P("tensor", None),
        ),
        out_specs=P("seq", "tensor"),
        check_vma=False,
    )
```

```python
import functools
import math

import jax
import jax.numpy as jnp
from jax import lax
from jax.experimental import pallas as pl
from jax.experimental.pallas import tpu as pltpu
from jax.sharding import PartitionSpec as P

HQ = 16
KVH = 2
HD = 128
SEQ = 64
TENSOR = 4
ROW = 4
THETA = 500000.0
EMPTY = -1e30
MASKED = -1e32
LOG2E = math.log2(math.e)
BLOCK = 256
ROW_TOKENS = ROW * BLOCK
HEADS = 8
LANES = HEADS * BLOCK
STATE = HD + 8
TILE = 256
MIB = 1024 * 1024


def device_perm(move):
    pairs = []
    for s in range(SEQ):
        for hi in range(2):
            for core in range(2):
                to = move(s, hi, core)
                if to is not None:
                    pairs.append((s * TENSOR + hi * 2 + core, to[0] * TENSOR + to[1] * 2 + to[2]))
    return pairs


def permute(x, move):
    return lax.ppermute(x, ("seq", "tensor"), device_perm(move))


def in_row(shift):
    return lambda s, hi, core: (s - s % ROW + (s + shift) % ROW, hi, core)


def other_core(s, hi, core):
    return s, hi, 1 - core


def other_hi(s, hi, core):
    return s, 1 - hi, core


def far_block(s, hi, core):
    if core == 0 and s % ROW == ROW - 1 and s + 33 < SEQ:
        return s + 33, hi, core
    return None


def first_hop(s, hi, core):
    if core == 0:
        return (s + ROW, hi, core) if s + ROW < SEQ else None
    return (s + SEQ // 2) % SEQ, hi, core


def next_hop(s, hi, core):
    if core == 0:
        return (s + ROW, hi, core) if s + ROW < SEQ else None
    return (s - ROW) % SEQ, hi, core


def rope_tables(positions):
    half = HD // 2
    exponents = jnp.arange(half, dtype=jnp.float32) * (2.0 / HD)
    inverse = jnp.power(jnp.float32(THETA), -exponents)
    angles = positions.astype(jnp.float32)[:, None] * inverse[None, :]
    return jnp.cos(angles), jnp.sin(angles)


def rope(values, cosine, sine):
    half = HD // 2
    first, second = values[..., :half], values[..., half:]
    return jnp.concatenate(
        [first * cosine - second * sine, second * cosine + first * sine], axis=-1
    )


def live_only(s, base_refs, bounds, end):
    low = bounds[0:1, :]
    high = jnp.minimum(bounds[1:2, :], end - 1)
    parts = []
    for b, base in enumerate(base_refs):
        part = s[b * BLOCK : (b + 1) * BLOCK]
        at = lax.broadcasted_iota(jnp.int32, part.shape, 0) + base
        parts.append(jnp.where((at >= low) & (at <= high), part, MASKED))
    return jnp.concatenate(parts, axis=0) if len(parts) > 1 else parts[0]


def update(state, kept, q, kvs, mask):
    scale = HD**-0.5 * LOG2E
    scores = [jnp.dot(kv[:, :HD], q, preferred_element_type=jnp.float32) for kv in kvs]
    s = mask(jnp.concatenate(scores, axis=0) if len(scores) > 1 else scores[0])
    peak = jnp.max(s, axis=0, keepdims=True) * scale
    old = jnp.full_like(peak, EMPTY) if kept is None else kept[HD : HD + 1, :]
    new = jnp.maximum(old, peak)
    weights = jnp.exp2(s * scale - new).astype(jnp.bfloat16)
    values = jnp.concatenate([kv[:, HD:] for kv in kvs], axis=0) if len(kvs) > 1 else kvs[0][:, HD:]
    values = jnp.concatenate([values.T, jnp.ones((16, values.shape[0]), jnp.bfloat16)], axis=0)
    summed = jnp.dot(values, weights, preferred_element_type=jnp.float32)
    denom = summed[HD : HD + 1]
    summed = summed[:HD]
    if kept is not None:
        alpha = jnp.exp2(old - new)
        summed = summed + kept[:HD, :] * alpha
        denom = denom + kept[HD + 1 : HD + 2, :] * alpha
    state[:HD, :] = summed
    state[HD:, :] = jnp.concatenate([new, denom, jnp.zeros((6, LANES), jnp.float32)], axis=0)


def first_kernel(scalars, q_ref, bounds, far, kv_a, kv_b, state):
    mode = scalars[5]

    @pl.when(mode == 0)
    def _():
        state[:HD, :] = jnp.zeros((HD, LANES), jnp.float32)
        state[HD:, :] = jnp.concatenate(
            [jnp.full((1, LANES), EMPTY, jnp.float32), jnp.zeros((7, LANES), jnp.float32)], axis=0
        )

    @pl.when(mode == 1)
    def _():
        mask = lambda s: live_only(s, [scalars[0]], bounds, scalars[4])
        update(state, None, q_ref[...], [far[...]], mask)

    @pl.when(mode == 2)
    def _():
        mask = lambda s: live_only(s, [scalars[i] for i in range(ROW)], bounds, scalars[4])
        update(state, None, q_ref[...], [kv_a[...], kv_b[...]], mask)


def next_kernel(scalars, q_ref, bounds, kv_a, kv_b, kept, state):
    mode = scalars[5]

    @pl.when(mode == 0)
    def _():
        state[...] = kept[...]

    @pl.when(mode == 1)
    def _():
        update(state, kept, q_ref[...], [kv_a[...], kv_b[...]], lambda s: s)

    @pl.when(mode == 2)
    def _():
        mask = lambda s: live_only(s, [scalars[i] for i in range(ROW)], bounds, scalars[4])
        update(state, kept, q_ref[...], [kv_a[...], kv_b[...]], mask)


def attend(kernel, aliases, name, scalars, *operands):
    return pl.pallas_call(
        kernel,
        out_shape=jax.ShapeDtypeStruct((STATE, LANES), jnp.float32),
        in_specs=[pl.BlockSpec(memory_space=pltpu.SMEM)]
        + [pl.BlockSpec(memory_space=pltpu.VMEM)] * len(operands),
        out_specs=pl.BlockSpec(memory_space=pltpu.VMEM),
        input_output_aliases=aliases,
        compiler_params=pltpu.CompilerParams(vmem_limit_bytes=32 * MIB),
        cost_estimate=pl.CostEstimate(
            flops=4 * LANES * ROW_TOKENS * HD,
            bytes_accessed=3 * MIB,
            transcendentals=LANES * ROW_TOKENS,
        ),
        name=name,
    )(scalars, *operands)


def merge_kernel(mine, theirs, out):
    for h in range(HEADS):
        a = slice(h * BLOCK, (h + 1) * BLOCK)
        g = (h + HEADS // 2) % HEADS
        b = slice(g * BLOCK, (g + 1) * BLOCK)
        peak_a, peak_b = mine[HD : HD + 1, a], theirs[HD : HD + 1, b]
        peak = jnp.maximum(peak_a, peak_b)
        scale_a, scale_b = jnp.exp2(peak_a - peak), jnp.exp2(peak_b - peak)
        denom = mine[HD + 1 : HD + 2, a] * scale_a + theirs[HD + 1 : HD + 2, b] * scale_b
        summed = mine[:HD, a] * scale_a + theirs[:HD, b] * scale_b
        out[:, h * HD : (h + 1) * HD] = (summed / denom).T.astype(jnp.bfloat16)


def merge(mine, theirs):
    return pl.pallas_call(
        merge_kernel,
        out_shape=jax.ShapeDtypeStruct((BLOCK, HEADS * HD), jnp.bfloat16),
        in_specs=[pl.BlockSpec(memory_space=pltpu.VMEM)] * 2,
        out_specs=pl.BlockSpec(memory_space=pltpu.VMEM),
        compiler_params=pltpu.CompilerParams(vmem_limit_bytes=24 * MIB),
        cost_estimate=pl.CostEstimate(flops=8 * LANES * HD, bytes_accessed=3 * MIB, transcendentals=0),
        name="merge",
    )(mine, theirs)


def project_kernel(start, attended, own_weight, other_weight, out):
    half = HEADS * HD // 2
    total = jnp.dot(attended[:, :half], own_weight[...], preferred_element_type=jnp.float32)
    total += jnp.dot(attended[:, half:], other_weight[...], preferred_element_type=jnp.float32)
    out[...] = total.astype(out.dtype)


def project(start, attended, own_weight, other_weight, columns, dtype):
    half = HEADS * HD // 2
    return pl.pallas_call(
        project_kernel,
        out_shape=jax.ShapeDtypeStruct((BLOCK, columns), dtype),
        grid_spec=pltpu.PrefetchScalarGridSpec(
            num_scalar_prefetch=1,
            grid=(columns // TILE,),
            in_specs=[
                pl.BlockSpec((BLOCK, 2 * half), lambda j, at: (0, 0)),
                pl.BlockSpec((half, TILE), lambda j, at: (0, at[0] + j)),
                pl.BlockSpec((half, TILE), lambda j, at: (0, at[0] + j)),
            ],
            out_specs=pl.BlockSpec((BLOCK, TILE), lambda j, at: (0, j)),
        ),
        compiler_params=pltpu.CompilerParams(vmem_limit_bytes=60 * MIB),
        cost_estimate=pl.CostEstimate(
            flops=2 * BLOCK * 2 * half * columns,
            bytes_accessed=2 * half * 2 * columns + 2 * BLOCK * columns,
            transcendentals=0,
        ),
        name="project",
    )(start, attended, own_weight, other_weight)


def finish_kernel(kept, received, *rest):
    rest[-1][...] = (kept[...] + received[...].astype(jnp.float32)).astype(jnp.bfloat16)


def finish(kept, received, first, out):
    columns, start = received.shape[1], first // TILE
    tile = pl.BlockSpec((BLOCK, TILE), lambda j: (0, start + j))
    in_specs = [tile, pl.BlockSpec((BLOCK, TILE), lambda j: (0, j))]
    operands = [kept, received]
    if out is not None:
        in_specs.append(pl.BlockSpec(memory_space=pl.ANY))
        operands.append(out)
    return pl.pallas_call(
        finish_kernel,
        out_shape=jax.ShapeDtypeStruct(kept.shape, jnp.bfloat16),
        grid=(columns // TILE,),
        in_specs=in_specs,
        out_specs=tile,
        input_output_aliases={} if out is None else {2: 0},
        compiler_params=pltpu.CompilerParams(vmem_limit_bytes=32 * MIB),
        cost_estimate=pl.CostEstimate(
            flops=BLOCK * columns, bytes_accessed=8 * BLOCK * columns, transcendentals=0
        ),
        name="finish",
    )(*operands)


def body(queries, key_heads, value_heads, doc_lengths, out_weight):
    s = lax.axis_index("seq")
    t = lax.axis_index("tensor")
    hi, core = t // 2, t % 2
    row, col = s // ROW, s % ROW

    query_pos = s * BLOCK + jnp.arange(BLOCK, dtype=jnp.int32)
    cosine, sine = rope_tables(query_pos)
    own_key = lax.dynamic_index_in_dim(key_heads, hi, 1, keepdims=False).astype(jnp.float32)
    own_key = rope(own_key, cosine, sine).astype(jnp.bfloat16)
    own_value = lax.dynamic_index_in_dim(value_heads, hi, 1, keepdims=False)
    block = jnp.concatenate([own_key, own_value], axis=1)

    up, down, across = (permute(block, in_row(shift)) for shift in (1, -1, 2))
    far = permute(block, far_block)
    offsets = jnp.array([0, -1, 1, 2], jnp.int32)
    own_a = jnp.concatenate([block, up], axis=0)
    own_b = jnp.concatenate([down, across], axis=0)

    heads = queries.shape[1] // HD
    q_rot = rope(
        queries.astype(jnp.float32).reshape(BLOCK, heads, HD), cosine[:, None], sine[:, None]
    ).astype(jnp.bfloat16)
    q_own = jnp.transpose(q_rot, (2, 1, 0)).reshape(HD, heads * BLOCK)
    q_all = jnp.concatenate([q_own, permute(q_own, other_core)], axis=1)
    other_weight = permute(out_weight, other_core)

    doc_ends = jnp.cumsum(doc_lengths)
    low = jnp.max(
        jnp.where(doc_ends[None, :] <= query_pos[:, None], doc_ends[None, :], 0), axis=1
    )
    low_first = jnp.max(jnp.where(doc_ends <= s * BLOCK, doc_ends, 0))
    low_last = jnp.max(jnp.where(doc_ends <= s * BLOCK + BLOCK - 1, doc_ends, 0))
    bounds = jnp.tile(
        jnp.concatenate([low[None], query_pos[None], jnp.zeros((6, BLOCK), jnp.int32)], axis=0),
        (1, HEADS),
    )

    def pack(bases, end, mode):
        return jnp.concatenate([bases, jnp.stack([end, mode, 0, 0])]).astype(jnp.int32)

    def row_scalars(index):
        first, end = index * ROW_TOKENS, (index + 1) * ROW_TOKENS
        none = (low_first >= end) | (index < 0)
        whole = (low_last <= first) & (end <= s * BLOCK)
        bases = (index * ROW + (col + offsets) % ROW) * BLOCK
        return pack(bases, end, jnp.where(none, 0, jnp.where(whole, 1, 2)))

    far_first = (s - 33) * BLOCK
    far_live = (col == 0) & (far_first >= 0) & (low_first < far_first + BLOCK)
    far_scalars = pack(
        far_first + jnp.arange(ROW, dtype=jnp.int32) * BLOCK,
        far_first + BLOCK,
        jnp.where(far_live, 1, 0),
    )
    own_scalars = pack(
        (row * ROW + (col + offsets) % ROW) * BLOCK, (row + 1) * ROW_TOKENS, jnp.int32(2)
    )

    a = permute(own_a, first_hop)
    b = permute(own_b, first_hop)
    state = attend(
        first_kernel,
        {},
        "attend_first",
        jnp.where(core == 0, far_scalars, own_scalars),
        q_all,
        bounds,
        far,
        own_a,
        own_b,
    )
    for step in range(1, 5):
        a, state = lax.optimization_barrier((a, state))
        held_a, held_b = a, b
        if step < 4:
            a = permute(held_a, next_hop)
            b = permute(held_b, next_hop)
        index = jnp.where(core == 0, row - step, row - 9 + step)
        state = attend(
            next_kernel, {5: 0}, "attend", row_scalars(index), q_all, bounds, held_a, held_b, state
        )

    attended = merge(state, permute(state, other_core))

    columns = out_weight.shape[1] // TENSOR
    send_at = (2 * (1 - hi) + core) * (columns // TILE)
    keep_at = ((2 * hi + core) * (columns // TILE)).astype(jnp.int32).reshape(1)
    pieces = ((0, 512), (512, 1024), (1536, 512))
    received = []
    for first, width in pieces:
        at = (send_at + first // TILE).astype(jnp.int32).reshape(1)
        partial = project(at, attended, out_weight, other_weight, width, jnp.bfloat16)
        received.append(permute(partial, other_hi))
    kept = project(keep_at, attended, out_weight, other_weight, columns, jnp.float32)
    out = None
    for (first, _), piece in zip(pieces, received):
        out = finish(kept, piece, first, out)
    return out


def solution(mesh):
    return jax.shard_map(
        body,
        mesh=mesh,
        in_specs=(
            P("seq", "tensor"),
            P("seq", None, None),
            P("seq", None, None),
            P(),
            P("tensor", None),
        ),
        out_specs=P("seq", "tensor"),
        check_vma=False,
    )
```

```python
import functools
import math

import jax
import jax.numpy as jnp
from jax import lax
from jax.experimental import pallas as pl
from jax.experimental.pallas import tpu as pltpu
from jax.sharding import PartitionSpec as P

HQ = 16
KVH = 2
HD = 128
SEQ = 64
TENSOR = 4
ROW = 4
THETA = 500000.0
EMPTY = -1e30
MASKED = -1e32
LOG2E = math.log2(math.e)
BLOCK = 256
ROW_TOKENS = ROW * BLOCK
HEADS = 8
LANES = HEADS * BLOCK
STATE = HD + 8
TILE = 512
WIDE = 1024
NOWHERE = 1 << 24
MIB = 1024 * 1024


def device_perm(move):
    pairs = []
    for s in range(SEQ):
        for hi in range(2):
            for core in range(2):
                to = move(s, hi, core)
                if to is not None:
                    pairs.append((s * TENSOR + hi * 2 + core, to[0] * TENSOR + to[1] * 2 + to[2]))
    return pairs


def permute(x, move):
    return lax.ppermute(x, ("seq", "tensor"), device_perm(move))


def in_row(shift):
    return lambda s, hi, core: (s - s % ROW + (s + shift) % ROW, hi, core)


def other_core(s, hi, core):
    return s, hi, 1 - core


def other_hi(s, hi, core):
    return s, 1 - hi, core


def far_block(s, hi, core):
    if core == 0 and s % ROW == ROW - 1 and s + 33 < SEQ:
        return s + 33, hi, core
    return None


def along_rows(step):
    def move(s, hi, core):
        if core == 0:
            return (s + step * ROW, hi, core) if s + step * ROW < SEQ else None
        return (s + (9 - step) * ROW) % SEQ, hi, core

    return move


def rope_tables(positions):
    half = HD // 2
    exponents = jnp.arange(half, dtype=jnp.float32) * (2.0 / HD)
    inverse = jnp.power(jnp.float32(THETA), -exponents)
    angles = positions.astype(jnp.float32)[:, None] * inverse[None, :]
    return jnp.cos(angles), jnp.sin(angles)


def rope(values, cosine, sine):
    half = HD // 2
    first, second = values[..., :half], values[..., half:]
    return jnp.concatenate(
        [first * cosine - second * sine, second * cosine + first * sine], axis=-1
    )


def attend_kernel(sizes, fresh, scalars, q_ref, bounds, *rest):
    state = rest[-1]
    kept, refs = (None, rest[:-1]) if fresh else (rest[-2], rest[:-2])
    parts = []
    for ref in refs:
        at = 0
        while at < ref.shape[0]:
            size = sizes[len(parts)]
            parts.append(ref.at[at : at + size])
            at += size
    scale = HD**-0.5 * LOG2E
    mode = scalars[0]

    def step(lanes, masked):
        q = q_ref[:, lanes]
        scores = []
        for i, part in enumerate(parts):
            s = jnp.dot(part[:, :HD], q, preferred_element_type=jnp.float32)
            if masked:
                at = lax.broadcasted_iota(jnp.int32, s.shape, 0) + scalars[1 + i]
                live = (at >= bounds[0:1, lanes]) & (at <= bounds[1:2, lanes])
                s = jnp.where(live, s, MASKED)
            scores.append(s)
        s = jnp.concatenate(scores, axis=0) if len(scores) > 1 else scores[0]
        values = [part[:, HD:].T for part in parts]
        values = jnp.concatenate(values, axis=1) if len(values) > 1 else values[0]
        values = jnp.concatenate([values, jnp.ones((16, values.shape[1]), jnp.bfloat16)], axis=0)
        peak = jnp.max(s, axis=0, keepdims=True) * scale
        old = jnp.full_like(peak, EMPTY) if fresh else kept[HD : HD + 1, lanes]
        new = jnp.maximum(old, peak)
        weights = jnp.exp2(s * scale - new).astype(jnp.bfloat16)
        summed = jnp.dot(values, weights, preferred_element_type=jnp.float32)
        denom = summed[HD : HD + 1]
        summed = summed[:HD]
        if not fresh:
            alpha = jnp.exp2(old - new)
            summed = summed + kept[:HD, lanes] * alpha
            denom = denom + kept[HD + 1 : HD + 2, lanes] * alpha
        state[:HD, lanes] = summed
        state[HD:, lanes] = jnp.concatenate([new, denom, jnp.zeros((6, WIDE), jnp.float32)], axis=0)

    def steps(masked):
        def one(i, carry):
            step(pl.ds(pl.multiple_of(i * WIDE, WIDE), WIDE), masked)
            return carry

        lax.fori_loop(0, LANES // WIDE, one, 0)

    @pl.when(mode == 0)
    def _():
        if fresh:
            state[:HD, :] = jnp.zeros((HD, LANES), jnp.float32)
            state[HD:, :] = jnp.concatenate(
                [jnp.full((1, LANES), EMPTY, jnp.float32), jnp.zeros((7, LANES), jnp.float32)],
                axis=0,
            )
        else:
            state[...] = kept[...]

    if not fresh:

        @pl.when(mode == 1)
        def _():
            steps(False)

    @pl.when(mode == 2)
    def _():
        steps(True)


def attend(scalars, q_all, bounds, parts, state=None, sizes=None):
    sizes = tuple(sizes or [part.shape[0] for part in parts])
    operands = list(parts) + ([] if state is None else [state])
    return pl.pallas_call(
        functools.partial(attend_kernel, sizes, state is None),
        out_shape=jax.ShapeDtypeStruct((STATE, LANES), jnp.float32),
        in_specs=[pl.BlockSpec(memory_space=pltpu.SMEM)]
        + [pl.BlockSpec(memory_space=pltpu.VMEM)] * (2 + len(operands)),
        out_specs=pl.BlockSpec(memory_space=pltpu.VMEM),
        input_output_aliases={} if state is None else {2 + len(operands): 0},
        compiler_params=pltpu.CompilerParams(vmem_limit_bytes=32 * MIB),
        cost_estimate=pl.CostEstimate(flops=1, bytes_accessed=1, transcendentals=0),
        name="attend",
    )(scalars, q_all, bounds, *operands)


def merge_kernel(mine, theirs, out):
    for h in range(HEADS):
        a = slice(h * BLOCK, (h + 1) * BLOCK)
        g = (h + HEADS // 2) % HEADS
        b = slice(g * BLOCK, (g + 1) * BLOCK)
        peak_a, peak_b = mine[HD : HD + 1, a], theirs[HD : HD + 1, b]
        peak = jnp.maximum(peak_a, peak_b)
        scale_a, scale_b = jnp.exp2(peak_a - peak), jnp.exp2(peak_b - peak)
        denom = mine[HD + 1 : HD + 2, a] * scale_a + theirs[HD + 1 : HD + 2, b] * scale_b
        summed = mine[:HD, a] * scale_a + theirs[:HD, b] * scale_b
        out[:, h * HD : (h + 1) * HD] = (summed / denom).T.astype(jnp.bfloat16)


def merge(mine, theirs):
    return pl.pallas_call(
        merge_kernel,
        out_shape=jax.ShapeDtypeStruct((BLOCK, HEADS * HD), jnp.bfloat16),
        in_specs=[pl.BlockSpec(memory_space=pltpu.VMEM)] * 2,
        out_specs=pl.BlockSpec(memory_space=pltpu.VMEM),
        compiler_params=pltpu.CompilerParams(vmem_limit_bytes=24 * MIB),
        cost_estimate=pl.CostEstimate(flops=8 * LANES * HD, bytes_accessed=3 * MIB, transcendentals=0),
        name="merge",
    )(mine, theirs)


def project_kernel(first, attended, own_weight, other_weight, out):
    half = HEADS * HD // 2
    columns = slice(first, first + out.shape[1])
    total = jnp.dot(attended[:, :half], own_weight[:, columns], preferred_element_type=jnp.float32)
    total += jnp.dot(attended[:, half:], other_weight[:, columns], preferred_element_type=jnp.float32)
    out[...] = total.astype(out.dtype)


def project(attended, own_weight, other_weight, first, columns, dtype):
    return pl.pallas_call(
        functools.partial(project_kernel, first),
        out_shape=jax.ShapeDtypeStruct((BLOCK, columns), dtype),
        in_specs=[pl.BlockSpec(memory_space=pltpu.VMEM)] * 3,
        out_specs=pl.BlockSpec(memory_space=pltpu.VMEM),
        compiler_params=pltpu.CompilerParams(vmem_limit_bytes=32 * MIB),
        cost_estimate=pl.CostEstimate(flops=1, bytes_accessed=1, transcendentals=0),
        name="project",
    )(attended, own_weight, other_weight)


def finish_kernel(kept, received, *rest):
    rest[-1][...] = (kept[...] + received[...].astype(jnp.float32)).astype(jnp.bfloat16)


def finish(kept, received, first, out):
    columns, start = received.shape[1], first // TILE
    tile = pl.BlockSpec((BLOCK, TILE), lambda j: (0, start + j))
    in_specs = [tile, pl.BlockSpec((BLOCK, TILE), lambda j: (0, j))]
    operands = [kept, received]
    if out is not None:
        in_specs.append(pl.BlockSpec(memory_space=pl.ANY))
        operands.append(out)
    return pl.pallas_call(
        finish_kernel,
        out_shape=jax.ShapeDtypeStruct(kept.shape, jnp.bfloat16),
        grid=(columns // TILE,),
        in_specs=in_specs,
        out_specs=tile,
        input_output_aliases={} if out is None else {2: 0},
        compiler_params=pltpu.CompilerParams(vmem_limit_bytes=32 * MIB),
        cost_estimate=pl.CostEstimate(
            flops=BLOCK * columns, bytes_accessed=8 * BLOCK * columns, transcendentals=0
        ),
        name="finish",
    )(*operands)


def body(queries, key_heads, value_heads, doc_lengths, out_weight):
    s = lax.axis_index("seq")
    t = lax.axis_index("tensor")
    hi, core = t // 2, t % 2
    row, col = s // ROW, s % ROW

    query_pos = s * BLOCK + jnp.arange(BLOCK, dtype=jnp.int32)
    cosine, sine = rope_tables(query_pos)
    own_key = lax.dynamic_index_in_dim(key_heads, hi, 1, keepdims=False).astype(jnp.float32)
    own_key = rope(own_key, cosine, sine).astype(jnp.bfloat16)
    own_value = lax.dynamic_index_in_dim(value_heads, hi, 1, keepdims=False)
    block = jnp.concatenate([own_key, own_value], axis=1)

    near = [permute(block, along_rows(step)) for step in (1, 2, 3, 4)]
    far = permute(block, far_block)
    half = lax.dynamic_slice_in_dim(block, core * (BLOCK // 2), BLOCK // 2, 0)
    shifts = (1, -1, 2)
    group_1 = jnp.concatenate([half, near[0], near[1]], axis=0)
    columns_1 = [permute(group_1, in_row(shift)) for shift in shifts]
    group_2 = jnp.concatenate([near[2], near[3]], axis=0)

    heads = queries.shape[1] // HD
    q_rot = rope(
        queries.astype(jnp.float32).reshape(BLOCK, heads, HD), cosine[:, None], sine[:, None]
    ).astype(jnp.bfloat16)
    q_own = jnp.transpose(q_rot, (2, 1, 0)).reshape(HD, heads * BLOCK)
    q_all = jnp.concatenate([q_own, permute(q_own, other_core)], axis=1)

    doc_ends = jnp.cumsum(doc_lengths)
    low = jnp.max(
        jnp.where(doc_ends[None, :] <= query_pos[:, None], doc_ends[None, :], 0), axis=1
    )
    low_first = jnp.max(jnp.where(doc_ends <= s * BLOCK, doc_ends, 0))
    low_last = jnp.max(jnp.where(doc_ends <= s * BLOCK + BLOCK - 1, doc_ends, 0))
    bounds = jnp.tile(
        jnp.concatenate([low[None], query_pos[None], jnp.zeros((6, BLOCK), jnp.int32)], axis=0),
        (1, HEADS),
    )

    def rows_of(steps):
        return [jnp.where(core == 0, row - k, row - 9 + k) for k in steps]

    def bases_1(shift):
        at = (col - shift) % ROW
        own = (row * ROW + at) * BLOCK + core * (BLOCK // 2)
        return [own] + [(r * ROW + at) * BLOCK for r in rows_of((1, 2))]

    def bases_2(shift):
        at = (col - shift) % ROW
        return [(r * ROW + at) * BLOCK for r in rows_of((3, 4))]

    def scalars_of(bases, sizes):
        none, whole = True, True
        for base, size in zip(bases, sizes):
            none = none & ((base < 0) | (low_first >= base + size) | (base >= (s + 1) * BLOCK))
            whole = whole & (base >= 0) & (low_last <= base) & (base + size <= s * BLOCK)
        mode = jnp.where(none, 0, jnp.where(whole, 1, 2))
        return jnp.stack([mode] + bases).astype(jnp.int32)

    sizes_1, sizes_2 = [BLOCK // 2, BLOCK, BLOCK], [BLOCK, BLOCK]

    columns = out_weight.shape[1] // TENSOR

    def weight_of(to_hi, to_core):
        return lax.dynamic_slice_in_dim(out_weight, (2 * to_hi + to_core) * columns, columns, 1)

    far_base = jnp.where((core == 0) & (col == 0) & (s >= 33), (s - 33) * BLOCK, NOWHERE)
    state = attend(
        scalars_of([far_base] + bases_1(0) + bases_2(0), [BLOCK] + sizes_1 + sizes_2),
        q_all,
        bounds,
        [far, half] + near,
    )
    send_own, keep_own = weight_of(1 - hi, core), weight_of(hi, core)
    send_other = permute(weight_of(1 - hi, 1 - core), other_core)
    keep_other = permute(weight_of(hi, 1 - core), other_core)
    group_2, send_own, keep_own, send_other, keep_other, state = lax.optimization_barrier(
        (group_2, send_own, keep_own, send_other, keep_other, state)
    )
    columns_2 = [permute(group_2, in_row(shift)) for shift in shifts]
    for shift, keys in zip(shifts, columns_1):
        state = attend(scalars_of(bases_1(shift), sizes_1), q_all, bounds, [keys], state, sizes_1)
    state = attend(
        scalars_of(bases_2(1) + bases_2(-1), sizes_2 * 2), q_all, bounds, columns_2[:2], state, sizes_2 * 2
    )
    state = attend(scalars_of(bases_2(2), sizes_2), q_all, bounds, columns_2[2:], state, sizes_2)

    attended = merge(state, permute(state, other_core))

    pieces = ((0, 512), (512, 512), (1024, 512), (1536, 512))
    received = []
    for first, width in pieces:
        partial = project(attended, send_own, send_other, first, width, jnp.bfloat16)
        received.append(permute(partial, other_hi))
    kept = project(attended, keep_own, keep_other, 0, columns, jnp.float32)
    out = None
    for (first, _), piece in zip(pieces, received):
        out = finish(kept, piece, first, out)
    return out


def solution(mesh):
    return jax.shard_map(
        body,
        mesh=mesh,
        in_specs=(
            P("seq", "tensor"),
            P("seq", None, None),
            P("seq", None, None),
            P(),
            P("tensor", None),
        ),
        out_specs=P("seq", "tensor"),
        check_vma=False,
    )
```

```python
import functools
import math

import jax
import jax.numpy as jnp
from jax import lax
from jax.experimental import pallas as pl
from jax.experimental.pallas import tpu as pltpu
from jax.sharding import PartitionSpec as P

HQ = 16
KVH = 2
HD = 128
SEQ = 64
TENSOR = 4
ROW = 4
THETA = 500000.0
EMPTY = -1e30
MASKED = -1e32
LOG2E = math.log2(math.e)
BLOCK = 256
ROW_TOKENS = ROW * BLOCK
HEADS = 8
LANES = HEADS * BLOCK
STATE = HD + 8
TILE = 512
WIDE = 1024
NOWHERE = 1 << 24
OUT_COLUMNS = 2048
MIB = 1024 * 1024


def device_perm(move):
    pairs = []
    for s in range(SEQ):
        for hi in range(2):
            for core in range(2):
                to = move(s, hi, core)
                if to is not None:
                    pairs.append((s * TENSOR + hi * 2 + core, to[0] * TENSOR + to[1] * 2 + to[2]))
    return pairs


def permute(x, move):
    return lax.ppermute(x, ("seq", "tensor"), device_perm(move))


def in_row(shift):
    return lambda s, hi, core: (s - s % ROW + (s + shift) % ROW, hi, core)


def other_core(s, hi, core):
    return s, hi, 1 - core


def other_hi(s, hi, core):
    return s, 1 - hi, core


def far_block(s, hi, core):
    if core == 0 and s % ROW == ROW - 1 and s + 33 < SEQ:
        return s + 33, hi, core
    return None


def along_rows(step):
    def move(s, hi, core):
        if core == 0:
            return (s + step * ROW, hi, core) if s + step * ROW < SEQ else None
        return (s + (9 - step) * ROW) % SEQ, hi, core

    return move


def rope_tables(positions):
    half = HD // 2
    exponents = jnp.arange(half, dtype=jnp.float32) * (2.0 / HD)
    inverse = jnp.power(jnp.float32(THETA), -exponents)
    angles = positions.astype(jnp.float32)[:, None] * inverse[None, :]
    return jnp.cos(angles), jnp.sin(angles)


def rope(values, cosine, sine):
    half = HD // 2
    first, second = values[..., :half], values[..., half:]
    return jnp.concatenate(
        [first * cosine - second * sine, second * cosine + first * sine], axis=-1
    )


def place(ids):
    s, t = ids[0], ids[1]
    return s, t >> 1, t & 1, s >> 2, s & 3


def part_at(ids, kind, shift):
    s, _, core, row, col = place(ids)
    at = (col + ROW - shift) & 3
    if kind == "far":
        there = (core == 0) & (col == 0) & (s >= 33)
        return jnp.where(there, (s - 33) * BLOCK, NOWHERE), BLOCK
    if kind == "half":
        return (row * ROW + at) * BLOCK + core * (BLOCK // 2), BLOCK // 2
    return (jnp.where(core == 0, row - kind, row - 9 + kind) * ROW + at) * BLOCK, BLOCK


def attend_kernel(kinds, fresh, ids, lengths, q_ref, *rest):
    state = rest[-1]
    kept, refs = (None, rest[:-1]) if fresh else (rest[-2], rest[:-2])
    scale = HD**-0.5 * LOG2E
    first_query = ids[0] * BLOCK
    ends, end = [], 0
    for i in range(lengths.shape[0]):
        end = end + lengths[i]
        ends.append(end)
    low_first, low_last = 0, 0
    for end in ends:
        low_first = jnp.where(end <= first_query, end, low_first)
        low_last = jnp.where(end <= first_query + BLOCK - 1, end, low_last)
    parts, bases, none, whole = [], [], True, True
    at, i = 0, 0
    for kind, shift in kinds:
        base, size = part_at(ids, kind, shift)
        parts.append(refs[i].at[at : at + size])
        at += size
        if at == refs[i].shape[0]:
            at, i = 0, i + 1
        bases.append(base)
        dead = (base < 0) | (low_first >= base + size) | (base >= first_query + BLOCK)
        full = (base >= 0) & (low_last <= base) & (base + size <= first_query)
        none, whole = dead & none, full & whole

    def step(lanes, masked):
        q = q_ref[:, lanes]
        if masked:
            high = lax.broadcasted_iota(jnp.int32, (1, WIDE), 1) % BLOCK + first_query
            low = jnp.zeros_like(high)
            for end in ends:
                low = jnp.where(end <= high, end, low)
        scores = []
        for part, base in zip(parts, bases):
            s = jnp.dot(part[:, :HD], q, preferred_element_type=jnp.float32)
            if masked:
                at = lax.broadcasted_iota(jnp.int32, s.shape, 0) + base
                s = jnp.where((at >= low) & (at <= high), s, MASKED)
            scores.append(s)
        s = jnp.concatenate(scores, axis=0) if len(scores) > 1 else scores[0]
        values = [part[:, HD:].T for part in parts]
        values = jnp.concatenate(values, axis=1) if len(values) > 1 else values[0]
        values = jnp.concatenate([values, jnp.ones((16, values.shape[1]), jnp.bfloat16)], axis=0)
        peak = jnp.max(s, axis=0, keepdims=True) * scale
        old = jnp.full_like(peak, EMPTY) if fresh else kept[HD : HD + 1, lanes]
        new = jnp.maximum(old, peak)
        weights = jnp.exp2(s * scale - new).astype(jnp.bfloat16)
        summed = jnp.dot(values, weights, preferred_element_type=jnp.float32)
        denom = summed[HD : HD + 1]
        summed = summed[:HD]
        if not fresh:
            alpha = jnp.exp2(old - new)
            summed = summed + kept[:HD, lanes] * alpha
            denom = denom + kept[HD + 1 : HD + 2, lanes] * alpha
        state[:HD, lanes] = summed
        state[HD:, lanes] = jnp.concatenate([new, denom, jnp.zeros((6, WIDE), jnp.float32)], axis=0)

    def steps(masked):
        def one(i, carry):
            step(pl.ds(pl.multiple_of(i * WIDE, WIDE), WIDE), masked)
            return carry

        lax.fori_loop(0, LANES // WIDE, one, 0)

    if fresh:
        steps(True)
    else:

        @pl.when(none)
        def _():
            state[...] = kept[...]

        @pl.when(whole)
        def _():
            steps(False)

        @pl.when(jnp.logical_not(none | whole))
        def _():
            steps(True)


def attend(ids, lengths, q_all, refs, kinds, state=None):
    operands = list(refs) + ([] if state is None else [state])
    return pl.pallas_call(
        functools.partial(attend_kernel, kinds, state is None),
        out_shape=jax.ShapeDtypeStruct((STATE, LANES), jnp.float32),
        in_specs=[pl.BlockSpec(memory_space=pltpu.SMEM)] * 2
        + [pl.BlockSpec(memory_space=pltpu.VMEM)] * (1 + len(operands)),
        out_specs=pl.BlockSpec(memory_space=pltpu.VMEM),
        input_output_aliases={} if state is None else {2 + len(operands): 0},
        compiler_params=pltpu.CompilerParams(vmem_limit_bytes=32 * MIB),
        cost_estimate=pl.CostEstimate(flops=1, bytes_accessed=1, transcendentals=0),
        name="attend",
    )(ids, lengths, q_all, *operands)


def turn_kernel(queries, cosine, sine, out):
    half = HD // 2
    for h in range(queries.shape[1] // HD):
        x = queries[:, h * HD : (h + 1) * HD].astype(jnp.float32)
        turned = rope(x, cosine[...], sine[...]).astype(jnp.bfloat16)
        out[:, h * BLOCK : (h + 1) * BLOCK] = turned.T


def turn(queries, cosine, sine):
    return pl.pallas_call(
        turn_kernel,
        out_shape=jax.ShapeDtypeStruct((HD, queries.shape[1] // HD * BLOCK), jnp.bfloat16),
        in_specs=[pl.BlockSpec(memory_space=pltpu.VMEM)] * 3,
        out_specs=pl.BlockSpec(memory_space=pltpu.VMEM),
        compiler_params=pltpu.CompilerParams(vmem_limit_bytes=16 * MIB),
        cost_estimate=pl.CostEstimate(flops=1, bytes_accessed=1, transcendentals=0),
        name="turn",
    )(queries, cosine, sine)


def merged(mine, theirs, out):
    for h in range(HEADS):
        a = slice(h * BLOCK, (h + 1) * BLOCK)
        g = (h + HEADS // 2) % HEADS
        b = slice(g * BLOCK, (g + 1) * BLOCK)
        peak_a, peak_b = mine[HD : HD + 1, a], theirs[HD : HD + 1, b]
        peak = jnp.maximum(peak_a, peak_b)
        scale_a, scale_b = jnp.exp2(peak_a - peak), jnp.exp2(peak_b - peak)
        denom = mine[HD + 1 : HD + 2, a] * scale_a + theirs[HD + 1 : HD + 2, b] * scale_b
        summed = mine[:HD, a] * scale_a + theirs[:HD, b] * scale_b
        out[:, h * HD : (h + 1) * HD] = (summed / denom).T.astype(jnp.bfloat16)


def project_kernel(other_side, first, merging, ids, *rest):
    half = HEADS * HD // 2
    _, hi, core, _, _ = place(ids)
    weights, sems = rest[-2:]
    if merging:
        mine, theirs, own_weight, other_weight, attended = rest[:5]
        outs = rest[5:-2]
    else:
        attended, own_weight, other_weight = rest[:3]
        outs = rest[3:-2]
    at = (2 * (1 - hi if other_side else hi) + core) * OUT_COLUMNS + first
    pieces = weights.shape[0]
    for i in range(pieces):
        columns = pl.ds(pl.multiple_of(at + i * TILE, TILE), TILE)
        for j, weight in enumerate((own_weight, other_weight)):
            pltpu.make_async_copy(weight.at[:, columns], weights.at[i, j], sems.at[i, j]).start()
    if merging:
        merged(mine, theirs, attended)
    out, filled = 0, 0
    for i in range(pieces):
        columns = pl.ds(pl.multiple_of(at + i * TILE, TILE), TILE)
        for j, weight in enumerate((own_weight, other_weight)):
            pltpu.make_async_copy(weight.at[:, columns], weights.at[i, j], sems.at[i, j]).wait()
        total = jnp.dot(attended[:, :half], weights[i, 0], preferred_element_type=jnp.float32)
        total += jnp.dot(attended[:, half:], weights[i, 1], preferred_element_type=jnp.float32)
        outs[out][:, filled : filled + TILE] = total.astype(outs[out].dtype)
        filled += TILE
        if filled == outs[out].shape[1]:
            out, filled = out + 1, 0


def project(ids, operands, weights, other_side, first, widths, dtype, merging=False):
    half = HEADS * HD // 2
    shapes = [jax.ShapeDtypeStruct((BLOCK, width), dtype) for width in widths]
    if merging:
        shapes = [jax.ShapeDtypeStruct((BLOCK, 2 * half), jnp.bfloat16)] + shapes
    pieces = sum(widths) // TILE
    vmem = pl.BlockSpec(memory_space=pltpu.VMEM)
    return pl.pallas_call(
        functools.partial(project_kernel, other_side, first, merging),
        out_shape=shapes,
        in_specs=[pl.BlockSpec(memory_space=pltpu.SMEM)]
        + [vmem] * len(operands)
        + [pl.BlockSpec(memory_space=pltpu.HBM)] * 2,
        out_specs=[vmem] * len(shapes),
        scratch_shapes=[
            pltpu.VMEM((pieces, 2, half, TILE), jnp.bfloat16),
            pltpu.SemaphoreType.DMA((pieces, 2)),
        ],
        compiler_params=pltpu.CompilerParams(vmem_limit_bytes=32 * MIB),
        cost_estimate=pl.CostEstimate(flops=1, bytes_accessed=1, transcendentals=0),
        name="project",
    )(ids, *operands, *weights)


def finish_kernel(kept, received, *rest):
    rest[-1][...] = (kept[...] + received[...].astype(jnp.float32)).astype(jnp.bfloat16)


def finish(kept, received, first, out):
    columns, start = received.shape[1], first // TILE
    tile = pl.BlockSpec((BLOCK, TILE), lambda j: (0, start + j))
    in_specs = [tile, pl.BlockSpec((BLOCK, TILE), lambda j: (0, j))]
    operands = [kept, received]
    if out is not None:
        in_specs.append(pl.BlockSpec(memory_space=pl.ANY))
        operands.append(out)
    return pl.pallas_call(
        finish_kernel,
        out_shape=jax.ShapeDtypeStruct(kept.shape, jnp.bfloat16),
        grid=(columns // TILE,),
        in_specs=in_specs,
        out_specs=tile,
        input_output_aliases={} if out is None else {2: 0},
        compiler_params=pltpu.CompilerParams(vmem_limit_bytes=32 * MIB),
        cost_estimate=pl.CostEstimate(
            flops=BLOCK * columns, bytes_accessed=8 * BLOCK * columns, transcendentals=0
        ),
        name="finish",
    )(*operands)


def body(queries, key_heads, value_heads, doc_lengths, out_weight):
    s = lax.axis_index("seq")
    t = lax.axis_index("tensor")
    hi, core = t // 2, t % 2
    ids = jnp.stack([s, t]).astype(jnp.int32)

    query_pos = s * BLOCK + jnp.arange(BLOCK, dtype=jnp.int32)
    cosine, sine = rope_tables(query_pos)
    own_key = lax.dynamic_index_in_dim(key_heads, hi, 1, keepdims=False).astype(jnp.float32)
    own_key = rope(own_key, cosine, sine).astype(jnp.bfloat16)
    own_value = lax.dynamic_index_in_dim(value_heads, hi, 1, keepdims=False)
    block = jnp.concatenate([own_key, own_value], axis=1)

    near = [permute(block, along_rows(step)) for step in (1, 2, 3, 4)]
    far = permute(block, far_block)
    half = lax.dynamic_slice_in_dim(block, core * (BLOCK // 2), BLOCK // 2, 0)
    shifts = (1, -1, 2)
    group_1 = jnp.concatenate([half, near[0], near[1]], axis=0)
    group_1, far, out_weight = lax.optimization_barrier((group_1, far, out_weight))
    other_weight = permute(out_weight, other_core)
    columns_1 = [permute(group_1, in_row(shift)) for shift in shifts]
    group_2 = jnp.concatenate([near[2], near[3]], axis=0)

    q_own = turn(queries, cosine, sine)
    q_all = jnp.concatenate([q_own, permute(q_own, other_core)], axis=1)
    step = functools.partial(attend, ids, doc_lengths, q_all)

    state = step([half] + near, [("half", 0)] + [(k, 0) for k in (1, 2, 3, 4)])
    group_2, state = lax.optimization_barrier((group_2, state))
    columns_2 = [permute(group_2, in_row(shift)) for shift in shifts]
    for shift, keys in zip(shifts, columns_1):
        kinds = [("half", shift), (1, shift), (2, shift)]
        if shift == 2:
            state = step([keys, far], kinds + [("far", 0)], state)
        else:
            state = step([keys], kinds, state)
    state, other_weight = lax.optimization_barrier((state, other_weight))
    weights = (out_weight, other_weight)
    state = step(columns_2[:2], [(k, shift) for shift in shifts[:2] for k in (3, 4)], state)
    state = step(columns_2[2:], [(3, 2), (4, 2)], state)

    theirs = permute(state, other_core)
    attended, partial = project(ids, (state, theirs), weights, True, 0, (512,), jnp.bfloat16, True)
    received = [permute(partial, other_hi)]
    for partial in project(ids, (attended,), weights, True, 512, (512,) * 3, jnp.bfloat16):
        received.append(permute(partial, other_hi))
    (kept,) = project(ids, (attended,), weights, False, 0, (OUT_COLUMNS,), jnp.float32)
    out, first = None, 0
    for piece in received:
        out = finish(kept, piece, first, out)
        first += piece.shape[1]
    return out


def solution(mesh):
    return jax.shard_map(
        body,
        mesh=mesh,
        in_specs=(
            P("seq", "tensor"),
            P("seq", None, None),
            P("seq", None, None),
            P(),
            P("tensor", None),
        ),
        out_specs=P("seq", "tensor"),
        check_vma=False,
    )
```

```python
import functools
import math

import jax
import jax.numpy as jnp
from jax import lax
from jax.experimental import pallas as pl
from jax.experimental.pallas import tpu as pltpu
from jax.sharding import PartitionSpec as P

HQ = 16
KVH = 2
HD = 128
SEQ = 64
TENSOR = 4
ROW = 4
THETA = 500000.0
EMPTY = -1e30
MASKED = -1e32
LOG2E = math.log2(math.e)
BLOCK = 256
ROW_TOKENS = ROW * BLOCK
HEADS = 8
LANES = HEADS * BLOCK
STATE = HD + 8
TILE = 512
WIDE = 1024
NOWHERE = 1 << 24
OUT_COLUMNS = 2048
MIB = 1024 * 1024


def device_perm(move):
    pairs = []
    for s in range(SEQ):
        for hi in range(2):
            for core in range(2):
                to = move(s, hi, core)
                if to is not None:
                    pairs.append((s * TENSOR + hi * 2 + core, to[0] * TENSOR + to[1] * 2 + to[2]))
    return pairs


def permute(x, move):
    return lax.ppermute(x, ("seq", "tensor"), device_perm(move))


def in_row(shift):
    return lambda s, hi, core: (s - s % ROW + (s + shift) % ROW, hi, core)


def other_core(s, hi, core):
    return s, hi, 1 - core


def other_hi(s, hi, core):
    return s, 1 - hi, core


def far_block(s, hi, core):
    if core == 0 and s % ROW == ROW - 1 and s + 33 < SEQ:
        return s + 33, hi, core
    return None


def along_rows(step):
    def move(s, hi, core):
        if core == 0:
            return (s + step * ROW, hi, core) if s + step * ROW < SEQ else None
        return (s + (9 - step) * ROW) % SEQ, hi, core

    return move


def rope_tables(positions):
    half = HD // 2
    exponents = jnp.arange(half, dtype=jnp.float32) * (2.0 / HD)
    inverse = jnp.power(jnp.float32(THETA), -exponents)
    angles = positions.astype(jnp.float32)[:, None] * inverse[None, :]
    return jnp.cos(angles), jnp.sin(angles)


def rope(values, cosine, sine):
    half = HD // 2
    first, second = values[..., :half], values[..., half:]
    return jnp.concatenate(
        [first * cosine - second * sine, second * cosine + first * sine], axis=-1
    )


def place(ids):
    s, t = ids[0], ids[1]
    return s, t >> 1, t & 1, s >> 2, s & 3


def part_at(ids, kind, shift):
    s, _, core, row, col = place(ids)
    at = (col + ROW - shift) & 3
    if kind == "far":
        there = (core == 0) & (col == 0) & (s >= 33)
        return jnp.where(there, (s - 33) * BLOCK, NOWHERE), BLOCK
    if kind == "half":
        return (row * ROW + at) * BLOCK + core * (BLOCK // 2), BLOCK // 2
    return (jnp.where(core == 0, row - kind, row - 9 + kind) * ROW + at) * BLOCK, BLOCK


def attend_kernel(kinds, fresh, ids, lengths, q_ref, *rest):
    state = rest[-1]
    kept, refs = (None, rest[:-1]) if fresh else (rest[-2], rest[:-2])
    scale = HD**-0.5 * LOG2E
    first_query = ids[0] * BLOCK
    ends, end = [], 0
    for i in range(lengths.shape[0]):
        end = end + lengths[i]
        ends.append(end)
    low_first, low_last = 0, 0
    for end in ends:
        low_first = jnp.where(end <= first_query, end, low_first)
        low_last = jnp.where(end <= first_query + BLOCK - 1, end, low_last)
    parts, bases, none, whole = [], [], True, True
    at, i = 0, 0
    for kind, shift in kinds:
        base, size = part_at(ids, kind, shift)
        parts.append(refs[i].at[at : at + size])
        at += size
        if at == refs[i].shape[0]:
            at, i = 0, i + 1
        bases.append(base)
        dead = (base < 0) | (low_first >= base + size) | (base >= first_query + BLOCK)
        full = (base >= 0) & (low_last <= base) & (base + size <= first_query)
        none, whole = dead & none, full & whole

    def step(lanes, masked):
        q = q_ref[:, lanes]
        if masked:
            high = lax.broadcasted_iota(jnp.int32, (1, WIDE), 1) % BLOCK + first_query
            low = jnp.zeros_like(high)
            for end in ends:
                low = jnp.where(end <= high, end, low)
        scores = []
        for part, base in zip(parts, bases):
            s = jnp.dot(part[:, :HD], q, preferred_element_type=jnp.float32)
            if masked:
                at = lax.broadcasted_iota(jnp.int32, s.shape, 0) + base
                s = jnp.where((at >= low) & (at <= high), s, MASKED)
            scores.append(s)
        s = jnp.concatenate(scores, axis=0) if len(scores) > 1 else scores[0]
        values = [part[:, HD:].T for part in parts]
        values = jnp.concatenate(values, axis=1) if len(values) > 1 else values[0]
        values = jnp.concatenate([values, jnp.ones((16, values.shape[1]), jnp.bfloat16)], axis=0)
        peak = jnp.max(s, axis=0, keepdims=True) * scale
        old = jnp.full_like(peak, EMPTY) if fresh else kept[HD : HD + 1, lanes]
        new = jnp.maximum(old, peak)
        weights = jnp.exp2(s * scale - new).astype(jnp.bfloat16)
        summed = jnp.dot(values, weights, preferred_element_type=jnp.float32)
        denom = summed[HD : HD + 1]
        summed = summed[:HD]
        if not fresh:
            alpha = jnp.exp2(old - new)
            summed = summed + kept[:HD, lanes] * alpha
            denom = denom + kept[HD + 1 : HD + 2, lanes] * alpha
        state[:HD, lanes] = summed
        state[HD:, lanes] = jnp.concatenate([new, denom, jnp.zeros((6, WIDE), jnp.float32)], axis=0)

    def steps(masked):
        def one(i, carry):
            step(pl.ds(pl.multiple_of(i * WIDE, WIDE), WIDE), masked)
            return carry

        lax.fori_loop(0, LANES // WIDE, one, 0)

    if fresh:
        steps(True)
    else:

        @pl.when(none)
        def _():
            state[...] = kept[...]

        @pl.when(whole)
        def _():
            steps(False)

        @pl.when(jnp.logical_not(none | whole))
        def _():
            steps(True)


def attend(ids, lengths, q_all, refs, kinds, state=None):
    operands = list(refs) + ([] if state is None else [state])
    return pl.pallas_call(
        functools.partial(attend_kernel, kinds, state is None),
        out_shape=jax.ShapeDtypeStruct((STATE, LANES), jnp.float32),
        in_specs=[pl.BlockSpec(memory_space=pltpu.SMEM)] * 2
        + [pl.BlockSpec(memory_space=pltpu.VMEM)] * (1 + len(operands)),
        out_specs=pl.BlockSpec(memory_space=pltpu.VMEM),
        input_output_aliases={} if state is None else {2 + len(operands): 0},
        compiler_params=pltpu.CompilerParams(vmem_limit_bytes=32 * MIB),
        cost_estimate=pl.CostEstimate(flops=1, bytes_accessed=1, transcendentals=0),
        name="attend",
    )(ids, lengths, q_all, *operands)


def turn_kernel(queries, cosine, sine, out):
    half = HD // 2
    for h in range(queries.shape[1] // HD):
        x = queries[:, h * HD : (h + 1) * HD].astype(jnp.float32)
        turned = rope(x, cosine[...], sine[...]).astype(jnp.bfloat16)
        out[:, h * BLOCK : (h + 1) * BLOCK] = turned.T


def turn(queries, cosine, sine):
    return pl.pallas_call(
        turn_kernel,
        out_shape=jax.ShapeDtypeStruct((HD, queries.shape[1] // HD * BLOCK), jnp.bfloat16),
        in_specs=[pl.BlockSpec(memory_space=pltpu.VMEM)] * 3,
        out_specs=pl.BlockSpec(memory_space=pltpu.VMEM),
        compiler_params=pltpu.CompilerParams(vmem_limit_bytes=16 * MIB),
        cost_estimate=pl.CostEstimate(flops=1, bytes_accessed=1, transcendentals=0),
        name="turn",
    )(queries, cosine, sine)


def merged(mine, theirs, out):
    for h in range(HEADS):
        a = slice(h * BLOCK, (h + 1) * BLOCK)
        g = (h + HEADS // 2) % HEADS
        b = slice(g * BLOCK, (g + 1) * BLOCK)
        peak_a, peak_b = mine[HD : HD + 1, a], theirs[HD : HD + 1, b]
        peak = jnp.maximum(peak_a, peak_b)
        scale_a, scale_b = jnp.exp2(peak_a - peak), jnp.exp2(peak_b - peak)
        denom = mine[HD + 1 : HD + 2, a] * scale_a + theirs[HD + 1 : HD + 2, b] * scale_b
        summed = mine[:HD, a] * scale_a + theirs[:HD, b] * scale_b
        out[:, h * HD : (h + 1) * HD] = (summed / denom).T.astype(jnp.bfloat16)


def project_kernel(other_side, first, merging, ids, *rest):
    half = HEADS * HD // 2
    _, hi, core, _, _ = place(ids)
    weights, sems = rest[-2:]
    if merging:
        mine, theirs, own_weight, other_weight, attended = rest[:5]
        outs = rest[5:-2]
    else:
        attended, own_weight, other_weight = rest[:3]
        outs = rest[3:-2]
    at = (2 * (1 - hi if other_side else hi) + core) * OUT_COLUMNS + first
    pieces = weights.shape[0]
    for i in range(pieces):
        columns = pl.ds(pl.multiple_of(at + i * TILE, TILE), TILE)
        for j, weight in enumerate((own_weight, other_weight)):
            pltpu.make_async_copy(weight.at[:, columns], weights.at[i, j], sems.at[i, j]).start()
    if merging:
        merged(mine, theirs, attended)
    out, filled = 0, 0
    for i in range(pieces):
        columns = pl.ds(pl.multiple_of(at + i * TILE, TILE), TILE)
        for j, weight in enumerate((own_weight, other_weight)):
            pltpu.make_async_copy(weight.at[:, columns], weights.at[i, j], sems.at[i, j]).wait()
        total = jnp.dot(attended[:, :half], weights[i, 0], preferred_element_type=jnp.float32)
        total += jnp.dot(attended[:, half:], weights[i, 1], preferred_element_type=jnp.float32)
        outs[out][:, filled : filled + TILE] = total.astype(outs[out].dtype)
        filled += TILE
        if filled == outs[out].shape[1]:
            out, filled = out + 1, 0


def project(ids, operands, weights, other_side, first, widths, dtype, merging=False):
    half = HEADS * HD // 2
    shapes = [jax.ShapeDtypeStruct((BLOCK, width), dtype) for width in widths]
    if merging:
        shapes = [jax.ShapeDtypeStruct((BLOCK, 2 * half), jnp.bfloat16)] + shapes
    pieces = sum(widths) // TILE
    vmem = pl.BlockSpec(memory_space=pltpu.VMEM)
    return pl.pallas_call(
        functools.partial(project_kernel, other_side, first, merging),
        out_shape=shapes,
        in_specs=[pl.BlockSpec(memory_space=pltpu.SMEM)]
        + [vmem] * len(operands)
        + [pl.BlockSpec(memory_space=pltpu.HBM)] * 2,
        out_specs=[vmem] * len(shapes),
        scratch_shapes=[
            pltpu.VMEM((pieces, 2, half, TILE), jnp.bfloat16),
            pltpu.SemaphoreType.DMA((pieces, 2)),
        ],
        compiler_params=pltpu.CompilerParams(vmem_limit_bytes=32 * MIB),
        cost_estimate=pl.CostEstimate(flops=1, bytes_accessed=1, transcendentals=0),
        name="project",
    )(ids, *operands, *weights)


def finish_kernel(kept, received, *rest):
    rest[-1][...] = (kept[...] + received[...].astype(jnp.float32)).astype(jnp.bfloat16)


def finish(kept, received, first, out):
    columns, start = received.shape[1], first // TILE
    tile = pl.BlockSpec((BLOCK, TILE), lambda j: (0, start + j))
    in_specs = [tile, pl.BlockSpec((BLOCK, TILE), lambda j: (0, j))]
    operands = [kept, received]
    if out is not None:
        in_specs.append(pl.BlockSpec(memory_space=pl.ANY))
        operands.append(out)
    return pl.pallas_call(
        finish_kernel,
        out_shape=jax.ShapeDtypeStruct(kept.shape, jnp.bfloat16),
        grid=(columns // TILE,),
        in_specs=in_specs,
        out_specs=tile,
        input_output_aliases={} if out is None else {2: 0},
        compiler_params=pltpu.CompilerParams(vmem_limit_bytes=32 * MIB),
        cost_estimate=pl.CostEstimate(
            flops=BLOCK * columns, bytes_accessed=8 * BLOCK * columns, transcendentals=0
        ),
        name="finish",
    )(*operands)


def body(queries, key_heads, value_heads, doc_lengths, out_weight):
    s = lax.axis_index("seq")
    t = lax.axis_index("tensor")
    hi, core = t // 2, t % 2
    ids = jnp.stack([s, t]).astype(jnp.int32)

    query_pos = s * BLOCK + jnp.arange(BLOCK, dtype=jnp.int32)
    cosine, sine = rope_tables(query_pos)
    own_key = lax.dynamic_index_in_dim(key_heads, hi, 1, keepdims=False).astype(jnp.float32)
    own_key = rope(own_key, cosine, sine).astype(jnp.bfloat16)
    own_value = lax.dynamic_index_in_dim(value_heads, hi, 1, keepdims=False)
    block = jnp.concatenate([own_key, own_value], axis=1)

    near = [permute(block, along_rows(step)) for step in (1, 2, 3, 4)]
    far = permute(block, far_block)
    half = lax.dynamic_slice_in_dim(block, core * (BLOCK // 2), BLOCK // 2, 0)
    shifts = (1, -1, 2)
    group_1 = jnp.concatenate([half, near[0], near[1]], axis=0)
    q_own = turn(queries, cosine, sine)
    q_other = permute(q_own, other_core)
    group_1, out_weight, q_other, *near[2:] = lax.optimization_barrier(
        (group_1, out_weight, q_other, *near[2:])
    )
    other_weight = permute(out_weight, other_core)
    columns_1 = [permute(group_1, in_row(shift)) for shift in shifts]
    group_2 = jnp.concatenate([near[2], near[3]], axis=0)

    q_all = jnp.concatenate([q_own, q_other], axis=1)
    step = functools.partial(attend, ids, doc_lengths, q_all)

    state = step([half] + near, [("half", 0)] + [(k, 0) for k in (1, 2, 3, 4)])
    columns_2 = []
    for shift, keys in zip(shifts, columns_1):
        group_2, state = lax.optimization_barrier((group_2, state))
        columns_2.append(permute(group_2, in_row(shift)))
        kinds = [("half", shift), (1, shift), (2, shift)]
        if shift == 2:
            state = step([keys, far], kinds + [("far", 0)], state)
        else:
            state = step([keys], kinds, state)
    state, other_weight = lax.optimization_barrier((state, other_weight))
    weights = (out_weight, other_weight)
    for shift, keys in zip(shifts, columns_2):
        state = step([keys], [(3, shift), (4, shift)], state)

    theirs = permute(state, other_core)
    attended, partial = project(ids, (state, theirs), weights, True, 0, (512,), jnp.bfloat16, True)
    received = [permute(partial, other_hi)]
    for partial in project(ids, (attended,), weights, True, 512, (512,) * 3, jnp.bfloat16):
        received.append(permute(partial, other_hi))
    (kept,) = project(ids, (attended,), weights, False, 0, (OUT_COLUMNS,), jnp.float32)
    out, first = None, 0
    for piece in received:
        out = finish(kept, piece, first, out)
        first += piece.shape[1]
    return out


def solution(mesh):
    return jax.shard_map(
        body,
        mesh=mesh,
        in_specs=(
            P("seq", "tensor"),
            P("seq", None, None),
            P("seq", None, None),
            P(),
            P("tensor", None),
        ),
        out_specs=P("seq", "tensor"),
        check_vma=False,
    )
```

```python
import functools
import math

import jax
import jax.numpy as jnp
from jax import lax
from jax.experimental import pallas as pl
from jax.experimental.pallas import tpu as pltpu
from jax.sharding import PartitionSpec as P

HQ = 16
KVH = 2
HD = 128
SEQ = 64
TENSOR = 4
ROW = 4
THETA = 500000.0
EMPTY = -1e30
MASKED = -1e32
LOG2E = math.log2(math.e)
BLOCK = 256
ROW_TOKENS = ROW * BLOCK
HEADS = 8
LANES = HEADS * BLOCK
STATE = HD + 8
TILE = 512
WIDE = 1024
NOWHERE = 1 << 24
OUT_COLUMNS = 2048
MIB = 1024 * 1024


def device_perm(move):
    pairs = []
    for s in range(SEQ):
        for hi in range(2):
            for core in range(2):
                to = move(s, hi, core)
                if to is not None:
                    pairs.append((s * TENSOR + hi * 2 + core, to[0] * TENSOR + to[1] * 2 + to[2]))
    return pairs


def permute(x, move):
    return lax.ppermute(x, ("seq", "tensor"), device_perm(move))


def in_row(shift):
    return lambda s, hi, core: (s - s % ROW + (s + shift) % ROW, hi, core)


def other_core(s, hi, core):
    return s, hi, 1 - core


def other_hi(s, hi, core):
    return s, 1 - hi, core


def far_block(s, hi, core):
    if core == 0 and s % ROW == ROW - 1 and s + 33 < SEQ:
        return s + 33, hi, core
    return None


def along_rows(step):
    def move(s, hi, core):
        if core == 0:
            return (s + step * ROW, hi, core) if s + step * ROW < SEQ else None
        return (s + (9 - step) * ROW) % SEQ, hi, core

    return move


def rope_tables(positions):
    half = HD // 2
    exponents = jnp.arange(half, dtype=jnp.float32) * (2.0 / HD)
    inverse = jnp.power(jnp.float32(THETA), -exponents)
    angles = positions.astype(jnp.float32)[:, None] * inverse[None, :]
    return jnp.cos(angles), jnp.sin(angles)


def rope(values, cosine, sine):
    half = HD // 2
    first, second = values[..., :half], values[..., half:]
    return jnp.concatenate(
        [first * cosine - second * sine, second * cosine + first * sine], axis=-1
    )


def place(ids):
    s, t = ids[0], ids[1]
    return s, t >> 1, t & 1, s >> 2, s & 3


def part_at(ids, kind, shift):
    s, _, core, row, col = place(ids)
    at = (col + ROW - shift) & 3
    if kind == "far":
        there = (core == 0) & (col == 0) & (s >= 33)
        return jnp.where(there, (s - 33) * BLOCK, NOWHERE), BLOCK
    if kind == "half":
        return (row * ROW + at) * BLOCK + core * (BLOCK // 2), BLOCK // 2
    return (jnp.where(core == 0, row - kind, row - 9 + kind) * ROW + at) * BLOCK, BLOCK


def attend_kernel(kinds, fresh, ids, lengths, q_ref, *rest):
    state = rest[-1]
    kept, refs = (None, rest[:-1]) if fresh else (rest[-2], rest[:-2])
    scale = HD**-0.5 * LOG2E
    first_query = ids[0] * BLOCK
    ends, end = [], 0
    for i in range(lengths.shape[0]):
        end = end + lengths[i]
        ends.append(end)
    low_first, low_last = 0, 0
    for end in ends:
        low_first = jnp.where(end <= first_query, end, low_first)
        low_last = jnp.where(end <= first_query + BLOCK - 1, end, low_last)
    parts, bases, none, whole = [], [], True, True
    at, i = 0, 0
    for kind, shift in kinds:
        base, size = part_at(ids, kind, shift)
        parts.append(refs[i].at[at : at + size])
        at += size
        if at == refs[i].shape[0]:
            at, i = 0, i + 1
        bases.append(base)
        dead = (base < 0) | (low_first >= base + size) | (base >= first_query + BLOCK)
        full = (base >= 0) & (low_last <= base) & (base + size <= first_query)
        none, whole = dead & none, full & whole

    def step(lanes, masked):
        q = q_ref[:, lanes]
        if masked:
            high = lax.broadcasted_iota(jnp.int32, (1, WIDE), 1) % BLOCK + first_query
            low = jnp.zeros_like(high)
            for end in ends:
                low = jnp.where(end <= high, end, low)
        scores = []
        for part, base in zip(parts, bases):
            s = jnp.dot(part[:, :HD], q, preferred_element_type=jnp.float32)
            if masked:
                at = lax.broadcasted_iota(jnp.int32, s.shape, 0) + base
                s = jnp.where((at >= low) & (at <= high), s, MASKED)
            scores.append(s)
        s = jnp.concatenate(scores, axis=0) if len(scores) > 1 else scores[0]
        values = [part[:, HD:].T for part in parts]
        values = jnp.concatenate(values, axis=1) if len(values) > 1 else values[0]
        values = jnp.concatenate([values, jnp.ones((16, values.shape[1]), jnp.bfloat16)], axis=0)
        peak = jnp.max(s, axis=0, keepdims=True) * scale
        old = jnp.full_like(peak, EMPTY) if fresh else kept[HD : HD + 1, lanes]
        new = jnp.maximum(old, peak)
        weights = jnp.exp2(s * scale - new).astype(jnp.bfloat16)
        summed = jnp.dot(values, weights, preferred_element_type=jnp.float32)
        denom = summed[HD : HD + 1]
        summed = summed[:HD]
        if not fresh:
            alpha = jnp.exp2(old - new)
            summed = summed + kept[:HD, lanes] * alpha
            denom = denom + kept[HD + 1 : HD + 2, lanes] * alpha
        state[:HD, lanes] = summed
        state[HD:, lanes] = jnp.concatenate([new, denom, jnp.zeros((6, WIDE), jnp.float32)], axis=0)

    def steps(masked):
        def one(i, carry):
            step(pl.ds(pl.multiple_of(i * WIDE, WIDE), WIDE), masked)
            return carry

        lax.fori_loop(0, LANES // WIDE, one, 0)

    if fresh:
        steps(True)
    else:

        @pl.when(none)
        def _():
            state[...] = kept[...]

        @pl.when(whole)
        def _():
            steps(False)

        @pl.when(jnp.logical_not(none | whole))
        def _():
            steps(True)


def attend(ids, lengths, q_all, refs, kinds, state=None):
    operands = list(refs) + ([] if state is None else [state])
    return pl.pallas_call(
        functools.partial(attend_kernel, kinds, state is None),
        out_shape=jax.ShapeDtypeStruct((STATE, LANES), jnp.float32),
        in_specs=[pl.BlockSpec(memory_space=pltpu.SMEM)] * 2
        + [pl.BlockSpec(memory_space=pltpu.VMEM)] * (1 + len(operands)),
        out_specs=pl.BlockSpec(memory_space=pltpu.VMEM),
        input_output_aliases={} if state is None else {2 + len(operands): 0},
        compiler_params=pltpu.CompilerParams(vmem_limit_bytes=32 * MIB),
        cost_estimate=pl.CostEstimate(flops=1, bytes_accessed=1, transcendentals=0),
        name="attend",
    )(ids, lengths, q_all, *operands)


def turn_kernel(queries, cosine, sine, out):
    half = HD // 2
    for h in range(queries.shape[1] // HD):
        x = queries[:, h * HD : (h + 1) * HD].astype(jnp.float32)
        turned = rope(x, cosine[...], sine[...]).astype(jnp.bfloat16)
        out[:, h * BLOCK : (h + 1) * BLOCK] = turned.T


def turn(queries, cosine, sine):
    return pl.pallas_call(
        turn_kernel,
        out_shape=jax.ShapeDtypeStruct((HD, queries.shape[1] // HD * BLOCK), jnp.bfloat16),
        in_specs=[pl.BlockSpec(memory_space=pltpu.VMEM)] * 3,
        out_specs=pl.BlockSpec(memory_space=pltpu.VMEM),
        compiler_params=pltpu.CompilerParams(vmem_limit_bytes=16 * MIB),
        cost_estimate=pl.CostEstimate(flops=1, bytes_accessed=1, transcendentals=0),
        name="turn",
    )(queries, cosine, sine)


def merged(mine, theirs, out):
    for h in range(HEADS):
        a = slice(h * BLOCK, (h + 1) * BLOCK)
        g = (h + HEADS // 2) % HEADS
        b = slice(g * BLOCK, (g + 1) * BLOCK)
        peak_a, peak_b = mine[HD : HD + 1, a], theirs[HD : HD + 1, b]
        peak = jnp.maximum(peak_a, peak_b)
        scale_a, scale_b = jnp.exp2(peak_a - peak), jnp.exp2(peak_b - peak)
        denom = mine[HD + 1 : HD + 2, a] * scale_a + theirs[HD + 1 : HD + 2, b] * scale_b
        summed = mine[:HD, a] * scale_a + theirs[:HD, b] * scale_b
        out[:, h * HD : (h + 1) * HD] = (summed / denom).T.astype(jnp.bfloat16)


def project_kernel(other_side, first, merging, ids, *rest):
    half = HEADS * HD // 2
    _, hi, core, _, _ = place(ids)
    weights, sems = rest[-2:]
    if merging:
        mine, theirs, pair, attended = rest[:4]
        outs = rest[4:-2]
    else:
        attended, pair = rest[:2]
        outs = rest[2:-2]
    at = (2 * (1 - hi if other_side else hi) + core) * OUT_COLUMNS + first
    pieces = weights.shape[0]

    def copy(i, j):
        rows = pl.ds(pl.multiple_of((core if j == 0 else 1 - core) * half, half), half)
        columns = pl.ds(pl.multiple_of(at + i * TILE, TILE), TILE)
        return pltpu.make_async_copy(pair.at[rows, columns], weights.at[i, j], sems.at[i, j])

    for i in range(pieces):
        copy(i, 0).start()
        copy(i, 1).start()
    if merging:
        merged(mine, theirs, attended)
    out, filled = 0, 0
    for i in range(pieces):
        copy(i, 0).wait()
        copy(i, 1).wait()
        total = jnp.dot(attended[:, :half], weights[i, 0], preferred_element_type=jnp.float32)
        total += jnp.dot(attended[:, half:], weights[i, 1], preferred_element_type=jnp.float32)
        outs[out][:, filled : filled + TILE] = total.astype(outs[out].dtype)
        filled += TILE
        if filled == outs[out].shape[1]:
            out, filled = out + 1, 0


def project(ids, operands, weights, other_side, first, widths, dtype, merging=False):
    half = HEADS * HD // 2
    shapes = [jax.ShapeDtypeStruct((BLOCK, width), dtype) for width in widths]
    if merging:
        shapes = [jax.ShapeDtypeStruct((BLOCK, 2 * half), jnp.bfloat16)] + shapes
    pieces = sum(widths) // TILE
    vmem = pl.BlockSpec(memory_space=pltpu.VMEM)
    return pl.pallas_call(
        functools.partial(project_kernel, other_side, first, merging),
        out_shape=shapes,
        in_specs=[pl.BlockSpec(memory_space=pltpu.SMEM)]
        + [vmem] * len(operands)
        + [pl.BlockSpec(memory_space=pltpu.HBM)],
        out_specs=[vmem] * len(shapes),
        scratch_shapes=[
            pltpu.VMEM((pieces, 2, half, TILE), jnp.bfloat16),
            pltpu.SemaphoreType.DMA((pieces, 2)),
        ],
        compiler_params=pltpu.CompilerParams(vmem_limit_bytes=52 * MIB),
        cost_estimate=pl.CostEstimate(flops=1, bytes_accessed=1, transcendentals=0),
        name="project",
    )(ids, *operands, weights)


def finish_kernel(kept, received, *rest):
    rest[-1][...] = (kept[...] + received[...].astype(jnp.float32)).astype(jnp.bfloat16)


def finish(kept, received, first, out):
    columns, start = received.shape[1], first // TILE
    tile = pl.BlockSpec((BLOCK, TILE), lambda j: (0, start + j))
    in_specs = [tile, pl.BlockSpec((BLOCK, TILE), lambda j: (0, j))]
    operands = [kept, received]
    if out is not None:
        in_specs.append(pl.BlockSpec(memory_space=pl.ANY))
        operands.append(out)
    return pl.pallas_call(
        finish_kernel,
        out_shape=jax.ShapeDtypeStruct(kept.shape, jnp.bfloat16),
        grid=(columns // TILE,),
        in_specs=in_specs,
        out_specs=tile,
        input_output_aliases={} if out is None else {2: 0},
        compiler_params=pltpu.CompilerParams(vmem_limit_bytes=32 * MIB),
        cost_estimate=pl.CostEstimate(
            flops=BLOCK * columns, bytes_accessed=8 * BLOCK * columns, transcendentals=0
        ),
        name="finish",
    )(*operands)


def body(queries, key_heads, value_heads, doc_lengths, out_weight):
    s = lax.axis_index("seq")
    t = lax.axis_index("tensor")
    hi, core = t // 2, t % 2
    ids = jnp.stack([s, t]).astype(jnp.int32)

    query_pos = s * BLOCK + jnp.arange(BLOCK, dtype=jnp.int32)
    cosine, sine = rope_tables(query_pos)
    own_key = lax.dynamic_index_in_dim(key_heads, hi, 1, keepdims=False).astype(jnp.float32)
    own_key = rope(own_key, cosine, sine).astype(jnp.bfloat16)
    own_value = lax.dynamic_index_in_dim(value_heads, hi, 1, keepdims=False)
    block = jnp.concatenate([own_key, own_value], axis=1)

    weights = lax.all_gather(
        out_weight, "tensor", axis=0, tiled=True, axis_index_groups=[[0, 1], [2, 3]]
    )
    q_own = turn(queries, cosine, sine)
    q_other = permute(q_own, other_core)
    near = [permute(block, along_rows(step)) for step in (1, 2)]
    half = lax.dynamic_slice_in_dim(block, core * (BLOCK // 2), BLOCK // 2, 0)
    group_1 = jnp.concatenate([half, *near], axis=0)
    group_1, block, q_other = lax.optimization_barrier((group_1, block, q_other))
    shifts = (1, -1, 2)
    columns_1 = [permute(group_1, in_row(shift)) for shift in shifts]
    near += [permute(block, along_rows(step)) for step in (3, 4)]
    group_2 = jnp.concatenate(near[2:], axis=0)

    q_all = jnp.concatenate([q_own, q_other], axis=1)
    step = functools.partial(attend, ids, doc_lengths, q_all)

    state = step([half] + near, [("half", 0)] + [(k, 0) for k in (1, 2, 3, 4)])
    block, state = lax.optimization_barrier((block, state))
    far = permute(block, far_block)
    columns_2 = []
    for shift, keys in zip(shifts, columns_1):
        group_2, state = lax.optimization_barrier((group_2, state))
        columns_2.append(permute(group_2, in_row(shift)))
        kinds = [("half", shift), (1, shift), (2, shift)]
        if shift == 2:
            state = step([keys, far], kinds + [("far", 0)], state)
        else:
            state = step([keys], kinds, state)
    for shift, keys in zip(shifts, columns_2):
        state = step([keys], [(3, shift), (4, shift)], state)

    theirs = permute(state, other_core)
    attended, partial = project(ids, (state, theirs), weights, True, 0, (512,), jnp.bfloat16, True)
    received = [permute(partial, other_hi)]
    for partial in project(ids, (attended,), weights, True, 512, (512,) * 3, jnp.bfloat16):
        received.append(permute(partial, other_hi))
    (kept,) = project(ids, (attended,), weights, False, 0, (OUT_COLUMNS,), jnp.float32)
    out, first = None, 0
    for piece in received:
        out = finish(kept, piece, first, out)
        first += piece.shape[1]
    return out


def solution(mesh):
    return jax.shard_map(
        body,
        mesh=mesh,
        in_specs=(
            P("seq", "tensor"),
            P("seq", None, None),
            P("seq", None, None),
            P(),
            P("tensor", None),
        ),
        out_specs=P("seq", "tensor"),
        check_vma=False,
    )
```

```python
import functools
import math

import jax
import jax.numpy as jnp
from jax import lax
from jax.experimental import pallas as pl
from jax.experimental.pallas import tpu as pltpu
from jax.sharding import PartitionSpec as P

HQ = 16
KVH = 2
HD = 128
SEQ = 64
TENSOR = 4
ROW = 4
THETA = 500000.0
EMPTY = -1e30
MASKED = -1e32
LOG2E = math.log2(math.e)
BLOCK = 256
ROW_TOKENS = ROW * BLOCK
HEADS = 8
LANES = HEADS * BLOCK
STATE = HD + 8
TILE = 512
WIDE = 1024
NOWHERE = 1 << 24
OUT_COLUMNS = 2048
MIB = 1024 * 1024


def device_perm(move):
    pairs = []
    for s in range(SEQ):
        for hi in range(2):
            for core in range(2):
                to = move(s, hi, core)
                if to is not None:
                    pairs.append((s * TENSOR + hi * 2 + core, to[0] * TENSOR + to[1] * 2 + to[2]))
    return pairs


def permute(x, move):
    return lax.ppermute(x, ("seq", "tensor"), device_perm(move))


def in_row(shift):
    return lambda s, hi, core: (s - s % ROW + (s + shift) % ROW, hi, core)


def other_core(s, hi, core):
    return s, hi, 1 - core


def other_hi(s, hi, core):
    return s, 1 - hi, core


def far_block(s, hi, core):
    if core == 0 and s % ROW == ROW - 1 and s + 33 < SEQ:
        return s + 33, hi, core
    return None


def along_rows(step):
    def move(s, hi, core):
        if core == 0:
            return (s + step * ROW, hi, core) if s + step * ROW < SEQ else None
        return (s + (9 - step) * ROW) % SEQ, hi, core

    return move


def two_rows_on(s, hi, core):
    if core == 0:
        return (s + 2 * ROW, hi, core) if s + 2 * ROW < SEQ else None
    return (s - 2 * ROW) % SEQ, hi, core


def rope_tables(positions):
    half = HD // 2
    exponents = jnp.arange(half, dtype=jnp.float32) * (2.0 / HD)
    inverse = jnp.power(jnp.float32(THETA), -exponents)
    angles = positions.astype(jnp.float32)[:, None] * inverse[None, :]
    return jnp.cos(angles), jnp.sin(angles)


def rope(values, cosine, sine):
    half = HD // 2
    first, second = values[..., :half], values[..., half:]
    return jnp.concatenate(
        [first * cosine - second * sine, second * cosine + first * sine], axis=-1
    )


def place(ids):
    s, t = ids[0], ids[1]
    return s, t >> 1, t & 1, s >> 2, s & 3


def part_at(ids, kind, shift):
    s, _, core, row, col = place(ids)
    at = (col + ROW - shift) & 3
    if kind == "far":
        there = (core == 0) & (col == 0) & (s >= 33)
        return jnp.where(there, (s - 33) * BLOCK, NOWHERE), BLOCK
    if kind == "half":
        return (row * ROW + at) * BLOCK + core * (BLOCK // 2), BLOCK // 2
    return (jnp.where(core == 0, row - kind, row - 9 + kind) * ROW + at) * BLOCK, BLOCK


def attend_kernel(kinds, fresh, ids, lengths, q_ref, *rest):
    state = rest[-1]
    kept, refs = (None, rest[:-1]) if fresh else (rest[-2], rest[:-2])
    scale = HD**-0.5 * LOG2E
    first_query = ids[0] * BLOCK
    ends, end = [], 0
    for i in range(lengths.shape[0]):
        end = end + lengths[i]
        ends.append(end)
    low_first, low_last = 0, 0
    for end in ends:
        low_first = jnp.where(end <= first_query, end, low_first)
        low_last = jnp.where(end <= first_query + BLOCK - 1, end, low_last)
    parts, bases, none, whole = [], [], True, True
    at, i = 0, 0
    for kind, shift in kinds:
        base, size = part_at(ids, kind, shift)
        parts.append(refs[i].at[at : at + size])
        at += size
        if at == refs[i].shape[0]:
            at, i = 0, i + 1
        bases.append(base)
        dead = (base < 0) | (low_first >= base + size) | (base >= first_query + BLOCK)
        full = (base >= 0) & (low_last <= base) & (base + size <= first_query)
        none, whole = dead & none, full & whole

    def step(lanes, masked):
        q = q_ref[:, lanes]
        if masked:
            high = lax.broadcasted_iota(jnp.int32, (1, WIDE), 1) % BLOCK + first_query
            low = jnp.zeros_like(high)
            for end in ends:
                low = jnp.where(end <= high, end, low)
        scores = []
        for part, base in zip(parts, bases):
            s = jnp.dot(part[:, :HD], q, preferred_element_type=jnp.float32)
            if masked:
                at = lax.broadcasted_iota(jnp.int32, s.shape, 0) + base
                s = jnp.where((at >= low) & (at <= high), s, MASKED)
            scores.append(s)
        s = jnp.concatenate(scores, axis=0) if len(scores) > 1 else scores[0]
        values = [part[:, HD:].T for part in parts]
        values = jnp.concatenate(values, axis=1) if len(values) > 1 else values[0]
        values = jnp.concatenate([values, jnp.ones((16, values.shape[1]), jnp.bfloat16)], axis=0)
        peak = jnp.max(s, axis=0, keepdims=True) * scale
        old = jnp.full_like(peak, EMPTY) if fresh else kept[HD : HD + 1, lanes]
        new = jnp.maximum(old, peak)
        weights = jnp.exp2(s * scale - new).astype(jnp.bfloat16)
        summed = jnp.dot(values, weights, preferred_element_type=jnp.float32)
        denom = summed[HD : HD + 1]
        summed = summed[:HD]
        if not fresh:
            alpha = jnp.exp2(old - new)
            summed = summed + kept[:HD, lanes] * alpha
            denom = denom + kept[HD + 1 : HD + 2, lanes] * alpha
        state[:HD, lanes] = summed
        state[HD:, lanes] = jnp.concatenate([new, denom, jnp.zeros((6, WIDE), jnp.float32)], axis=0)

    def steps(masked):
        def one(i, carry):
            step(pl.ds(pl.multiple_of(i * WIDE, WIDE), WIDE), masked)
            return carry

        lax.fori_loop(0, LANES // WIDE, one, 0)

    if fresh:
        steps(True)
    else:

        @pl.when(none)
        def _():
            state[...] = kept[...]

        @pl.when(whole)
        def _():
            steps(False)

        @pl.when(jnp.logical_not(none | whole))
        def _():
            steps(True)


def attend(ids, lengths, q_all, refs, kinds, state=None):
    operands = list(refs) + ([] if state is None else [state])
    return pl.pallas_call(
        functools.partial(attend_kernel, kinds, state is None),
        out_shape=jax.ShapeDtypeStruct((STATE, LANES), jnp.float32),
        in_specs=[pl.BlockSpec(memory_space=pltpu.SMEM)] * 2
        + [pl.BlockSpec(memory_space=pltpu.VMEM)] * (1 + len(operands)),
        out_specs=pl.BlockSpec(memory_space=pltpu.VMEM),
        input_output_aliases={} if state is None else {2 + len(operands): 0},
        compiler_params=pltpu.CompilerParams(vmem_limit_bytes=32 * MIB),
        cost_estimate=pl.CostEstimate(flops=1, bytes_accessed=1, transcendentals=0),
        name="attend",
    )(ids, lengths, q_all, *operands)


def turn_kernel(queries, cosine, sine, out):
    half = HD // 2
    for h in range(queries.shape[1] // HD):
        x = queries[:, h * HD : (h + 1) * HD].astype(jnp.float32)
        turned = rope(x, cosine[...], sine[...]).astype(jnp.bfloat16)
        out[:, h * BLOCK : (h + 1) * BLOCK] = turned.T


def turn(queries, cosine, sine):
    return pl.pallas_call(
        turn_kernel,
        out_shape=jax.ShapeDtypeStruct((HD, queries.shape[1] // HD * BLOCK), jnp.bfloat16),
        in_specs=[pl.BlockSpec(memory_space=pltpu.VMEM)] * 3,
        out_specs=pl.BlockSpec(memory_space=pltpu.VMEM),
        compiler_params=pltpu.CompilerParams(vmem_limit_bytes=16 * MIB),
        cost_estimate=pl.CostEstimate(flops=1, bytes_accessed=1, transcendentals=0),
        name="turn",
    )(queries, cosine, sine)


def merged(mine, theirs, out):
    for h in range(HEADS):
        a = slice(h * BLOCK, (h + 1) * BLOCK)
        g = (h + HEADS // 2) % HEADS
        b = slice(g * BLOCK, (g + 1) * BLOCK)
        peak_a, peak_b = mine[HD : HD + 1, a], theirs[HD : HD + 1, b]
        peak = jnp.maximum(peak_a, peak_b)
        scale_a, scale_b = jnp.exp2(peak_a - peak), jnp.exp2(peak_b - peak)
        denom = mine[HD + 1 : HD + 2, a] * scale_a + theirs[HD + 1 : HD + 2, b] * scale_b
        summed = mine[:HD, a] * scale_a + theirs[:HD, b] * scale_b
        out[:, h * HD : (h + 1) * HD] = (summed / denom).T.astype(jnp.bfloat16)


def project_kernel(other_side, first, merging, ids, *rest):
    half = HEADS * HD // 2
    _, hi, core, _, _ = place(ids)
    weights, sems = rest[-2:]
    if merging:
        mine, theirs, own_weight, other_weight, attended = rest[:5]
        outs = rest[5:-2]
    else:
        attended, own_weight, other_weight = rest[:3]
        outs = rest[3:-2]
    at = (2 * (1 - hi if other_side else hi) + core) * OUT_COLUMNS + first
    pieces = weights.shape[0]
    for i in range(pieces):
        columns = pl.ds(pl.multiple_of(at + i * TILE, TILE), TILE)
        for j, weight in enumerate((own_weight, other_weight)):
            pltpu.make_async_copy(weight.at[:, columns], weights.at[i, j], sems.at[i, j]).start()
    if merging:
        merged(mine, theirs, attended)
    out, filled = 0, 0
    for i in range(pieces):
        columns = pl.ds(pl.multiple_of(at + i * TILE, TILE), TILE)
        for j, weight in enumerate((own_weight, other_weight)):
            pltpu.make_async_copy(weight.at[:, columns], weights.at[i, j], sems.at[i, j]).wait()
        total = jnp.dot(attended[:, :half], weights[i, 0], preferred_element_type=jnp.float32)
        total += jnp.dot(attended[:, half:], weights[i, 1], preferred_element_type=jnp.float32)
        outs[out][:, filled : filled + TILE] = total.astype(outs[out].dtype)
        filled += TILE
        if filled == outs[out].shape[1]:
            out, filled = out + 1, 0


def project(ids, operands, weights, other_side, first, widths, dtype, merging=False):
    half = HEADS * HD // 2
    shapes = [jax.ShapeDtypeStruct((BLOCK, width), dtype) for width in widths]
    if merging:
        shapes = [jax.ShapeDtypeStruct((BLOCK, 2 * half), jnp.bfloat16)] + shapes
    pieces = sum(widths) // TILE
    vmem = pl.BlockSpec(memory_space=pltpu.VMEM)
    return pl.pallas_call(
        functools.partial(project_kernel, other_side, first, merging),
        out_shape=shapes,
        in_specs=[pl.BlockSpec(memory_space=pltpu.SMEM)]
        + [vmem] * len(operands)
        + [pl.BlockSpec(memory_space=pltpu.HBM)] * 2,
        out_specs=[vmem] * len(shapes),
        scratch_shapes=[
            pltpu.VMEM((pieces, 2, half, TILE), jnp.bfloat16),
            pltpu.SemaphoreType.DMA((pieces, 2)),
        ],
        compiler_params=pltpu.CompilerParams(vmem_limit_bytes=32 * MIB),
        cost_estimate=pl.CostEstimate(flops=1, bytes_accessed=1, transcendentals=0),
        name="project",
    )(ids, *operands, *weights)


def finish_kernel(kept, received, *rest):
    rest[-1][...] = (kept[...] + received[...].astype(jnp.float32)).astype(jnp.bfloat16)


def finish(kept, received, first, out):
    columns, start = received.shape[1], first // TILE
    tile = pl.BlockSpec((BLOCK, TILE), lambda j: (0, start + j))
    in_specs = [tile, pl.BlockSpec((BLOCK, TILE), lambda j: (0, j))]
    operands = [kept, received]
    if out is not None:
        in_specs.append(pl.BlockSpec(memory_space=pl.ANY))
        operands.append(out)
    return pl.pallas_call(
        finish_kernel,
        out_shape=jax.ShapeDtypeStruct(kept.shape, jnp.bfloat16),
        grid=(columns // TILE,),
        in_specs=in_specs,
        out_specs=tile,
        input_output_aliases={} if out is None else {2: 0},
        compiler_params=pltpu.CompilerParams(vmem_limit_bytes=32 * MIB),
        cost_estimate=pl.CostEstimate(
            flops=BLOCK * columns, bytes_accessed=8 * BLOCK * columns, transcendentals=0
        ),
        name="finish",
    )(*operands)


def body(queries, key_heads, value_heads, doc_lengths, out_weight):
    s = lax.axis_index("seq")
    t = lax.axis_index("tensor")
    hi, core = t // 2, t % 2
    ids = jnp.stack([s, t]).astype(jnp.int32)

    query_pos = s * BLOCK + jnp.arange(BLOCK, dtype=jnp.int32)
    cosine, sine = rope_tables(query_pos)
    own_key = lax.dynamic_index_in_dim(key_heads, hi, 1, keepdims=False).astype(jnp.float32)
    own_key = rope(own_key, cosine, sine).astype(jnp.bfloat16)
    own_value = lax.dynamic_index_in_dim(value_heads, hi, 1, keepdims=False)
    block = jnp.concatenate([own_key, own_value], axis=1)

    q_own = turn(queries, cosine, sine)
    q_other = permute(q_own, other_core)
    near = [permute(block, along_rows(step)) for step in (1, 2)]
    far = permute(block, far_block)
    half = lax.dynamic_slice_in_dim(block, core * (BLOCK // 2), BLOCK // 2, 0)
    group_1 = jnp.concatenate([half, *near], axis=0)
    near = jnp.concatenate(near, axis=0)
    group_1, near, q_other, far, out_weight = lax.optimization_barrier(
        (group_1, near, q_other, far, out_weight)
    )
    shifts = (1, -1, 2)
    group_2 = permute(near, two_rows_on)
    columns_1 = [permute(group_1, in_row(shift)) for shift in shifts]
    other_weight = permute(out_weight, other_core)

    q_all = jnp.concatenate([q_own, q_other], axis=1)
    step = functools.partial(attend, ids, doc_lengths, q_all)

    state = step([half, near, group_2], [("half", 0)] + [(k, 0) for k in (1, 2, 3, 4)])
    columns_2 = []
    for shift, keys in zip(shifts, columns_1):
        group_2, state = lax.optimization_barrier((group_2, state))
        columns_2.append(permute(group_2, in_row(shift)))
        kinds = [("half", shift), (1, shift), (2, shift)]
        if shift == 2:
            state = step([keys, far], kinds + [("far", 0)], state)
        else:
            state = step([keys], kinds, state)
    state, other_weight = lax.optimization_barrier((state, other_weight))
    weights = (out_weight, other_weight)
    for shift, keys in zip(shifts, columns_2):
        state = step([keys], [(3, shift), (4, shift)], state)

    theirs = permute(state, other_core)
    attended, partial = project(ids, (state, theirs), weights, True, 0, (512,), jnp.bfloat16, True)
    received = [permute(partial, other_hi)]
    for partial in project(ids, (attended,), weights, True, 512, (512,) * 3, jnp.bfloat16):
        received.append(permute(partial, other_hi))
    (kept,) = project(ids, (attended,), weights, False, 0, (OUT_COLUMNS,), jnp.float32)
    out, first = None, 0
    for piece in received:
        out = finish(kept, piece, first, out)
        first += piece.shape[1]
    return out


def solution(mesh):
    return jax.shard_map(
        body,
        mesh=mesh,
        in_specs=(
            P("seq", "tensor"),
            P("seq", None, None),
            P("seq", None, None),
            P(),
            P("tensor", None),
        ),
        out_specs=P("seq", "tensor"),
        check_vma=False,
    )
```

```python
import functools
import math

import jax
import jax.numpy as jnp
from jax import lax
from jax.experimental import pallas as pl
from jax.experimental.pallas import tpu as pltpu
from jax.sharding import PartitionSpec as P

HQ = 16
KVH = 2
HD = 128
SEQ = 64
TENSOR = 4
ROW = 4
THETA = 500000.0
EMPTY = -1e30
MASKED = -1e32
LOG2E = math.log2(math.e)
BLOCK = 256
ROW_TOKENS = ROW * BLOCK
HEADS = 8
LANES = HEADS * BLOCK
STATE = HD + 8
TILE = 512
NOWHERE = 1 << 24
OUT_COLUMNS = 2048
MIB = 1024 * 1024


def device_perm(move):
    pairs = []
    for s in range(SEQ):
        for hi in range(2):
            for core in range(2):
                to = move(s, hi, core)
                if to is not None:
                    pairs.append((s * TENSOR + hi * 2 + core, to[0] * TENSOR + to[1] * 2 + to[2]))
    return pairs


def permute(x, move):
    return lax.ppermute(x, ("seq", "tensor"), device_perm(move))


def in_row(shift):
    return lambda s, hi, core: (s - s % ROW + (s + shift) % ROW, hi, core)


def other_core(s, hi, core):
    return s, hi, 1 - core


def other_hi(s, hi, core):
    return s, 1 - hi, core


def far_block(s, hi, core):
    if core == 0 and s % ROW == ROW - 1 and s + 33 < SEQ:
        return s + 33, hi, core
    return None


def along_rows(step):
    def move(s, hi, core):
        if core == 0:
            return (s + step * ROW, hi, core) if s + step * ROW < SEQ else None
        return (s + (9 - step) * ROW) % SEQ, hi, core

    return move


def two_rows_on(s, hi, core):
    if core == 0:
        return (s + 2 * ROW, hi, core) if s + 2 * ROW < SEQ else None
    return (s - 2 * ROW) % SEQ, hi, core


def rope_tables(positions):
    half = HD // 2
    exponents = jnp.arange(half, dtype=jnp.float32) * (2.0 / HD)
    inverse = jnp.power(jnp.float32(THETA), -exponents)
    angles = positions.astype(jnp.float32)[:, None] * inverse[None, :]
    return jnp.cos(angles), jnp.sin(angles)


def rope(values, cosine, sine):
    half = HD // 2
    first, second = values[..., :half], values[..., half:]
    return jnp.concatenate(
        [first * cosine - second * sine, second * cosine + first * sine], axis=-1
    )


def place(ids):
    s, t = ids[0], ids[1]
    return s, t >> 1, t & 1, s >> 2, s & 3


def part_at(ids, kind, shift):
    s, _, core, row, col = place(ids)
    at = (col + ROW - shift) & 3
    if kind == "far":
        there = (core == 0) & (col == 0) & (s >= 33)
        return jnp.where(there, (s - 33) * BLOCK, NOWHERE), BLOCK
    if kind == "half":
        return (row * ROW + at) * BLOCK + core * (BLOCK // 2), BLOCK // 2
    return (jnp.where(core == 0, row - kind, row - 9 + kind) * ROW + at) * BLOCK, BLOCK


def attend_kernel(kinds, fresh, ids, q_ref, *rest):
    state = rest[-1]
    kept, refs = (None, rest[:-1]) if fresh else (rest[-2], rest[:-2])
    scale = HD**-0.5 * LOG2E
    first_query = ids[0] * BLOCK
    ends, end = [], 0
    for i in range(2, ids.shape[0]):
        end = end + ids[i]
        ends.append(end)
    low_first, low_last = 0, 0
    for end in ends:
        low_first = jnp.where(end <= first_query, end, low_first)
        low_last = jnp.where(end <= first_query + BLOCK - 1, end, low_last)
    parts, bases, none, whole = [], [], True, True
    at, i = 0, 0
    for kind, shift in kinds:
        base, size = part_at(ids, kind, shift)
        parts.append(refs[i].at[at : at + size])
        at += size
        if at == refs[i].shape[0]:
            at, i = 0, i + 1
        bases.append(base)
        dead = (base < 0) | (low_first >= base + size) | (base >= first_query + BLOCK)
        full = (base >= 0) & (low_last <= base) & (base + size <= first_query)
        none, whole = dead & none, full & whole

    def step(masked):
        q = q_ref[...]
        if masked:
            high = lax.broadcasted_iota(jnp.int32, (1, LANES), 1) % BLOCK + first_query
            low = jnp.zeros_like(high)
            for end in ends:
                low = jnp.where(end <= high, end, low)
        scores = []
        for part, base in zip(parts, bases):
            s = jnp.dot(part[:, :HD], q, preferred_element_type=jnp.float32)
            if masked:
                at = lax.broadcasted_iota(jnp.int32, s.shape, 0) + base
                s = jnp.where((at >= low) & (at <= high), s, MASKED)
            scores.append(s)
        s = jnp.concatenate(scores, axis=0) if len(scores) > 1 else scores[0]
        values = [part[:, HD:].T for part in parts]
        values = jnp.concatenate(values, axis=1) if len(values) > 1 else values[0]
        values = jnp.concatenate([values, jnp.ones((16, values.shape[1]), jnp.bfloat16)], axis=0)
        peak = jnp.max(s, axis=0, keepdims=True) * scale
        old = jnp.full_like(peak, EMPTY) if fresh else kept[HD : HD + 1, :]
        new = jnp.maximum(old, peak)
        weights = jnp.exp2(s * scale - new).astype(jnp.bfloat16)
        summed = jnp.dot(values, weights, preferred_element_type=jnp.float32)
        denom = summed[HD : HD + 1]
        summed = summed[:HD]
        if not fresh:
            alpha = jnp.exp2(old - new)
            summed = summed + kept[:HD, :] * alpha
            denom = denom + kept[HD + 1 : HD + 2, :] * alpha
        state[:HD, :] = summed
        state[HD:, :] = jnp.concatenate([new, denom, jnp.zeros((6, LANES), jnp.float32)], axis=0)

    if fresh:
        step(True)
    else:

        @pl.when(none)
        def _():
            state[...] = kept[...]

        @pl.when(whole)
        def _():
            step(False)

        @pl.when(jnp.logical_not(none | whole))
        def _():
            step(True)


def attend(ids, q_all, refs, kinds, state=None):
    operands = list(refs) + ([] if state is None else [state])
    return pl.pallas_call(
        functools.partial(attend_kernel, kinds, state is None),
        out_shape=jax.ShapeDtypeStruct((STATE, LANES), jnp.float32),
        in_specs=[pl.BlockSpec(memory_space=pltpu.SMEM)]
        + [pl.BlockSpec(memory_space=pltpu.VMEM)] * (1 + len(operands)),
        out_specs=pl.BlockSpec(memory_space=pltpu.VMEM),
        input_output_aliases={} if state is None else {1 + len(operands): 0},
        compiler_params=pltpu.CompilerParams(vmem_limit_bytes=32 * MIB),
        cost_estimate=pl.CostEstimate(flops=1, bytes_accessed=1, transcendentals=0),
        name="attend",
    )(ids, q_all, *operands)


def turn_kernel(queries, cosine, sine, out):
    half = HD // 2
    for h in range(queries.shape[1] // HD):
        x = queries[:, h * HD : (h + 1) * HD].astype(jnp.float32)
        turned = rope(x, cosine[...], sine[...]).astype(jnp.bfloat16)
        out[:, h * BLOCK : (h + 1) * BLOCK] = turned.T


def turn(queries, cosine, sine):
    return pl.pallas_call(
        turn_kernel,
        out_shape=jax.ShapeDtypeStruct((HD, queries.shape[1] // HD * BLOCK), jnp.bfloat16),
        in_specs=[pl.BlockSpec(memory_space=pltpu.VMEM)] * 3,
        out_specs=pl.BlockSpec(memory_space=pltpu.VMEM),
        compiler_params=pltpu.CompilerParams(vmem_limit_bytes=16 * MIB),
        cost_estimate=pl.CostEstimate(flops=1, bytes_accessed=1, transcendentals=0),
        name="turn",
    )(queries, cosine, sine)


def merged(mine, theirs, out):
    for h in range(HEADS):
        a = slice(h * BLOCK, (h + 1) * BLOCK)
        g = (h + HEADS // 2) % HEADS
        b = slice(g * BLOCK, (g + 1) * BLOCK)
        peak_a, peak_b = mine[HD : HD + 1, a], theirs[HD : HD + 1, b]
        peak = jnp.maximum(peak_a, peak_b)
        scale_a, scale_b = jnp.exp2(peak_a - peak), jnp.exp2(peak_b - peak)
        denom = mine[HD + 1 : HD + 2, a] * scale_a + theirs[HD + 1 : HD + 2, b] * scale_b
        summed = mine[:HD, a] * scale_a + theirs[:HD, b] * scale_b
        out[:, h * HD : (h + 1) * HD] = (summed / denom).T.astype(jnp.bfloat16)


def project_kernel(other_side, first, merging, ids, *rest):
    half = HEADS * HD // 2
    _, hi, core, _, _ = place(ids)
    weights, sems = rest[-2:]
    if merging:
        mine, theirs, own_weight, other_weight, attended = rest[:5]
        outs = rest[5:-2]
    else:
        attended, own_weight, other_weight = rest[:3]
        outs = rest[3:-2]
    at = (2 * (1 - hi if other_side else hi) + core) * OUT_COLUMNS + first
    pieces = weights.shape[0]
    for i in range(pieces):
        columns = pl.ds(pl.multiple_of(at + i * TILE, TILE), TILE)
        for j, weight in enumerate((own_weight, other_weight)):
            pltpu.make_async_copy(weight.at[:, columns], weights.at[i, j], sems.at[i, j]).start()
    if merging:
        merged(mine, theirs, attended)
    out, filled = 0, 0
    for i in range(pieces):
        columns = pl.ds(pl.multiple_of(at + i * TILE, TILE), TILE)
        for j, weight in enumerate((own_weight, other_weight)):
            pltpu.make_async_copy(weight.at[:, columns], weights.at[i, j], sems.at[i, j]).wait()
        total = jnp.dot(attended[:, :half], weights[i, 0], preferred_element_type=jnp.float32)
        total += jnp.dot(attended[:, half:], weights[i, 1], preferred_element_type=jnp.float32)
        outs[out][:, filled : filled + TILE] = total.astype(outs[out].dtype)
        filled += TILE
        if filled == outs[out].shape[1]:
            out, filled = out + 1, 0


def project(ids, operands, weights, other_side, first, widths, dtype, merging=False):
    half = HEADS * HD // 2
    shapes = [jax.ShapeDtypeStruct((BLOCK, width), dtype) for width in widths]
    if merging:
        shapes = [jax.ShapeDtypeStruct((BLOCK, 2 * half), jnp.bfloat16)] + shapes
    pieces = sum(widths) // TILE
    vmem = pl.BlockSpec(memory_space=pltpu.VMEM)
    return pl.pallas_call(
        functools.partial(project_kernel, other_side, first, merging),
        out_shape=shapes,
        in_specs=[pl.BlockSpec(memory_space=pltpu.SMEM)]
        + [vmem] * len(operands)
        + [pl.BlockSpec(memory_space=pltpu.HBM)] * 2,
        out_specs=[vmem] * len(shapes),
        scratch_shapes=[
            pltpu.VMEM((pieces, 2, half, TILE), jnp.bfloat16),
            pltpu.SemaphoreType.DMA((pieces, 2)),
        ],
        compiler_params=pltpu.CompilerParams(vmem_limit_bytes=32 * MIB),
        cost_estimate=pl.CostEstimate(flops=1, bytes_accessed=1, transcendentals=0),
        name="project",
    )(ids, *operands, *weights)


def finish_kernel(kept, received, *rest):
    rest[-1][...] = (kept[...] + received[...].astype(jnp.float32)).astype(jnp.bfloat16)


def finish(kept, received, first, out):
    columns, start = received.shape[1], first // TILE
    tile = pl.BlockSpec((BLOCK, TILE), lambda j: (0, start + j))
    in_specs = [tile, pl.BlockSpec((BLOCK, TILE), lambda j: (0, j))]
    operands = [kept, received]
    if out is not None:
        in_specs.append(pl.BlockSpec(memory_space=pl.ANY))
        operands.append(out)
    return pl.pallas_call(
        finish_kernel,
        out_shape=jax.ShapeDtypeStruct(kept.shape, jnp.bfloat16),
        grid=(columns // TILE,),
        in_specs=in_specs,
        out_specs=tile,
        input_output_aliases={} if out is None else {2: 0},
        compiler_params=pltpu.CompilerParams(vmem_limit_bytes=32 * MIB),
        cost_estimate=pl.CostEstimate(
            flops=BLOCK * columns, bytes_accessed=8 * BLOCK * columns, transcendentals=0
        ),
        name="finish",
    )(*operands)


def body(queries, key_heads, value_heads, doc_lengths, out_weight):
    s = lax.axis_index("seq")
    t = lax.axis_index("tensor")
    hi, core = t // 2, t % 2
    ids = jnp.concatenate([jnp.stack([s, t]).astype(jnp.int32), doc_lengths])

    query_pos = s * BLOCK + jnp.arange(BLOCK, dtype=jnp.int32)
    cosine, sine = rope_tables(query_pos)
    own_key = lax.dynamic_index_in_dim(key_heads, hi, 1, keepdims=False).astype(jnp.float32)
    own_key = rope(own_key, cosine, sine).astype(jnp.bfloat16)
    own_value = lax.dynamic_index_in_dim(value_heads, hi, 1, keepdims=False)
    block = jnp.concatenate([own_key, own_value], axis=1)

    q_own = turn(queries, cosine, sine)
    q_other = permute(q_own, other_core)
    near = [permute(block, along_rows(step)) for step in (1, 2)]
    far = permute(block, far_block)
    half = lax.dynamic_slice_in_dim(block, core * (BLOCK // 2), BLOCK // 2, 0)
    group_1 = jnp.concatenate([half, *near], axis=0)
    near = jnp.concatenate(near, axis=0)
    group_1, near, q_other, far, out_weight = lax.optimization_barrier(
        (group_1, near, q_other, far, out_weight)
    )
    shifts = (1, -1, 2)
    group_2 = permute(near, two_rows_on)
    columns_1 = [permute(group_1, in_row(shift)) for shift in shifts]
    other_weight = permute(out_weight, other_core)

    q_all = jnp.concatenate([q_own, q_other], axis=1)
    step = functools.partial(attend, ids, q_all)

    state = step([half, near], [("half", 0), (1, 0), (2, 0)])
    rows_2 = lambda shift: [(3, shift), (4, shift)]
    columns_2 = []
    for shift, keys in zip(shifts, columns_1):
        group_2, state = lax.optimization_barrier((group_2, state))
        columns_2.append(permute(group_2, in_row(shift)))
        refs, kinds = [keys], [("half", shift), (1, shift), (2, shift)]
        if shift == 1:
            refs, kinds = [group_2] + refs, rows_2(0) + kinds
        if shift == 2:
            refs, kinds = refs + [far], kinds + [("far", 0)]
        state = step(refs, kinds, state)
    state, other_weight = lax.optimization_barrier((state, other_weight))
    weights = (out_weight, other_weight)
    state = step(columns_2[:2], rows_2(1) + rows_2(-1), state)
    state = step(columns_2[2:], rows_2(2), state)

    theirs = permute(state, other_core)
    attended, partial = project(ids, (state, theirs), weights, True, 0, (512,), jnp.bfloat16, True)
    received = [permute(partial, other_hi)]
    for partial in project(ids, (attended,), weights, True, 512, (512,) * 3, jnp.bfloat16):
        received.append(permute(partial, other_hi))
    (kept,) = project(ids, (attended,), weights, False, 0, (OUT_COLUMNS,), jnp.float32)
    out, first = None, 0
    for piece in received:
        out = finish(kept, piece, first, out)
        first += piece.shape[1]
    return out


def solution(mesh):
    return jax.shard_map(
        body,
        mesh=mesh,
        in_specs=(
            P("seq", "tensor"),
            P("seq", None, None),
            P("seq", None, None),
            P(),
            P("tensor", None),
        ),
        out_specs=P("seq", "tensor"),
        check_vma=False,
    )
```

```python
import functools
import math

import jax
import jax.numpy as jnp
from jax import lax
from jax.experimental import pallas as pl
from jax.experimental.pallas import tpu as pltpu
from jax.sharding import PartitionSpec as P

HQ = 16
KVH = 2
HD = 128
SEQ = 64
TENSOR = 4
ROW = 4
THETA = 500000.0
EMPTY = -1e30
MASKED = -1e32
LOG2E = math.log2(math.e)
BLOCK = 256
ROW_TOKENS = ROW * BLOCK
HEADS = 8
LANES = HEADS * BLOCK
STATE = HD + 8
TILE = 512
NOWHERE = -(1 << 24)
OUT_COLUMNS = 2048
MIB = 1024 * 1024


def device_perm(move):
    pairs = []
    for s in range(SEQ):
        for hi in range(2):
            for core in range(2):
                to = move(s, hi, core)
                if to is not None:
                    pairs.append((s * TENSOR + hi * 2 + core, to[0] * TENSOR + to[1] * 2 + to[2]))
    return pairs


def permute(x, move):
    return lax.ppermute(x, ("seq", "tensor"), device_perm(move))


def in_row(shift):
    return lambda s, hi, core: (s - s % ROW + (s + shift) % ROW, hi, core)


def other_core(s, hi, core):
    return s, hi, 1 - core


def other_hi(s, hi, core):
    return s, 1 - hi, core


def far_block(s, hi, core):
    if core == 0 and s % ROW == ROW - 1 and s + 33 < SEQ:
        return s + 33, hi, core
    return None


def along_rows(step):
    def move(s, hi, core):
        if core == 0:
            return (s + step * ROW, hi, core) if s + step * ROW < SEQ else None
        return (s + (9 - step) * ROW) % SEQ, hi, core

    return move


def two_rows_on(s, hi, core):
    if core == 0:
        return (s + 2 * ROW, hi, core) if s + 2 * ROW < SEQ else None
    return (s - 2 * ROW) % SEQ, hi, core


def rope_tables(positions):
    half = HD // 2
    exponents = jnp.arange(half, dtype=jnp.float32) * (2.0 / HD)
    inverse = jnp.power(jnp.float32(THETA), -exponents)
    angles = positions.astype(jnp.float32)[:, None] * inverse[None, :]
    return jnp.cos(angles), jnp.sin(angles)


def rope(values, cosine, sine):
    half = HD // 2
    first, second = values[..., :half], values[..., half:]
    return jnp.concatenate(
        [first * cosine - second * sine, second * cosine + first * sine], axis=-1
    )


def place():
    s, t = lax.axis_index("seq"), lax.axis_index("tensor")
    return s, t >> 1, t & 1, s >> 2, s & 3


def part_at(kind, shift):
    s, _, core, row, col = place()
    at = (col + ROW - shift) & 3
    if kind == "far":
        there = (core == 0) & (col == 0) & (s >= 33)
        return jnp.where(there, (s - 33) * BLOCK, NOWHERE), BLOCK
    if kind == "half":
        base = (row * ROW + at) * BLOCK + core * (BLOCK // 2)
        return jnp.where(at > col, NOWHERE, base), BLOCK // 2
    return (jnp.where(core == 0, row - kind, row - 9 + kind) * ROW + at) * BLOCK, BLOCK


def attend_kernel(kinds, fresh, q_ref, low_ref, *rest):
    state = rest[-1]
    kept, refs = (None, rest[:-1]) if fresh else (rest[-2], rest[:-2])
    scale = HD**-0.5 * LOG2E
    first_query = place()[0] * BLOCK
    low_first = jnp.min(low_ref[0:1, 0:HD])
    parts, bases, none = [], [], True
    at, i = 0, 0
    for kind, shift in kinds:
        base, size = part_at(kind, shift)
        parts.append(refs[i].at[at : at + size])
        at += size
        if at == refs[i].shape[0]:
            at, i = 0, i + 1
        bases.append(base)
        none = (low_first >= base + size) & none

    def step():
        q = q_ref[...]
        low = low_ref[0:1, :]
        scores = []
        for part, base, kind in zip(parts, bases, kinds):
            s = jnp.dot(part[:, :HD], q, preferred_element_type=jnp.float32)
            at = lax.broadcasted_iota(jnp.int32, s.shape, 0)
            live = at >= low - base
            if kind == ("half", 0):
                query = lax.broadcasted_iota(jnp.int32, (1, LANES), 1) % BLOCK + first_query
                live = live & (at <= query - base)
            scores.append(jnp.where(live, s, MASKED))
        s = jnp.concatenate(scores, axis=0) if len(scores) > 1 else scores[0]
        values = [part[:, HD:].T for part in parts]
        values = jnp.concatenate(values, axis=1) if len(values) > 1 else values[0]
        values = jnp.concatenate([values, jnp.ones((16, values.shape[1]), jnp.bfloat16)], axis=0)
        peak = jnp.max(s, axis=0, keepdims=True) * scale
        old = jnp.full_like(peak, EMPTY) if fresh else kept[HD : HD + 1, :]
        new = jnp.maximum(old, peak)
        weights = jnp.exp2(s * scale - new).astype(jnp.bfloat16)
        summed = jnp.dot(values, weights, preferred_element_type=jnp.float32)
        denom = summed[HD : HD + 1]
        summed = summed[:HD]
        if not fresh:
            alpha = jnp.exp2(old - new)
            summed = summed + kept[:HD, :] * alpha
            denom = denom + kept[HD + 1 : HD + 2, :] * alpha
        state[:HD, :] = summed
        state[HD:, :] = jnp.concatenate([new, denom, jnp.zeros((6, LANES), jnp.float32)], axis=0)

    if fresh:
        step()
    else:

        @pl.when(none)
        def _():
            state[...] = kept[...]

        @pl.when(jnp.logical_not(none))
        def _():
            step()


def attend(q_all, low, refs, kinds, state=None):
    operands = list(refs) + ([] if state is None else [state])
    return pl.pallas_call(
        functools.partial(attend_kernel, kinds, state is None),
        out_shape=jax.ShapeDtypeStruct((STATE, LANES), jnp.float32),
        in_specs=[pl.BlockSpec(memory_space=pltpu.VMEM)] * (2 + len(operands)),
        out_specs=pl.BlockSpec(memory_space=pltpu.VMEM),
        input_output_aliases={} if state is None else {1 + len(operands): 0},
        compiler_params=pltpu.CompilerParams(vmem_limit_bytes=32 * MIB),
        cost_estimate=pl.CostEstimate(flops=1, bytes_accessed=1, transcendentals=0),
        name="attend",
    )(q_all, low, *operands)


def turn_kernel(queries, cosine, sine, out):
    half = HD // 2
    for h in range(queries.shape[1] // HD):
        x = queries[:, h * HD : (h + 1) * HD].astype(jnp.float32)
        turned = rope(x, cosine[...], sine[...]).astype(jnp.bfloat16)
        out[:, h * BLOCK : (h + 1) * BLOCK] = turned.T


def turn(queries, cosine, sine):
    return pl.pallas_call(
        turn_kernel,
        out_shape=jax.ShapeDtypeStruct((HD, queries.shape[1] // HD * BLOCK), jnp.bfloat16),
        in_specs=[pl.BlockSpec(memory_space=pltpu.VMEM)] * 3,
        out_specs=pl.BlockSpec(memory_space=pltpu.VMEM),
        compiler_params=pltpu.CompilerParams(vmem_limit_bytes=16 * MIB),
        cost_estimate=pl.CostEstimate(flops=1, bytes_accessed=1, transcendentals=0),
        name="turn",
    )(queries, cosine, sine)


def merged(mine, theirs, out):
    for h in range(HEADS):
        a = slice(h * BLOCK, (h + 1) * BLOCK)
        g = (h + HEADS // 2) % HEADS
        b = slice(g * BLOCK, (g + 1) * BLOCK)
        peak_a, peak_b = mine[HD : HD + 1, a], theirs[HD : HD + 1, b]
        peak = jnp.maximum(peak_a, peak_b)
        scale_a, scale_b = jnp.exp2(peak_a - peak), jnp.exp2(peak_b - peak)
        denom = mine[HD + 1 : HD + 2, a] * scale_a + theirs[HD + 1 : HD + 2, b] * scale_b
        summed = mine[:HD, a] * scale_a + theirs[:HD, b] * scale_b
        out[:, h * HD : (h + 1) * HD] = (summed / denom).T.astype(jnp.bfloat16)


def project_kernel(other_side, first, merging, *rest):
    half = HEADS * HD // 2
    _, hi, core, _, _ = place()
    weights, sems = rest[-2:]
    if merging:
        mine, theirs, own_weight, other_weight, attended = rest[:5]
        outs = rest[5:-2]
    else:
        attended, own_weight, other_weight = rest[:3]
        outs = rest[3:-2]
    at = (2 * (1 - hi if other_side else hi) + core) * OUT_COLUMNS + first
    pieces = weights.shape[0]
    for i in range(pieces):
        columns = pl.ds(pl.multiple_of(at + i * TILE, TILE), TILE)
        for j, weight in enumerate((own_weight, other_weight)):
            pltpu.make_async_copy(weight.at[:, columns], weights.at[i, j], sems.at[i, j]).start()
    if merging:
        merged(mine, theirs, attended)
    out, filled = 0, 0
    for i in range(pieces):
        columns = pl.ds(pl.multiple_of(at + i * TILE, TILE), TILE)
        for j, weight in enumerate((own_weight, other_weight)):
            pltpu.make_async_copy(weight.at[:, columns], weights.at[i, j], sems.at[i, j]).wait()
        total = jnp.dot(attended[:, :half], weights[i, 0], preferred_element_type=jnp.float32)
        total += jnp.dot(attended[:, half:], weights[i, 1], preferred_element_type=jnp.float32)
        outs[out][:, filled : filled + TILE] = total.astype(outs[out].dtype)
        filled += TILE
        if filled == outs[out].shape[1]:
            out, filled = out + 1, 0


def project(operands, weights, other_side, first, widths, dtype, merging=False):
    half = HEADS * HD // 2
    shapes = [jax.ShapeDtypeStruct((BLOCK, width), dtype) for width in widths]
    if merging:
        shapes = [jax.ShapeDtypeStruct((BLOCK, 2 * half), jnp.bfloat16)] + shapes
    pieces = sum(widths) // TILE
    vmem = pl.BlockSpec(memory_space=pltpu.VMEM)
    return pl.pallas_call(
        functools.partial(project_kernel, other_side, first, merging),
        out_shape=shapes,
        in_specs=[vmem] * len(operands)
        + [pl.BlockSpec(memory_space=pltpu.HBM)] * 2,
        out_specs=[vmem] * len(shapes),
        scratch_shapes=[
            pltpu.VMEM((pieces, 2, half, TILE), jnp.bfloat16),
            pltpu.SemaphoreType.DMA((pieces, 2)),
        ],
        compiler_params=pltpu.CompilerParams(vmem_limit_bytes=32 * MIB),
        cost_estimate=pl.CostEstimate(flops=1, bytes_accessed=1, transcendentals=0),
        name="project",
    )(*operands, *weights)


def finish_kernel(kept, received, *rest):
    rest[-1][...] = (kept[...] + received[...].astype(jnp.float32)).astype(jnp.bfloat16)


def finish(kept, received, first, out):
    columns, start = received.shape[1], first // TILE
    tile = pl.BlockSpec((BLOCK, TILE), lambda j: (0, start + j))
    in_specs = [tile, pl.BlockSpec((BLOCK, TILE), lambda j: (0, j))]
    operands = [kept, received]
    if out is not None:
        in_specs.append(pl.BlockSpec(memory_space=pl.ANY))
        operands.append(out)
    return pl.pallas_call(
        finish_kernel,
        out_shape=jax.ShapeDtypeStruct(kept.shape, jnp.bfloat16),
        grid=(columns // TILE,),
        in_specs=in_specs,
        out_specs=tile,
        input_output_aliases={} if out is None else {2: 0},
        compiler_params=pltpu.CompilerParams(vmem_limit_bytes=32 * MIB),
        cost_estimate=pl.CostEstimate(
            flops=BLOCK * columns, bytes_accessed=8 * BLOCK * columns, transcendentals=0
        ),
        name="finish",
    )(*operands)


def body(queries, key_heads, value_heads, doc_lengths, out_weight):
    s = lax.axis_index("seq")
    t = lax.axis_index("tensor")
    hi, core = t // 2, t % 2

    query_pos = s * BLOCK + jnp.arange(BLOCK, dtype=jnp.int32)
    cosine, sine = rope_tables(query_pos)
    own_key = lax.dynamic_index_in_dim(key_heads, hi, 1, keepdims=False).astype(jnp.float32)
    own_key = rope(own_key, cosine, sine).astype(jnp.bfloat16)
    own_value = lax.dynamic_index_in_dim(value_heads, hi, 1, keepdims=False)
    block = jnp.concatenate([own_key, own_value], axis=1)

    q_own = turn(queries, cosine, sine)
    q_other = permute(q_own, other_core)
    near = [permute(block, along_rows(step)) for step in (1, 2)]
    far = permute(block, far_block)
    half = lax.dynamic_slice_in_dim(block, core * (BLOCK // 2), BLOCK // 2, 0)
    group_1 = jnp.concatenate([half, *near], axis=0)
    near = jnp.concatenate(near, axis=0)
    group_1, near, q_other, far, out_weight = lax.optimization_barrier(
        (group_1, near, q_other, far, out_weight)
    )
    other_weight = permute(out_weight, other_core)
    shifts = (1, -1, 2)
    group_2 = permute(near, two_rows_on)
    columns_1 = [permute(group_1, in_row(shift)) for shift in shifts]

    q_all = jnp.concatenate([q_own, q_other], axis=1)
    doc_ends = jnp.cumsum(doc_lengths)
    low = jnp.max(jnp.where(doc_ends[:, None] <= query_pos[None], doc_ends[:, None], 0), axis=0)
    low = jnp.broadcast_to(low, (8, HEADS, BLOCK)).reshape(8, LANES)
    step = functools.partial(attend, q_all, low)

    state = step([half, near], [("half", 0), (1, 0), (2, 0)])
    rows_2 = lambda shift: [(3, shift), (4, shift)]
    columns_2 = []
    for shift, keys in zip(shifts, columns_1):
        group_2, state = lax.optimization_barrier((group_2, state))
        columns_2.append(permute(group_2, in_row(shift)))
        refs, kinds = [keys], [("half", shift), (1, shift), (2, shift)]
        if shift == 1:
            refs, kinds = [group_2] + refs, rows_2(0) + kinds
        if shift == 2:
            refs, kinds = refs + [far], kinds + [("far", 0)]
        state = step(refs, kinds, state)
    state, other_weight = lax.optimization_barrier((state, other_weight))
    weights = (out_weight, other_weight)
    state = step(columns_2[:2], rows_2(1) + rows_2(-1), state)
    state = step(columns_2[2:], rows_2(2), state)

    theirs = permute(state, other_core)
    attended, partial = project((state, theirs), weights, True, 0, (512,), jnp.bfloat16, True)
    received = [permute(partial, other_hi)]
    for partial in project((attended,), weights, True, 512, (512,) * 3, jnp.bfloat16):
        received.append(permute(partial, other_hi))
    (kept,) = project((attended,), weights, False, 0, (OUT_COLUMNS,), jnp.float32)
    out, first = None, 0
    for piece in received:
        out = finish(kept, piece, first, out)
        first += piece.shape[1]
    return out


def solution(mesh):
    return jax.shard_map(
        body,
        mesh=mesh,
        in_specs=(
            P("seq", "tensor"),
            P("seq", None, None),
            P("seq", None, None),
            P(),
            P("tensor", None),
        ),
        out_specs=P("seq", "tensor"),
        check_vma=False,
    )
```

```python
import functools
import math

import jax
import jax.numpy as jnp
from jax import lax
from jax.experimental import pallas as pl
from jax.experimental.pallas import tpu as pltpu
from jax.sharding import PartitionSpec as P

HQ = 16
KVH = 2
HD = 128
SEQ = 64
TENSOR = 4
ROW = 4
THETA = 500000.0
EMPTY = -1e30
MASKED = -1e32
LOG2E = math.log2(math.e)
BLOCK = 256
ROW_TOKENS = ROW * BLOCK
HEADS = 8
LANES = HEADS * BLOCK
STATE = HD + 8
TILE = 512
NOWHERE = -(1 << 24)
OUT_COLUMNS = 2048
MIB = 1024 * 1024


def device_perm(move):
    pairs = []
    for s in range(SEQ):
        for hi in range(2):
            for core in range(2):
                to = move(s, hi, core)
                if to is not None:
                    pairs.append((s * TENSOR + hi * 2 + core, to[0] * TENSOR + to[1] * 2 + to[2]))
    return pairs


def permute(x, move):
    return lax.ppermute(x, ("seq", "tensor"), device_perm(move))


def in_row(shift):
    return lambda s, hi, core: (s - s % ROW + (s + shift) % ROW, hi, core)


def other_core(s, hi, core):
    return s, hi, 1 - core


def other_hi(s, hi, core):
    return s, 1 - hi, core


def far_block(s, hi, core):
    if core == 0 and s % ROW == ROW - 1 and s + 33 < SEQ:
        return s + 33, hi, core
    return None


def along_rows(step):
    def move(s, hi, core):
        if core == 0:
            return (s + step * ROW, hi, core) if s + step * ROW < SEQ else None
        return (s + (9 - step) * ROW) % SEQ, hi, core

    return move


def two_rows_on(s, hi, core):
    if core == 0:
        return (s + 2 * ROW, hi, core) if s + 2 * ROW < SEQ else None
    return (s - 2 * ROW) % SEQ, hi, core


def rope_tables(positions):
    half = HD // 2
    exponents = jnp.arange(half, dtype=jnp.float32) * (2.0 / HD)
    inverse = jnp.power(jnp.float32(THETA), -exponents)
    angles = positions.astype(jnp.float32)[:, None] * inverse[None, :]
    return jnp.cos(angles), jnp.sin(angles)


def rope(values, cosine, sine):
    half = HD // 2
    first, second = values[..., :half], values[..., half:]
    return jnp.concatenate(
        [first * cosine - second * sine, second * cosine + first * sine], axis=-1
    )


def place():
    s, t = lax.axis_index("seq"), lax.axis_index("tensor")
    return s, t >> 1, t & 1, s >> 2, s & 3


def part_at(kind, shift):
    s, _, core, row, col = place()
    at = (col + ROW - shift) & 3
    if kind == "far":
        there = (core == 0) & (col == 0) & (s >= 33)
        return jnp.where(there, (s - 33) * BLOCK, NOWHERE), BLOCK
    if kind == "half":
        base = (row * ROW + at) * BLOCK + core * (BLOCK // 2)
        return jnp.where(at > col, NOWHERE, base), BLOCK // 2
    return (jnp.where(core == 0, row - kind, row - 9 + kind) * ROW + at) * BLOCK, BLOCK


def attend_kernel(kinds, fresh, q_ref, low_ref, *rest):
    state = rest[-1]
    kept, refs = (None, rest[:-1]) if fresh else (rest[-2], rest[:-2])
    scale = HD**-0.5 * LOG2E
    first_query = place()[0] * BLOCK
    low_first = jnp.min(low_ref[0:1, 0:HD])
    parts, bases, none = [], [], True
    at, i = 0, 0
    for kind, shift in kinds:
        base, size = part_at(kind, shift)
        parts.append(refs[i].at[at : at + size])
        at += size
        if at == refs[i].shape[0]:
            at, i = 0, i + 1
        bases.append(base)
        none = (low_first >= base + size) & none

    def step():
        q = q_ref[...]
        low = low_ref[0:1, :]
        scores = []
        for part, base, kind in zip(parts, bases, kinds):
            s = jnp.dot(part[:, :HD], q, preferred_element_type=jnp.float32)
            at = lax.broadcasted_iota(jnp.int32, s.shape, 0)
            live = at >= low - base
            if kind == ("half", 0):
                query = lax.broadcasted_iota(jnp.int32, (1, LANES), 1) % BLOCK + first_query
                live = live & (at <= query - base)
            scores.append(jnp.where(live, s, MASKED))
        s = jnp.concatenate(scores, axis=0) if len(scores) > 1 else scores[0]
        values = [part[:, HD:].T for part in parts]
        values = jnp.concatenate(values, axis=1) if len(values) > 1 else values[0]
        values = jnp.concatenate([values, jnp.ones((16, values.shape[1]), jnp.bfloat16)], axis=0)
        peak = jnp.max(s, axis=0, keepdims=True) * scale
        old = jnp.full_like(peak, EMPTY) if fresh else kept[HD : HD + 1, :]
        new = jnp.maximum(old, peak)
        weights = jnp.exp2(s * scale - new).astype(jnp.bfloat16)
        summed = jnp.dot(values, weights, preferred_element_type=jnp.float32)
        denom = summed[HD : HD + 1]
        summed = summed[:HD]
        if not fresh:
            alpha = jnp.exp2(old - new)
            summed = summed + kept[:HD, :] * alpha
            denom = denom + kept[HD + 1 : HD + 2, :] * alpha
        state[:HD, :] = summed
        state[HD:, :] = jnp.concatenate([new, denom, jnp.zeros((6, LANES), jnp.float32)], axis=0)

    if fresh:
        step()
    else:

        @pl.when(none)
        def _():
            state[...] = kept[...]

        @pl.when(jnp.logical_not(none))
        def _():
            step()


def attend(q_all, low, refs, kinds, state=None):
    operands = list(refs) + ([] if state is None else [state])
    return pl.pallas_call(
        functools.partial(attend_kernel, kinds, state is None),
        out_shape=jax.ShapeDtypeStruct((STATE, LANES), jnp.float32),
        in_specs=[pl.BlockSpec(memory_space=pltpu.VMEM)] * (2 + len(operands)),
        out_specs=pl.BlockSpec(memory_space=pltpu.VMEM),
        input_output_aliases={} if state is None else {1 + len(operands): 0},
        compiler_params=pltpu.CompilerParams(vmem_limit_bytes=32 * MIB),
        cost_estimate=pl.CostEstimate(flops=1, bytes_accessed=1, transcendentals=0),
        name="attend",
    )(q_all, low, *operands)


def turn_kernel(queries, cosine, sine, out):
    half = HD // 2
    for h in range(queries.shape[1] // HD):
        x = queries[:, h * HD : (h + 1) * HD].astype(jnp.float32)
        turned = rope(x, cosine[...], sine[...]).astype(jnp.bfloat16)
        out[:, h * BLOCK : (h + 1) * BLOCK] = turned.T


def turn(queries, cosine, sine):
    return pl.pallas_call(
        turn_kernel,
        out_shape=jax.ShapeDtypeStruct((HD, queries.shape[1] // HD * BLOCK), jnp.bfloat16),
        in_specs=[pl.BlockSpec(memory_space=pltpu.VMEM)] * 3,
        out_specs=pl.BlockSpec(memory_space=pltpu.VMEM),
        compiler_params=pltpu.CompilerParams(vmem_limit_bytes=16 * MIB),
        cost_estimate=pl.CostEstimate(flops=1, bytes_accessed=1, transcendentals=0),
        name="turn",
    )(queries, cosine, sine)


def merged(mine, theirs, out):
    for h in range(HEADS):
        a = slice(h * BLOCK, (h + 1) * BLOCK)
        g = (h + HEADS // 2) % HEADS
        b = slice(g * BLOCK, (g + 1) * BLOCK)
        peak_a, peak_b = mine[HD : HD + 1, a], theirs[HD : HD + 1, b]
        peak = jnp.maximum(peak_a, peak_b)
        scale_a, scale_b = jnp.exp2(peak_a - peak), jnp.exp2(peak_b - peak)
        denom = mine[HD + 1 : HD + 2, a] * scale_a + theirs[HD + 1 : HD + 2, b] * scale_b
        summed = mine[:HD, a] * scale_a + theirs[:HD, b] * scale_b
        out[:, h * HD : (h + 1) * HD] = (summed / denom).T.astype(jnp.bfloat16)


def project_kernel(other_side, first, merging, *rest):
    half = HEADS * HD // 2
    _, hi, core, _, _ = place()
    weights, sems = rest[-2:]
    if merging:
        mine, theirs, own_weight, other_weight, attended = rest[:5]
        outs = rest[5:-2]
    else:
        attended, own_weight, other_weight = rest[:3]
        outs = rest[3:-2]
    at = (2 * (1 - hi if other_side else hi) + core) * OUT_COLUMNS + first
    pieces = weights.shape[0]
    for i in range(pieces):
        columns = pl.ds(pl.multiple_of(at + i * TILE, TILE), TILE)
        for j, weight in enumerate((own_weight, other_weight)):
            pltpu.make_async_copy(weight.at[:, columns], weights.at[i, j], sems.at[i, j]).start()
    if merging:
        merged(mine, theirs, attended)
    out, filled = 0, 0
    for i in range(pieces):
        columns = pl.ds(pl.multiple_of(at + i * TILE, TILE), TILE)
        for j, weight in enumerate((own_weight, other_weight)):
            pltpu.make_async_copy(weight.at[:, columns], weights.at[i, j], sems.at[i, j]).wait()
        total = jnp.dot(attended[:, :half], weights[i, 0], preferred_element_type=jnp.float32)
        total += jnp.dot(attended[:, half:], weights[i, 1], preferred_element_type=jnp.float32)
        outs[out][:, filled : filled + TILE] = total.astype(outs[out].dtype)
        filled += TILE
        if filled == outs[out].shape[1]:
            out, filled = out + 1, 0


def project(operands, weights, other_side, first, widths, dtype, merging=False):
    half = HEADS * HD // 2
    shapes = [jax.ShapeDtypeStruct((BLOCK, width), dtype) for width in widths]
    if merging:
        shapes = [jax.ShapeDtypeStruct((BLOCK, 2 * half), jnp.bfloat16)] + shapes
    pieces = sum(widths) // TILE
    vmem = pl.BlockSpec(memory_space=pltpu.VMEM)
    return pl.pallas_call(
        functools.partial(project_kernel, other_side, first, merging),
        out_shape=shapes,
        in_specs=[vmem] * len(operands)
        + [pl.BlockSpec(memory_space=pltpu.HBM)] * 2,
        out_specs=[vmem] * len(shapes),
        scratch_shapes=[
            pltpu.VMEM((pieces, 2, half, TILE), jnp.bfloat16),
            pltpu.SemaphoreType.DMA((pieces, 2)),
        ],
        compiler_params=pltpu.CompilerParams(vmem_limit_bytes=32 * MIB),
        cost_estimate=pl.CostEstimate(flops=1, bytes_accessed=1, transcendentals=0),
        name="project",
    )(*operands, *weights)


def finish_kernel(kept, received, *rest):
    rest[-1][...] = (kept[...] + received[...].astype(jnp.float32)).astype(jnp.bfloat16)


def finish(kept, received, first, out):
    columns, start = received.shape[1], first // TILE
    tile = pl.BlockSpec((BLOCK, TILE), lambda j: (0, start + j))
    in_specs = [tile, pl.BlockSpec((BLOCK, TILE), lambda j: (0, j))]
    operands = [kept, received]
    if out is not None:
        in_specs.append(pl.BlockSpec(memory_space=pl.ANY))
        operands.append(out)
    return pl.pallas_call(
        finish_kernel,
        out_shape=jax.ShapeDtypeStruct(kept.shape, jnp.bfloat16),
        grid=(columns // TILE,),
        in_specs=in_specs,
        out_specs=tile,
        input_output_aliases={} if out is None else {2: 0},
        compiler_params=pltpu.CompilerParams(vmem_limit_bytes=32 * MIB),
        cost_estimate=pl.CostEstimate(
            flops=BLOCK * columns, bytes_accessed=8 * BLOCK * columns, transcendentals=0
        ),
        name="finish",
    )(*operands)


def body(queries, key_heads, value_heads, doc_lengths, out_weight):
    s = lax.axis_index("seq")
    t = lax.axis_index("tensor")
    hi, core = t // 2, t % 2

    query_pos = s * BLOCK + jnp.arange(BLOCK, dtype=jnp.int32)
    cosine, sine = rope_tables(query_pos)
    own_key = lax.dynamic_index_in_dim(key_heads, hi, 1, keepdims=False).astype(jnp.float32)
    own_key = rope(own_key, cosine, sine).astype(jnp.bfloat16)
    own_value = lax.dynamic_index_in_dim(value_heads, hi, 1, keepdims=False)
    block = jnp.concatenate([own_key, own_value], axis=1)

    q_own = turn(queries, cosine, sine)
    q_other = permute(q_own, other_core)
    near = [permute(block, along_rows(step)) for step in (1, 2)]
    far = permute(block, far_block)
    *near, far = lax.optimization_barrier((*near, far))
    half = lax.dynamic_slice_in_dim(block, core * (BLOCK // 2), BLOCK // 2, 0)
    group_1 = jnp.concatenate([half, *near], axis=0)
    near = jnp.concatenate(near, axis=0)
    group_1, near, q_other, out_weight = lax.optimization_barrier(
        (group_1, near, q_other, out_weight)
    )
    other_weight = permute(out_weight, other_core)
    shifts = (1, -1, 2)
    group_2 = permute(near, two_rows_on)
    columns_1 = [permute(group_1, in_row(shift)) for shift in shifts]

    q_all = jnp.concatenate([q_own, q_other], axis=1)
    doc_ends = jnp.cumsum(doc_lengths)
    low = jnp.max(jnp.where(doc_ends[:, None] <= query_pos[None], doc_ends[:, None], 0), axis=0)
    low = jnp.broadcast_to(low, (8, HEADS, BLOCK)).reshape(8, LANES)
    step = functools.partial(attend, q_all, low)

    state = step([half, near], [("half", 0), (1, 0), (2, 0)])
    rows_2 = lambda shift: [(3, shift), (4, shift)]
    group_2, state = lax.optimization_barrier((group_2, state))
    columns_2 = [permute(group_2, in_row(shift)) for shift in shifts]
    for shift, keys in zip(shifts, columns_1):
        refs, kinds = [keys], [("half", shift), (1, shift), (2, shift)]
        if shift == 1:
            refs, kinds = [group_2] + refs, rows_2(0) + kinds
        if shift == 2:
            refs, kinds = refs + [far], kinds + [("far", 0)]
        state = step(refs, kinds, state)
    state, other_weight = lax.optimization_barrier((state, other_weight))
    weights = (out_weight, other_weight)
    state = step(columns_2[:2], rows_2(1) + rows_2(-1), state)
    state = step(columns_2[2:], rows_2(2), state)

    theirs = permute(state, other_core)
    attended, partial = project((state, theirs), weights, True, 0, (512,), jnp.bfloat16, True)
    received = [permute(partial, other_hi)]
    for partial in project((attended,), weights, True, 512, (512,) * 3, jnp.bfloat16):
        received.append(permute(partial, other_hi))
    (kept,) = project((attended,), weights, False, 0, (OUT_COLUMNS,), jnp.float32)
    out, first = None, 0
    for piece in received:
        out = finish(kept, piece, first, out)
        first += piece.shape[1]
    return out


def solution(mesh):
    return jax.shard_map(
        body,
        mesh=mesh,
        in_specs=(
            P("seq", "tensor"),
            P("seq", None, None),
            P("seq", None, None),
            P(),
            P("tensor", None),
        ),
        out_specs=P("seq", "tensor"),
        check_vma=False,
    )
```

```python
import functools
import math

import jax
import jax.numpy as jnp
from jax import lax
from jax.experimental import pallas as pl
from jax.experimental.pallas import tpu as pltpu
from jax.sharding import PartitionSpec as P

HQ = 16
KVH = 2
HD = 128
SEQ = 64
TENSOR = 4
ROW = 4
THETA = 500000.0
EMPTY = -1e30
MASKED = -1e32
LOG2E = math.log2(math.e)
BLOCK = 256
ROW_TOKENS = ROW * BLOCK
HEADS = 8
LANES = HEADS * BLOCK
STATE = HD + 8
TILE = 512
NOWHERE = -(1 << 24)
OUT_COLUMNS = 2048
HALF = BLOCK // 2
MIB = 1024 * 1024


def device_perm(move):
    pairs = []
    for s in range(SEQ):
        for hi in range(2):
            for core in range(2):
                to = move(s, hi, core)
                if to is not None:
                    pairs.append((s * TENSOR + hi * 2 + core, to[0] * TENSOR + to[1] * 2 + to[2]))
    return pairs


def permute(x, move):
    return lax.ppermute(x, ("seq", "tensor"), device_perm(move))


def in_row(shift):
    return lambda s, hi, core: (s - s % ROW + (s + shift) % ROW, hi, core)


def other_core(s, hi, core):
    return s, hi, 1 - core


def other_hi(s, hi, core):
    return s, 1 - hi, core


def far_block(s, hi, core):
    if core == 0 and s % ROW == ROW - 1 and s + 33 < SEQ:
        return s + 33, hi, core
    return None


def along_rows(step):
    def move(s, hi, core):
        if core == 0:
            return (s + step * ROW, hi, core) if s + step * ROW < SEQ else None
        return (s + (9 - step) * ROW) % SEQ, hi, core

    return move


def two_rows_on(s, hi, core):
    if core == 0:
        return (s + 2 * ROW, hi, core) if s + 2 * ROW < SEQ else None
    return (s - 2 * ROW) % SEQ, hi, core


def rope_tables(positions):
    half = HD // 2
    exponents = jnp.arange(half, dtype=jnp.float32) * (2.0 / HD)
    inverse = jnp.power(jnp.float32(THETA), -exponents)
    angles = positions.astype(jnp.float32)[:, None] * inverse[None, :]
    return jnp.cos(angles), jnp.sin(angles)


def rope(values, cosine, sine):
    half = HD // 2
    first, second = values[..., :half], values[..., half:]
    return jnp.concatenate(
        [first * cosine - second * sine, second * cosine + first * sine], axis=-1
    )


def place():
    s, t = lax.axis_index("seq"), lax.axis_index("tensor")
    return s, t >> 1, t & 1, s >> 2, s & 3


def part_at(kind, shift):
    s, _, core, row, col = place()
    at = (col + ROW - shift) & 3
    if kind == "far":
        there = (core == 0) & (col == 0) & (s >= 33)
        return jnp.where(there, (s - 33) * BLOCK, NOWHERE), BLOCK
    if kind == "half":
        base = (row * ROW + at) * BLOCK + core * (BLOCK // 2)
        return jnp.where(at > col, NOWHERE, base), BLOCK // 2
    return (jnp.where(core == 0, row - kind, row - 9 + kind) * ROW + at) * BLOCK, BLOCK


def attend_kernel(kinds, fresh, first_lane, q_ref, low_ref, *rest):
    state = rest[-1]
    kept, refs = (None, rest[:-1]) if fresh else (rest[-2], rest[:-2])
    scale = HD**-0.5 * LOG2E
    first_query = place()[0] * BLOCK
    low_first = jnp.min(low_ref[0:1, 0:HD])
    parts, bases, none = [], [], True
    at, i = 0, 0
    for kind, shift in kinds:
        base, size = part_at(kind, shift)
        parts.append(refs[i].at[at : at + size])
        at += size
        if at == refs[i].shape[0]:
            at, i = 0, i + 1
        bases.append(base)
        none = (low_first >= base + size) & none

    width = state.shape[1]
    lanes = slice(first_lane, first_lane + width)

    def step():
        q = q_ref[:, lanes]
        low = low_ref[0:1, lanes]
        scores = []
        for part, base, kind in zip(parts, bases, kinds):
            s = jnp.dot(part[:, :HD], q, preferred_element_type=jnp.float32)
            at = lax.broadcasted_iota(jnp.int32, s.shape, 0)
            live = at >= low - base
            if kind == ("half", 0):
                lane = lax.broadcasted_iota(jnp.int32, (1, width), 1) + first_lane
                query = lane // (LANES // 2) * HALF + lane % HALF + first_query
                live = live & (at <= query - base)
            scores.append(jnp.where(live, s, MASKED))
        s = jnp.concatenate(scores, axis=0) if len(scores) > 1 else scores[0]
        values = [part[:, HD:].T for part in parts]
        values = jnp.concatenate(values, axis=1) if len(values) > 1 else values[0]
        values = jnp.concatenate([values, jnp.ones((16, values.shape[1]), jnp.bfloat16)], axis=0)
        peak = jnp.max(s, axis=0, keepdims=True) * scale
        old = jnp.full_like(peak, EMPTY) if fresh else kept[HD : HD + 1, lanes]
        new = jnp.maximum(old, peak)
        weights = jnp.exp2(s * scale - new).astype(jnp.bfloat16)
        summed = jnp.dot(values, weights, preferred_element_type=jnp.float32)
        denom = summed[HD : HD + 1]
        summed = summed[:HD]
        if not fresh:
            alpha = jnp.exp2(old - new)
            summed = summed + kept[:HD, lanes] * alpha
            denom = denom + kept[HD + 1 : HD + 2, lanes] * alpha
        state[:HD, :] = summed
        state[HD:, :] = jnp.concatenate([new, denom, jnp.zeros((6, width), jnp.float32)], axis=0)

    if fresh:
        step()
    else:

        @pl.when(none)
        def _():
            state[...] = kept[:, lanes]

        @pl.when(jnp.logical_not(none))
        def _():
            step()


def attend(q_all, low, refs, kinds, state=None, half=None):
    operands = list(refs) + ([] if state is None else [state])
    width, first_lane = (LANES, 0) if half is None else (LANES // 2, half * LANES // 2)
    in_place = state is not None and half is None
    return pl.pallas_call(
        functools.partial(attend_kernel, kinds, state is None, first_lane),
        out_shape=jax.ShapeDtypeStruct((STATE, width), jnp.float32),
        in_specs=[pl.BlockSpec(memory_space=pltpu.VMEM)] * (2 + len(operands)),
        out_specs=pl.BlockSpec(memory_space=pltpu.VMEM),
        input_output_aliases={1 + len(operands): 0} if in_place else {},
        compiler_params=pltpu.CompilerParams(vmem_limit_bytes=24 * MIB),
        cost_estimate=pl.CostEstimate(flops=1, bytes_accessed=1, transcendentals=0),
        name="attend",
    )(q_all, low, *operands)


def turn_kernel(queries, cosine, sine, out):
    heads = queries.shape[1] // HD
    for h in range(heads):
        x = queries[:, h * HD : (h + 1) * HD].astype(jnp.float32)
        turned = rope(x, cosine[...], sine[...]).astype(jnp.bfloat16).T
        for half in range(2):
            at = (half * heads + h) * HALF
            out[:, at : at + HALF] = turned[:, half * HALF : (half + 1) * HALF]


def turn(queries, cosine, sine):
    return pl.pallas_call(
        turn_kernel,
        out_shape=jax.ShapeDtypeStruct((HD, queries.shape[1] // HD * BLOCK), jnp.bfloat16),
        in_specs=[pl.BlockSpec(memory_space=pltpu.VMEM)] * 3,
        out_specs=pl.BlockSpec(memory_space=pltpu.VMEM),
        compiler_params=pltpu.CompilerParams(vmem_limit_bytes=16 * MIB),
        cost_estimate=pl.CostEstimate(flops=1, bytes_accessed=1, transcendentals=0),
        name="turn",
    )(queries, cosine, sine)


def merged(mine, theirs, out):
    for h in range(HEADS):
        a = slice(h * HALF, (h + 1) * HALF)
        g = (h + HEADS // 2) % HEADS
        b = slice(g * HALF, (g + 1) * HALF)
        peak_a, peak_b = mine[HD : HD + 1, a], theirs[HD : HD + 1, b]
        peak = jnp.maximum(peak_a, peak_b)
        scale_a, scale_b = jnp.exp2(peak_a - peak), jnp.exp2(peak_b - peak)
        denom = mine[HD + 1 : HD + 2, a] * scale_a + theirs[HD + 1 : HD + 2, b] * scale_b
        summed = mine[:HD, a] * scale_a + theirs[:HD, b] * scale_b
        out[:, h * HD : (h + 1) * HD] = (summed / denom).T.astype(jnp.bfloat16)


def project_kernel(other_side, first, merging, *rest):
    half = HEADS * HD // 2
    _, hi, core, _, _ = place()
    weights, sems = rest[-2:]
    if merging:
        mine, theirs, own_weight, other_weight, attended = rest[:5]
        outs = rest[5:-2]
    else:
        attended, own_weight, other_weight = rest[:3]
        outs = rest[3:-2]
    at = (2 * (1 - hi if other_side else hi) + core) * OUT_COLUMNS + first
    pieces = weights.shape[0]
    for i in range(pieces):
        columns = pl.ds(pl.multiple_of(at + i * TILE, TILE), TILE)
        for j, weight in enumerate((own_weight, other_weight)):
            pltpu.make_async_copy(weight.at[:, columns], weights.at[i, j], sems.at[i, j]).start()
    if merging:
        merged(mine, theirs, attended)
    out, filled = 0, 0
    for i in range(pieces):
        columns = pl.ds(pl.multiple_of(at + i * TILE, TILE), TILE)
        for j, weight in enumerate((own_weight, other_weight)):
            pltpu.make_async_copy(weight.at[:, columns], weights.at[i, j], sems.at[i, j]).wait()
        total = jnp.dot(attended[:, :half], weights[i, 0], preferred_element_type=jnp.float32)
        total += jnp.dot(attended[:, half:], weights[i, 1], preferred_element_type=jnp.float32)
        outs[out][:, filled : filled + TILE] = total.astype(outs[out].dtype)
        filled += TILE
        if filled == outs[out].shape[1]:
            out, filled = out + 1, 0


def project(operands, weights, other_side, first, widths, dtype, merging=False):
    half = HEADS * HD // 2
    shapes = [jax.ShapeDtypeStruct((HALF, width), dtype) for width in widths]
    if merging:
        shapes = [jax.ShapeDtypeStruct((HALF, 2 * half), jnp.bfloat16)] + shapes
    pieces = sum(widths) // TILE
    vmem = pl.BlockSpec(memory_space=pltpu.VMEM)
    return pl.pallas_call(
        functools.partial(project_kernel, other_side, first, merging),
        out_shape=shapes,
        in_specs=[vmem] * len(operands)
        + [pl.BlockSpec(memory_space=pltpu.HBM)] * 2,
        out_specs=[vmem] * len(shapes),
        scratch_shapes=[
            pltpu.VMEM((pieces, 2, half, TILE), jnp.bfloat16),
            pltpu.SemaphoreType.DMA((pieces, 2)),
        ],
        compiler_params=pltpu.CompilerParams(vmem_limit_bytes=16 * MIB),
        cost_estimate=pl.CostEstimate(flops=1, bytes_accessed=1, transcendentals=0),
        name="project",
    )(*operands, *weights)


def finish_kernel(kept, received, *rest):
    rest[-1][...] = (kept[...] + received[...].astype(jnp.float32)).astype(jnp.bfloat16)


def finish(kept, received, half, first, out):
    columns, start = received.shape[1], first // TILE
    in_specs = [
        pl.BlockSpec((HALF, TILE), lambda j: (0, start + j)),
        pl.BlockSpec((HALF, TILE), lambda j: (0, j)),
    ]
    operands = [kept, received]
    if out is not None:
        in_specs.append(pl.BlockSpec(memory_space=pl.ANY))
        operands.append(out)
    return pl.pallas_call(
        finish_kernel,
        out_shape=jax.ShapeDtypeStruct((BLOCK, OUT_COLUMNS), jnp.bfloat16),
        grid=(columns // TILE,),
        in_specs=in_specs,
        out_specs=pl.BlockSpec((HALF, TILE), lambda j: (half, start + j)),
        input_output_aliases={} if out is None else {2: 0},
        compiler_params=pltpu.CompilerParams(vmem_limit_bytes=16 * MIB),
        cost_estimate=pl.CostEstimate(flops=1, bytes_accessed=1, transcendentals=0),
        name="finish",
    )(*operands)


def body(queries, key_heads, value_heads, doc_lengths, out_weight):
    s = lax.axis_index("seq")
    t = lax.axis_index("tensor")
    hi, core = t // 2, t % 2

    query_pos = s * BLOCK + jnp.arange(BLOCK, dtype=jnp.int32)
    cosine, sine = rope_tables(query_pos)
    own_key = lax.dynamic_index_in_dim(key_heads, hi, 1, keepdims=False).astype(jnp.float32)
    own_key = rope(own_key, cosine, sine).astype(jnp.bfloat16)
    own_value = lax.dynamic_index_in_dim(value_heads, hi, 1, keepdims=False)
    block = jnp.concatenate([own_key, own_value], axis=1)

    q_own = turn(queries, cosine, sine)
    q_other = permute(q_own, other_core)
    near = [permute(block, along_rows(step)) for step in (1, 2)]
    far = permute(block, far_block)
    *near, far = lax.optimization_barrier((*near, far))
    half = lax.dynamic_slice_in_dim(block, core * (BLOCK // 2), BLOCK // 2, 0)
    group_1 = jnp.concatenate([half, *near], axis=0)
    near = jnp.concatenate(near, axis=0)
    group_1, near, q_other, out_weight = lax.optimization_barrier(
        (group_1, near, q_other, out_weight)
    )
    other_weight = permute(out_weight, other_core)
    shifts = (1, -1, 2)
    group_2 = permute(near, two_rows_on)
    columns_1 = [permute(group_1, in_row(shift)) for shift in shifts]

    own_lanes = LANES // 4
    q_all = jnp.concatenate(
        [q[:, i * own_lanes : (i + 1) * own_lanes] for i in range(2) for q in (q_own, q_other)],
        axis=1,
    )
    doc_ends = jnp.cumsum(doc_lengths)
    low = jnp.max(jnp.where(doc_ends[:, None] <= query_pos[None], doc_ends[:, None], 0), axis=0)
    low = jnp.broadcast_to(low.reshape(2, 1, HALF), (8, 2, HEADS, HALF)).reshape(8, LANES)
    step = functools.partial(attend, q_all, low)

    state = step([half, near], [("half", 0), (1, 0), (2, 0)])
    rows_2 = lambda shift: [(3, shift), (4, shift)]
    group_2, state = lax.optimization_barrier((group_2, state))
    columns_2 = [permute(group_2, in_row(shift)) for shift in shifts]
    for shift, keys in zip(shifts, columns_1):
        refs, kinds = [keys], [("half", shift), (1, shift), (2, shift)]
        if shift == 1:
            refs, kinds = [group_2] + refs, rows_2(0) + kinds
        if shift == 2:
            refs, kinds = refs + [far], kinds + [("far", 0)]
        state = step(refs, kinds, state)
    state, other_weight = lax.optimization_barrier((state, other_weight))
    weights = (out_weight, other_weight)
    state = step(columns_2[:1], rows_2(1), state)
    halves = []
    for half in range(2):
        mine = step(columns_2[1:], rows_2(-1) + rows_2(2), state, half)
        halves.append((mine, permute(mine, other_core)))

    sent, kept = [], []
    for half, (first, rest) in enumerate((((OUT_COLUMNS,), ()), ((1024,), (1024,)))):
        attended, partial = project(halves[half], weights, True, 0, first, jnp.bfloat16, True)
        partials = [partial]
        if rest:
            partials += project((attended,), weights, True, first[0], rest, jnp.bfloat16)
        sent.append([permute(partial, other_hi) for partial in partials])
        kept += project((attended,), weights, False, 0, (OUT_COLUMNS,), jnp.float32)
    out = None
    for half in range(2):
        first = 0
        for piece in sent[half]:
            out = finish(kept[half], piece, half, first, out)
            first += piece.shape[1]
    return out


def solution(mesh):
    return jax.shard_map(
        body,
        mesh=mesh,
        in_specs=(
            P("seq", "tensor"),
            P("seq", None, None),
            P("seq", None, None),
            P(),
            P("tensor", None),
        ),
        out_specs=P("seq", "tensor"),
        check_vma=False,
    )
```

```python
import functools
import math

import jax
import jax.numpy as jnp
from jax import lax
from jax.experimental import pallas as pl
from jax.experimental.pallas import tpu as pltpu
from jax.sharding import PartitionSpec as P

HQ = 16
KVH = 2
HD = 128
SEQ = 64
TENSOR = 4
ROW = 4
THETA = 500000.0
EMPTY = -1e30
MASKED = -1e32
LOG2E = math.log2(math.e)
BLOCK = 256
ROW_TOKENS = ROW * BLOCK
HEADS = 8
LANES = HEADS * BLOCK
STATE = HD + 8
TILE = 512
NOWHERE = -(1 << 24)
OUT_COLUMNS = 2048
HALF = BLOCK // 2
MIB = 1024 * 1024


def device_perm(move):
    pairs = []
    for s in range(SEQ):
        for hi in range(2):
            for core in range(2):
                to = move(s, hi, core)
                if to is not None:
                    pairs.append((s * TENSOR + hi * 2 + core, to[0] * TENSOR + to[1] * 2 + to[2]))
    return pairs


def permute(x, move):
    return lax.ppermute(x, ("seq", "tensor"), device_perm(move))


def in_row(shift):
    return lambda s, hi, core: (s - s % ROW + (s + shift) % ROW, hi, core)


def other_core(s, hi, core):
    return s, hi, 1 - core


def other_hi(s, hi, core):
    return s, 1 - hi, core


def far_block(s, hi, core):
    if core == 0 and s % ROW == ROW - 1 and s + 33 < SEQ:
        return s + 33, hi, core
    return None


def along_rows(step):
    def move(s, hi, core):
        if core == 0:
            return (s + step * ROW, hi, core) if s + step * ROW < SEQ else None
        return (s + (9 - step) * ROW) % SEQ, hi, core

    return move


def two_rows_on(s, hi, core):
    if core == 0:
        return (s + 2 * ROW, hi, core) if s + 2 * ROW < SEQ else None
    return (s - 2 * ROW) % SEQ, hi, core


def rope_tables(positions):
    half = HD // 2
    exponents = jnp.arange(half, dtype=jnp.float32) * (2.0 / HD)
    inverse = jnp.power(jnp.float32(THETA), -exponents)
    angles = positions.astype(jnp.float32)[:, None] * inverse[None, :]
    return jnp.cos(angles), jnp.sin(angles)


def rope(values, cosine, sine):
    half = HD // 2
    first, second = values[..., :half], values[..., half:]
    return jnp.concatenate(
        [first * cosine - second * sine, second * cosine + first * sine], axis=-1
    )


def place():
    s, t = lax.axis_index("seq"), lax.axis_index("tensor")
    return s, t >> 1, t & 1, s >> 2, s & 3


def part_at(kind, shift):
    s, _, core, row, col = place()
    at = (col + ROW - shift) & 3
    if kind == "far":
        there = (core == 0) & (col == 0) & (s >= 33)
        return jnp.where(there, (s - 33) * BLOCK, NOWHERE), BLOCK
    if kind == "half":
        base = (row * ROW + at) * BLOCK + core * (BLOCK // 2)
        return jnp.where(at > col, NOWHERE, base), BLOCK // 2
    return (jnp.where(core == 0, row - kind, row - 9 + kind) * ROW + at) * BLOCK, BLOCK


def attend_kernel(kinds, fresh, first_lane, q_ref, low_ref, *rest):
    state = rest[-1]
    kept, refs = (None, rest[:-1]) if fresh else (rest[-2], rest[:-2])
    scale = HD**-0.5 * LOG2E
    first_query = place()[0] * BLOCK
    low_first = jnp.min(low_ref[0:1, 0:HD])
    parts, bases, none = [], [], True
    at, i = 0, 0
    for kind, shift in kinds:
        base, size = part_at(kind, shift)
        parts.append(refs[i].at[at : at + size])
        at += size
        if at == refs[i].shape[0]:
            at, i = 0, i + 1
        bases.append(base)
        none = (low_first >= base + size) & none

    width = state.shape[1]
    lanes = slice(first_lane, first_lane + width)

    def step():
        q = q_ref[:, lanes]
        low = low_ref[0:1, lanes]
        scores = []
        for part, base, kind in zip(parts, bases, kinds):
            s = jnp.dot(part[:, :HD], q, preferred_element_type=jnp.float32)
            at = lax.broadcasted_iota(jnp.int32, s.shape, 0)
            live = at >= low - base
            if kind == ("half", 0):
                lane = lax.broadcasted_iota(jnp.int32, (1, width), 1) + first_lane
                query = lane // (LANES // 2) * HALF + lane % HALF + first_query
                live = live & (at <= query - base)
            scores.append(jnp.where(live, s, MASKED))
        s = jnp.concatenate(scores, axis=0) if len(scores) > 1 else scores[0]
        values = [part[:, HD:].T for part in parts]
        values = jnp.concatenate(values, axis=1) if len(values) > 1 else values[0]
        values = jnp.concatenate([values, jnp.ones((16, values.shape[1]), jnp.bfloat16)], axis=0)
        peak = jnp.max(s, axis=0, keepdims=True) * scale
        old = jnp.full_like(peak, EMPTY) if fresh else kept[HD : HD + 1, lanes]
        new = jnp.maximum(old, peak)
        weights = jnp.exp2(s * scale - new).astype(jnp.bfloat16)
        summed = jnp.dot(values, weights, preferred_element_type=jnp.float32)
        denom = summed[HD : HD + 1]
        summed = summed[:HD]
        if not fresh:
            alpha = jnp.exp2(old - new)
            summed = summed + kept[:HD, lanes] * alpha
            denom = denom + kept[HD + 1 : HD + 2, lanes] * alpha
        state[:HD, :] = summed
        state[HD:, :] = jnp.concatenate([new, denom, jnp.zeros((6, width), jnp.float32)], axis=0)

    if fresh:
        step()
    else:

        @pl.when(none)
        def _():
            state[...] = kept[:, lanes]

        @pl.when(jnp.logical_not(none))
        def _():
            step()


def attend(q_all, low, refs, kinds, state=None, half=None):
    operands = list(refs) + ([] if state is None else [state])
    width, first_lane = (LANES, 0) if half is None else (LANES // 2, half * LANES // 2)
    in_place = state is not None and half is None
    return pl.pallas_call(
        functools.partial(attend_kernel, kinds, state is None, first_lane),
        out_shape=jax.ShapeDtypeStruct((STATE, width), jnp.float32),
        in_specs=[pl.BlockSpec(memory_space=pltpu.VMEM)] * (2 + len(operands)),
        out_specs=pl.BlockSpec(memory_space=pltpu.VMEM),
        input_output_aliases={1 + len(operands): 0} if in_place else {},
        compiler_params=pltpu.CompilerParams(vmem_limit_bytes=24 * MIB),
        cost_estimate=pl.CostEstimate(flops=1, bytes_accessed=1, transcendentals=0),
        name="attend",
    )(q_all, low, *operands)


def turn_kernel(queries, cosine, sine, out):
    heads = queries.shape[1] // HD
    for h in range(heads):
        x = queries[:, h * HD : (h + 1) * HD].astype(jnp.float32)
        turned = rope(x, cosine[...], sine[...]).astype(jnp.bfloat16).T
        for half in range(2):
            at = (half * heads + h) * HALF
            out[:, at : at + HALF] = turned[:, half * HALF : (half + 1) * HALF]


def turn(queries, cosine, sine):
    return pl.pallas_call(
        turn_kernel,
        out_shape=jax.ShapeDtypeStruct((HD, queries.shape[1] // HD * BLOCK), jnp.bfloat16),
        in_specs=[pl.BlockSpec(memory_space=pltpu.VMEM)] * 3,
        out_specs=pl.BlockSpec(memory_space=pltpu.VMEM),
        compiler_params=pltpu.CompilerParams(vmem_limit_bytes=16 * MIB),
        cost_estimate=pl.CostEstimate(flops=1, bytes_accessed=1, transcendentals=0),
        name="turn",
    )(queries, cosine, sine)


def merged(mine, theirs, out):
    for h in range(HEADS):
        a = slice(h * HALF, (h + 1) * HALF)
        g = (h + HEADS // 2) % HEADS
        b = slice(g * HALF, (g + 1) * HALF)
        peak_a, peak_b = mine[HD : HD + 1, a], theirs[HD : HD + 1, b]
        peak = jnp.maximum(peak_a, peak_b)
        scale_a, scale_b = jnp.exp2(peak_a - peak), jnp.exp2(peak_b - peak)
        denom = mine[HD + 1 : HD + 2, a] * scale_a + theirs[HD + 1 : HD + 2, b] * scale_b
        summed = mine[:HD, a] * scale_a + theirs[:HD, b] * scale_b
        out[:, h * HD : (h + 1) * HD] = (summed / denom).T.astype(jnp.bfloat16)


def project_kernel(other_side, first, merging, *rest):
    half = HEADS * HD // 2
    _, hi, core, _, _ = place()
    weights, sems = rest[-2:]
    if merging:
        mine, theirs, own_weight, other_weight, attended = rest[:5]
        outs = rest[5:-2]
    else:
        attended, own_weight, other_weight = rest[:3]
        outs = rest[3:-2]
    at = (2 * (1 - hi if other_side else hi) + core) * OUT_COLUMNS + first
    pieces = weights.shape[0]
    for i in range(pieces):
        columns = pl.ds(pl.multiple_of(at + i * TILE, TILE), TILE)
        for j, weight in enumerate((own_weight, other_weight)):
            pltpu.make_async_copy(weight.at[:, columns], weights.at[i, j], sems.at[i, j]).start()
    if merging:
        merged(mine, theirs, attended)
    out, filled = 0, 0
    for i in range(pieces):
        columns = pl.ds(pl.multiple_of(at + i * TILE, TILE), TILE)
        for j, weight in enumerate((own_weight, other_weight)):
            pltpu.make_async_copy(weight.at[:, columns], weights.at[i, j], sems.at[i, j]).wait()
        total = jnp.dot(attended[:, :half], weights[i, 0], preferred_element_type=jnp.float32)
        total += jnp.dot(attended[:, half:], weights[i, 1], preferred_element_type=jnp.float32)
        outs[out][:, filled : filled + TILE] = total.astype(outs[out].dtype)
        filled += TILE
        if filled == outs[out].shape[1]:
            out, filled = out + 1, 0


def project(operands, weights, other_side, first, widths, dtype, merging=False):
    half = HEADS * HD // 2
    shapes = [jax.ShapeDtypeStruct((HALF, width), dtype) for width in widths]
    if merging:
        shapes = [jax.ShapeDtypeStruct((HALF, 2 * half), jnp.bfloat16)] + shapes
    pieces = sum(widths) // TILE
    vmem = pl.BlockSpec(memory_space=pltpu.VMEM)
    return pl.pallas_call(
        functools.partial(project_kernel, other_side, first, merging),
        out_shape=shapes,
        in_specs=[vmem] * len(operands)
        + [pl.BlockSpec(memory_space=pltpu.HBM)] * 2,
        out_specs=[vmem] * len(shapes),
        scratch_shapes=[
            pltpu.VMEM((pieces, 2, half, TILE), jnp.bfloat16),
            pltpu.SemaphoreType.DMA((pieces, 2)),
        ],
        compiler_params=pltpu.CompilerParams(vmem_limit_bytes=16 * MIB),
        cost_estimate=pl.CostEstimate(flops=1, bytes_accessed=1, transcendentals=0),
        name="project",
    )(*operands, *weights)


def finish_kernel(kept, received, *rest):
    rest[-1][...] = (kept[...] + received[...].astype(jnp.float32)).astype(jnp.bfloat16)


def finish(kept, received, half, first, out):
    columns, start = received.shape[1], first // TILE
    in_specs = [
        pl.BlockSpec((HALF, TILE), lambda j: (0, start + j)),
        pl.BlockSpec((HALF, TILE), lambda j: (0, j)),
    ]
    operands = [kept, received]
    if out is not None:
        in_specs.append(pl.BlockSpec(memory_space=pl.ANY))
        operands.append(out)
    return pl.pallas_call(
        finish_kernel,
        out_shape=jax.ShapeDtypeStruct((BLOCK, OUT_COLUMNS), jnp.bfloat16),
        grid=(columns // TILE,),
        in_specs=in_specs,
        out_specs=pl.BlockSpec((HALF, TILE), lambda j: (half, start + j)),
        input_output_aliases={} if out is None else {2: 0},
        compiler_params=pltpu.CompilerParams(vmem_limit_bytes=16 * MIB),
        cost_estimate=pl.CostEstimate(flops=1, bytes_accessed=1, transcendentals=0),
        name="finish",
    )(*operands)


def body(queries, key_heads, value_heads, doc_lengths, out_weight):
    s = lax.axis_index("seq")
    t = lax.axis_index("tensor")
    hi, core = t // 2, t % 2

    query_pos = s * BLOCK + jnp.arange(BLOCK, dtype=jnp.int32)
    cosine, sine = rope_tables(query_pos)
    own_key = lax.dynamic_index_in_dim(key_heads, hi, 1, keepdims=False).astype(jnp.float32)
    own_key = rope(own_key, cosine, sine).astype(jnp.bfloat16)
    own_value = lax.dynamic_index_in_dim(value_heads, hi, 1, keepdims=False)
    block = jnp.concatenate([own_key, own_value], axis=1)

    q_own = turn(queries, cosine, sine)
    q_other = permute(q_own, other_core)
    near = [permute(block, along_rows(step)) for step in (1, 2)]
    far = permute(block, far_block)
    *near, far = lax.optimization_barrier((*near, far))
    half = lax.dynamic_slice_in_dim(block, core * (BLOCK // 2), BLOCK // 2, 0)
    group_1 = jnp.concatenate([half, *near], axis=0)
    near = jnp.concatenate(near, axis=0)
    near, out_weight = lax.optimization_barrier((near, out_weight))
    other_weight = permute(out_weight, other_core)
    shifts = (1, -1, 2)
    group_2 = permute(near, two_rows_on)
    group_1, q_other = lax.optimization_barrier((group_1, q_other))
    columns_1 = [permute(group_1, in_row(shift)) for shift in shifts]

    own_lanes = LANES // 4
    q_all = jnp.concatenate(
        [q[:, i * own_lanes : (i + 1) * own_lanes] for i in range(2) for q in (q_own, q_other)],
        axis=1,
    )
    doc_ends = jnp.cumsum(doc_lengths)
    low = jnp.max(jnp.where(doc_ends[:, None] <= query_pos[None], doc_ends[:, None], 0), axis=0)
    low = jnp.broadcast_to(low.reshape(2, 1, HALF), (8, 2, HEADS, HALF)).reshape(8, LANES)
    step = functools.partial(attend, q_all, low)

    state = step([half, near], [("half", 0), (1, 0), (2, 0)])
    rows_2 = lambda shift: [(3, shift), (4, shift)]
    group_2, state = lax.optimization_barrier((group_2, state))
    columns_2 = [permute(group_2, in_row(shift)) for shift in shifts]
    state = step([group_2], rows_2(0), state)
    for shift, keys in zip(shifts, columns_1):
        refs, kinds = [keys], [("half", shift), (1, shift), (2, shift)]
        if shift == 2:
            refs, kinds = refs + [far], kinds + [("far", 0)]
        state = step(refs, kinds, state)
    state, other_weight = lax.optimization_barrier((state, other_weight))
    weights = (out_weight, other_weight)
    state = step(columns_2[:1], rows_2(1), state)
    halves = []
    for half in range(2):
        mine = step(columns_2[1:], rows_2(-1) + rows_2(2), state, half)
        halves.append((mine, permute(mine, other_core)))

    sent, kept = [], []
    for half, (first, rest) in enumerate((((OUT_COLUMNS,), ()), ((1024,), (1024,)))):
        attended, partial = project(halves[half], weights, True, 0, first, jnp.bfloat16, True)
        partials = [partial]
        if rest:
            partials += project((attended,), weights, True, first[0], rest, jnp.bfloat16)
        sent.append([permute(partial, other_hi) for partial in partials])
        kept += project((attended,), weights, False, 0, (OUT_COLUMNS,), jnp.float32)
    out = None
    for half in range(2):
        first = 0
        for piece in sent[half]:
            out = finish(kept[half], piece, half, first, out)
            first += piece.shape[1]
    return out


def solution(mesh):
    return jax.shard_map(
        body,
        mesh=mesh,
        in_specs=(
            P("seq", "tensor"),
            P("seq", None, None),
            P("seq", None, None),
            P(),
            P("tensor", None),
        ),
        out_specs=P("seq", "tensor"),
        check_vma=False,
    )
```

```python
import functools
import math

import jax
import jax.numpy as jnp
from jax import lax
from jax.experimental import pallas as pl
from jax.experimental.pallas import tpu as pltpu
from jax.sharding import PartitionSpec as P

HQ = 16
KVH = 2
HD = 128
SEQ = 64
TENSOR = 4
ROW = 4
THETA = 500000.0
EMPTY = -1e30
MASKED = -1e32
LOG2E = math.log2(math.e)
BLOCK = 256
ROW_TOKENS = ROW * BLOCK
HEADS = 8
LANES = HEADS * BLOCK
STATE = HD + 8
TILE = 512
NOWHERE = -(1 << 24)
OUT_COLUMNS = 2048
HALF = BLOCK // 2
MIB = 1024 * 1024


def device_perm(move):
    pairs = []
    for s in range(SEQ):
        for hi in range(2):
            for core in range(2):
                to = move(s, hi, core)
                if to is not None:
                    pairs.append((s * TENSOR + hi * 2 + core, to[0] * TENSOR + to[1] * 2 + to[2]))
    return pairs


def permute(x, move):
    return lax.ppermute(x, ("seq", "tensor"), device_perm(move))


def in_row(shift):
    return lambda s, hi, core: (s - s % ROW + (s + shift) % ROW, hi, core)


def other_core(s, hi, core):
    return s, hi, 1 - core


def other_hi(s, hi, core):
    return s, 1 - hi, core


def far_block(s, hi, core):
    if core == 0 and s % ROW == ROW - 1 and s + 33 < SEQ:
        return s + 33, hi, core
    return None


def along_rows(step):
    def move(s, hi, core):
        if core == 0:
            return (s + step * ROW, hi, core) if s + step * ROW < SEQ else None
        return (s + (9 - step) * ROW) % SEQ, hi, core

    return move


def two_rows_on(s, hi, core):
    if core == 0:
        return (s + 2 * ROW, hi, core) if s + 2 * ROW < SEQ else None
    return (s - 2 * ROW) % SEQ, hi, core


def rope_tables(positions):
    half = HD // 2
    exponents = jnp.arange(half, dtype=jnp.float32) * (2.0 / HD)
    inverse = jnp.power(jnp.float32(THETA), -exponents)
    angles = positions.astype(jnp.float32)[:, None] * inverse[None, :]
    return jnp.cos(angles), jnp.sin(angles)


def rope(values, cosine, sine):
    half = HD // 2
    first, second = values[..., :half], values[..., half:]
    return jnp.concatenate(
        [first * cosine - second * sine, second * cosine + first * sine], axis=-1
    )


def place():
    s, t = lax.axis_index("seq"), lax.axis_index("tensor")
    return s, t >> 1, t & 1, s >> 2, s & 3


def part_at(kind, shift):
    s, _, core, row, col = place()
    at = (col + ROW - shift) & 3
    if kind == "far":
        there = (core == 0) & (col == 0) & (s >= 33)
        return jnp.where(there, (s - 33) * BLOCK, NOWHERE), BLOCK
    if kind == "half":
        base = (row * ROW + at) * BLOCK + core * (BLOCK // 2)
        return jnp.where(at > col, NOWHERE, base), BLOCK // 2
    return (jnp.where(core == 0, row - kind, row - 9 + kind) * ROW + at) * BLOCK, BLOCK


def attend_kernel(kinds, fresh, first_lane, q_ref, low_ref, *rest):
    state = rest[-1]
    kept, refs = (None, rest[:-1]) if fresh else (rest[-2], rest[:-2])
    scale = HD**-0.5 * LOG2E
    first_query = place()[0] * BLOCK
    low_first = jnp.min(low_ref[0:1, 0:HD])
    parts, bases, none = [], [], True
    at, i = 0, 0
    for kind, shift in kinds:
        base, size = part_at(kind, shift)
        parts.append(refs[i].at[at : at + size])
        at += size
        if at == refs[i].shape[0]:
            at, i = 0, i + 1
        bases.append(base)
        none = (low_first >= base + size) & none

    width = state.shape[1]
    lanes = slice(first_lane, first_lane + width)

    def step():
        q = q_ref[:, lanes]
        low = low_ref[0:1, lanes]
        scores = []
        for part, base, kind in zip(parts, bases, kinds):
            s = jnp.dot(part[:, :HD], q, preferred_element_type=jnp.float32)
            at = lax.broadcasted_iota(jnp.int32, s.shape, 0)
            live = at >= low - base
            if kind == ("half", 0):
                lane = lax.broadcasted_iota(jnp.int32, (1, width), 1) + first_lane
                query = lane // (LANES // 2) * HALF + lane % HALF + first_query
                live = live & (at <= query - base)
            scores.append(jnp.where(live, s, MASKED))
        s = jnp.concatenate(scores, axis=0) if len(scores) > 1 else scores[0]
        values = [part[:, HD:].T for part in parts]
        values = jnp.concatenate(values, axis=1) if len(values) > 1 else values[0]
        values = jnp.concatenate([values, jnp.ones((16, values.shape[1]), jnp.bfloat16)], axis=0)
        peak = jnp.max(s, axis=0, keepdims=True) * scale
        old = jnp.full_like(peak, EMPTY) if fresh else kept[HD : HD + 1, lanes]
        new = jnp.maximum(old, peak)
        weights = jnp.exp2(s * scale - new).astype(jnp.bfloat16)
        summed = jnp.dot(values, weights, preferred_element_type=jnp.float32)
        denom = summed[HD : HD + 1]
        summed = summed[:HD]
        if not fresh:
            alpha = jnp.exp2(old - new)
            summed = summed + kept[:HD, lanes] * alpha
            denom = denom + kept[HD + 1 : HD + 2, lanes] * alpha
        state[:HD, :] = summed
        state[HD:, :] = jnp.concatenate([new, denom, jnp.zeros((6, width), jnp.float32)], axis=0)

    if fresh:
        step()
    else:

        @pl.when(none)
        def _():
            state[...] = kept[:, lanes]

        @pl.when(jnp.logical_not(none))
        def _():
            step()


def attend(q_all, low, refs, kinds, state=None, half=None):
    operands = list(refs) + ([] if state is None else [state])
    width, first_lane = (LANES, 0) if half is None else (LANES // 2, half * LANES // 2)
    in_place = state is not None and half is None
    return pl.pallas_call(
        functools.partial(attend_kernel, kinds, state is None, first_lane),
        out_shape=jax.ShapeDtypeStruct((STATE, width), jnp.float32),
        in_specs=[pl.BlockSpec(memory_space=pltpu.VMEM)] * (2 + len(operands)),
        out_specs=pl.BlockSpec(memory_space=pltpu.VMEM),
        input_output_aliases={1 + len(operands): 0} if in_place else {},
        compiler_params=pltpu.CompilerParams(vmem_limit_bytes=24 * MIB),
        cost_estimate=pl.CostEstimate(flops=1, bytes_accessed=1, transcendentals=0),
        name="attend",
    )(q_all, low, *operands)


def turn_kernel(queries, cosine, sine, out):
    heads = queries.shape[1] // HD
    for h in range(heads):
        x = queries[:, h * HD : (h + 1) * HD].astype(jnp.float32)
        turned = rope(x, cosine[...], sine[...]).astype(jnp.bfloat16).T
        for half in range(2):
            at = (half * heads + h) * HALF
            out[:, at : at + HALF] = turned[:, half * HALF : (half + 1) * HALF]


def turn(queries, cosine, sine):
    return pl.pallas_call(
        turn_kernel,
        out_shape=jax.ShapeDtypeStruct((HD, queries.shape[1] // HD * BLOCK), jnp.bfloat16),
        in_specs=[pl.BlockSpec(memory_space=pltpu.VMEM)] * 3,
        out_specs=pl.BlockSpec(memory_space=pltpu.VMEM),
        compiler_params=pltpu.CompilerParams(vmem_limit_bytes=16 * MIB),
        cost_estimate=pl.CostEstimate(flops=1, bytes_accessed=1, transcendentals=0),
        name="turn",
    )(queries, cosine, sine)


def merged(mine, theirs, out):
    for h in range(HEADS):
        a = slice(h * HALF, (h + 1) * HALF)
        g = (h + HEADS // 2) % HEADS
        b = slice(g * HALF, (g + 1) * HALF)
        peak_a, peak_b = mine[HD : HD + 1, a], theirs[HD : HD + 1, b]
        peak = jnp.maximum(peak_a, peak_b)
        scale_a, scale_b = jnp.exp2(peak_a - peak), jnp.exp2(peak_b - peak)
        denom = mine[HD + 1 : HD + 2, a] * scale_a + theirs[HD + 1 : HD + 2, b] * scale_b
        summed = mine[:HD, a] * scale_a + theirs[:HD, b] * scale_b
        out[:, h * HD : (h + 1) * HD] = (summed / denom).T.astype(jnp.bfloat16)


def project_kernel(other_side, first, merging, *rest):
    half = HEADS * HD // 2
    _, hi, core, _, _ = place()
    weights, sems = rest[-2:]
    if merging:
        mine, theirs, own_weight, other_weight, attended = rest[:5]
        outs = rest[5:-2]
    else:
        attended, own_weight, other_weight = rest[:3]
        outs = rest[3:-2]
    at = (2 * (1 - hi if other_side else hi) + core) * OUT_COLUMNS + first
    pieces = weights.shape[0]
    for i in range(pieces):
        columns = pl.ds(pl.multiple_of(at + i * TILE, TILE), TILE)
        for j, weight in enumerate((own_weight, other_weight)):
            pltpu.make_async_copy(weight.at[:, columns], weights.at[i, j], sems.at[i, j]).start()
    if merging:
        merged(mine, theirs, attended)
    out, filled = 0, 0
    for i in range(pieces):
        columns = pl.ds(pl.multiple_of(at + i * TILE, TILE), TILE)
        for j, weight in enumerate((own_weight, other_weight)):
            pltpu.make_async_copy(weight.at[:, columns], weights.at[i, j], sems.at[i, j]).wait()
        total = jnp.dot(attended[:, :half], weights[i, 0], preferred_element_type=jnp.float32)
        total += jnp.dot(attended[:, half:], weights[i, 1], preferred_element_type=jnp.float32)
        outs[out][:, filled : filled + TILE] = total.astype(outs[out].dtype)
        filled += TILE
        if filled == outs[out].shape[1]:
            out, filled = out + 1, 0


def project(operands, weights, other_side, first, widths, dtype, merging=False):
    half = HEADS * HD // 2
    shapes = [jax.ShapeDtypeStruct((HALF, width), dtype) for width in widths]
    if merging:
        shapes = [jax.ShapeDtypeStruct((HALF, 2 * half), jnp.bfloat16)] + shapes
    pieces = sum(widths) // TILE
    vmem = pl.BlockSpec(memory_space=pltpu.VMEM)
    return pl.pallas_call(
        functools.partial(project_kernel, other_side, first, merging),
        out_shape=shapes,
        in_specs=[vmem] * len(operands)
        + [pl.BlockSpec(memory_space=pltpu.HBM)] * 2,
        out_specs=[vmem] * len(shapes),
        scratch_shapes=[
            pltpu.VMEM((pieces, 2, half, TILE), jnp.bfloat16),
            pltpu.SemaphoreType.DMA((pieces, 2)),
        ],
        compiler_params=pltpu.CompilerParams(vmem_limit_bytes=16 * MIB),
        cost_estimate=pl.CostEstimate(flops=1, bytes_accessed=1, transcendentals=0),
        name="project",
    )(*operands, *weights)


def finish_kernel(kept, received, *rest):
    rest[-1][...] = (kept[...] + received[...].astype(jnp.float32)).astype(jnp.bfloat16)


def finish(kept, received, half, first, out):
    columns, start = received.shape[1], first // TILE
    in_specs = [
        pl.BlockSpec((HALF, TILE), lambda j: (0, start + j)),
        pl.BlockSpec((HALF, TILE), lambda j: (0, j)),
    ]
    operands = [kept, received]
    if out is not None:
        in_specs.append(pl.BlockSpec(memory_space=pl.ANY))
        operands.append(out)
    return pl.pallas_call(
        finish_kernel,
        out_shape=jax.ShapeDtypeStruct((BLOCK, OUT_COLUMNS), jnp.bfloat16),
        grid=(columns // TILE,),
        in_specs=in_specs,
        out_specs=pl.BlockSpec((HALF, TILE), lambda j: (half, start + j)),
        input_output_aliases={} if out is None else {2: 0},
        compiler_params=pltpu.CompilerParams(vmem_limit_bytes=16 * MIB),
        cost_estimate=pl.CostEstimate(flops=1, bytes_accessed=1, transcendentals=0),
        name="finish",
    )(*operands)


def body(queries, key_heads, value_heads, doc_lengths, out_weight):
    s = lax.axis_index("seq")
    t = lax.axis_index("tensor")
    hi, core = t // 2, t % 2

    query_pos = s * BLOCK + jnp.arange(BLOCK, dtype=jnp.int32)
    cosine, sine = rope_tables(query_pos)
    own_key = lax.dynamic_index_in_dim(key_heads, hi, 1, keepdims=False).astype(jnp.float32)
    own_key = rope(own_key, cosine, sine).astype(jnp.bfloat16)
    own_value = lax.dynamic_index_in_dim(value_heads, hi, 1, keepdims=False)
    block = jnp.concatenate([own_key, own_value], axis=1)

    q_own = turn(queries, cosine, sine)
    q_other = permute(q_own, other_core)
    near = [permute(block, along_rows(step)) for step in (1, 2)]
    far = permute(block, far_block)
    *near, far = lax.optimization_barrier((*near, far))
    half = lax.dynamic_slice_in_dim(block, core * (BLOCK // 2), BLOCK // 2, 0)
    group_1 = jnp.concatenate([half, *near], axis=0)
    near = jnp.concatenate(near, axis=0)
    near, block = lax.optimization_barrier((near, block))
    shifts = (1, -1, 2)
    group_2 = permute(near, two_rows_on)
    group_1, q_other, out_weight = lax.optimization_barrier((group_1, q_other, out_weight))
    other_weight = permute(out_weight, other_core)
    columns_1 = [permute(group_1, in_row(shift)) for shift in shifts]

    own_lanes = LANES // 4
    q_all = jnp.concatenate(
        [q[:, i * own_lanes : (i + 1) * own_lanes] for i in range(2) for q in (q_own, q_other)],
        axis=1,
    )
    doc_ends = jnp.cumsum(doc_lengths)
    low = jnp.max(jnp.where(doc_ends[:, None] <= query_pos[None], doc_ends[:, None], 0), axis=0)
    low = jnp.broadcast_to(low.reshape(2, 1, HALF), (8, 2, HEADS, HALF)).reshape(8, LANES)
    step = functools.partial(attend, q_all, low)

    state = step([half, near], [("half", 0), (1, 0), (2, 0)])
    rows_2 = lambda shift: [(3, shift), (4, shift)]
    group_2, state = lax.optimization_barrier((group_2, state))
    columns_2 = [permute(group_2, in_row(shift)) for shift in shifts]
    state = step([group_2], rows_2(0), state)
    for shift, keys in zip(shifts, columns_1):
        refs, kinds = [keys], [("half", shift), (1, shift), (2, shift)]
        if shift == 2:
            refs, kinds = refs + [far], kinds + [("far", 0)]
        state = step(refs, kinds, state)
    state, other_weight = lax.optimization_barrier((state, other_weight))
    weights = (out_weight, other_weight)
    state = step(columns_2[:1], rows_2(1), state)
    halves = []
    for half in range(2):
        mine = step(columns_2[1:], rows_2(-1) + rows_2(2), state, half)
        halves.append((mine, permute(mine, other_core)))

    sent, kept = [], []
    for half, (first, rest) in enumerate((((OUT_COLUMNS,), ()), ((1024,), (1024,)))):
        attended, partial = project(halves[half], weights, True, 0, first, jnp.bfloat16, True)
        partials = [partial]
        if rest:
            partials += project((attended,), weights, True, first[0], rest, jnp.bfloat16)
        sent.append([permute(partial, other_hi) for partial in partials])
        kept += project((attended,), weights, False, 0, (OUT_COLUMNS,), jnp.float32)
    out = None
    for half in range(2):
        first = 0
        for piece in sent[half]:
            out = finish(kept[half], piece, half, first, out)
            first += piece.shape[1]
    return out


def solution(mesh):
    return jax.shard_map(
        body,
        mesh=mesh,
        in_specs=(
            P("seq", "tensor"),
            P("seq", None, None),
            P("seq", None, None),
            P(),
            P("tensor", None),
        ),
        out_specs=P("seq", "tensor"),
        check_vma=False,
    )
```

```python
import functools
import math

import jax
import jax.numpy as jnp
from jax import lax
from jax.experimental import pallas as pl
from jax.experimental.pallas import tpu as pltpu
from jax.sharding import PartitionSpec as P

HQ = 16
KVH = 2
HD = 128
SEQ = 64
TENSOR = 4
ROW = 4
THETA = 500000.0
EMPTY = -1e30
MASKED = -1e32
LOG2E = math.log2(math.e)
BLOCK = 256
ROW_TOKENS = ROW * BLOCK
HEADS = 8
LANES = HEADS * BLOCK
STATE = HD + 8
TILE = 512
NOWHERE = -(1 << 24)
OUT_COLUMNS = 2048
MIB = 1024 * 1024


def device_perm(move):
    pairs = []
    for s in range(SEQ):
        for hi in range(2):
            for core in range(2):
                to = move(s, hi, core)
                if to is not None:
                    pairs.append((s * TENSOR + hi * 2 + core, to[0] * TENSOR + to[1] * 2 + to[2]))
    return pairs


def permute(x, move):
    return lax.ppermute(x, ("seq", "tensor"), device_perm(move))


def in_row(shift):
    return lambda s, hi, core: (s - s % ROW + (s + shift) % ROW, hi, core)


def other_core(s, hi, core):
    return s, hi, 1 - core


def other_hi(s, hi, core):
    return s, 1 - hi, core


def far_block(s, hi, core):
    if core == 0 and s % ROW == ROW - 1 and s + 33 < SEQ:
        return s + 33, hi, core
    return None


def along_rows(step):
    def move(s, hi, core):
        if core == 0:
            return (s + step * ROW, hi, core) if s + step * ROW < SEQ else None
        return (s + (9 - step) * ROW) % SEQ, hi, core

    return move


def two_rows_on(s, hi, core):
    if core == 0:
        return (s + 2 * ROW, hi, core) if s + 2 * ROW < SEQ else None
    return (s - 2 * ROW) % SEQ, hi, core


def rope_tables(positions):
    half = HD // 2
    exponents = jnp.arange(half, dtype=jnp.float32) * (2.0 / HD)
    inverse = jnp.power(jnp.float32(THETA), -exponents)
    angles = positions.astype(jnp.float32)[:, None] * inverse[None, :]
    return jnp.cos(angles), jnp.sin(angles)


def rope(values, cosine, sine):
    half = HD // 2
    first, second = values[..., :half], values[..., half:]
    return jnp.concatenate(
        [first * cosine - second * sine, second * cosine + first * sine], axis=-1
    )


def place():
    s, t = lax.axis_index("seq"), lax.axis_index("tensor")
    return s, t >> 1, t & 1, s >> 2, s & 3


def part_at(kind, shift):
    s, _, core, row, col = place()
    at = (col + ROW - shift) & 3
    if kind == "far":
        there = (core == 0) & (col == 0) & (s >= 33)
        return jnp.where(there, (s - 33) * BLOCK, NOWHERE), BLOCK
    if kind == "half":
        base = (row * ROW + at) * BLOCK + core * (BLOCK // 2)
        return jnp.where(at > col, NOWHERE, base), BLOCK // 2
    return (jnp.where(core == 0, row - kind, row - 9 + kind) * ROW + at) * BLOCK, BLOCK


def attend_kernel(kinds, fresh, q_ref, low_ref, *rest):
    state = rest[-1]
    kept, refs = (None, rest[:-1]) if fresh else (rest[-2], rest[:-2])
    scale = HD**-0.5 * LOG2E
    first_query = place()[0] * BLOCK
    low_first = jnp.min(low_ref[0:1, 0:HD])
    parts, bases, none = [], [], True
    at, i = 0, 0
    for kind, shift in kinds:
        base, size = part_at(kind, shift)
        parts.append(refs[i].at[at : at + size])
        at += size
        if at == refs[i].shape[0]:
            at, i = 0, i + 1
        bases.append(base)
        none = (low_first >= base + size) & none

    def step():
        q = q_ref[...]
        low = low_ref[0:1, :]
        scores = []
        for part, base, kind in zip(parts, bases, kinds):
            s = jnp.dot(part[:, :HD], q, preferred_element_type=jnp.float32)
            at = lax.broadcasted_iota(jnp.int32, s.shape, 0)
            live = at >= low - base
            if kind == ("half", 0):
                query = lax.broadcasted_iota(jnp.int32, (1, LANES), 1) % BLOCK + first_query
                live = live & (at <= query - base)
            scores.append(jnp.where(live, s, MASKED))
        s = jnp.concatenate(scores, axis=0) if len(scores) > 1 else scores[0]
        values = [part[:, HD:].T for part in parts]
        values = jnp.concatenate(values, axis=1) if len(values) > 1 else values[0]
        values = jnp.concatenate([values, jnp.ones((16, values.shape[1]), jnp.bfloat16)], axis=0)
        peak = jnp.max(s, axis=0, keepdims=True) * scale
        old = jnp.full_like(peak, EMPTY) if fresh else kept[HD : HD + 1, :]
        new = jnp.maximum(old, peak)
        weights = jnp.exp2(s * scale - new).astype(jnp.bfloat16)
        summed = jnp.dot(values, weights, preferred_element_type=jnp.float32)
        denom = summed[HD : HD + 1]
        summed = summed[:HD]
        if not fresh:
            alpha = jnp.exp2(old - new)
            summed = summed + kept[:HD, :] * alpha
            denom = denom + kept[HD + 1 : HD + 2, :] * alpha
        state[:HD, :] = summed
        state[HD:, :] = jnp.concatenate([new, denom, jnp.zeros((6, LANES), jnp.float32)], axis=0)

    if fresh:
        step()
    else:

        @pl.when(none)
        def _():
            state[...] = kept[...]

        @pl.when(jnp.logical_not(none))
        def _():
            step()


def attend(q_all, low, refs, kinds, state=None):
    operands = list(refs) + ([] if state is None else [state])
    return pl.pallas_call(
        functools.partial(attend_kernel, kinds, state is None),
        out_shape=jax.ShapeDtypeStruct((STATE, LANES), jnp.float32),
        in_specs=[pl.BlockSpec(memory_space=pltpu.VMEM)] * (2 + len(operands)),
        out_specs=pl.BlockSpec(memory_space=pltpu.VMEM),
        input_output_aliases={} if state is None else {1 + len(operands): 0},
        compiler_params=pltpu.CompilerParams(vmem_limit_bytes=32 * MIB),
        cost_estimate=pl.CostEstimate(flops=1, bytes_accessed=1, transcendentals=0),
        name="attend",
    )(q_all, low, *operands)


def turn_kernel(queries, cosine, sine, out):
    half = HD // 2
    for h in range(queries.shape[1] // HD):
        x = queries[:, h * HD : (h + 1) * HD].astype(jnp.float32)
        turned = rope(x, cosine[...], sine[...]).astype(jnp.bfloat16)
        out[:, h * BLOCK : (h + 1) * BLOCK] = turned.T


def turn(queries, cosine, sine):
    return pl.pallas_call(
        turn_kernel,
        out_shape=jax.ShapeDtypeStruct((HD, queries.shape[1] // HD * BLOCK), jnp.bfloat16),
        in_specs=[pl.BlockSpec(memory_space=pltpu.VMEM)] * 3,
        out_specs=pl.BlockSpec(memory_space=pltpu.VMEM),
        compiler_params=pltpu.CompilerParams(vmem_limit_bytes=16 * MIB),
        cost_estimate=pl.CostEstimate(flops=1, bytes_accessed=1, transcendentals=0),
        name="turn",
    )(queries, cosine, sine)


def merged(mine, theirs, out):
    for h in range(HEADS):
        a = slice(h * BLOCK, (h + 1) * BLOCK)
        g = (h + HEADS // 2) % HEADS
        b = slice(g * BLOCK, (g + 1) * BLOCK)
        peak_a, peak_b = mine[HD : HD + 1, a], theirs[HD : HD + 1, b]
        peak = jnp.maximum(peak_a, peak_b)
        scale_a, scale_b = jnp.exp2(peak_a - peak), jnp.exp2(peak_b - peak)
        denom = mine[HD + 1 : HD + 2, a] * scale_a + theirs[HD + 1 : HD + 2, b] * scale_b
        summed = mine[:HD, a] * scale_a + theirs[:HD, b] * scale_b
        out[:, h * HD : (h + 1) * HD] = (summed / denom).T.astype(jnp.bfloat16)


def project_kernel(other_side, first, merging, *rest):
    half = HEADS * HD // 2
    _, hi, core, _, _ = place()
    weights, sems = rest[-2:]
    if merging:
        mine, theirs, own_weight, other_weight, attended = rest[:5]
        outs = rest[5:-2]
    else:
        attended, own_weight, other_weight = rest[:3]
        outs = rest[3:-2]
    at = (2 * (1 - hi if other_side else hi) + core) * OUT_COLUMNS + first
    pieces = weights.shape[0]
    for i in range(pieces):
        columns = pl.ds(pl.multiple_of(at + i * TILE, TILE), TILE)
        for j, weight in enumerate((own_weight, other_weight)):
            pltpu.make_async_copy(weight.at[:, columns], weights.at[i, j], sems.at[i, j]).start()
    if merging:
        merged(mine, theirs, attended)
    out, filled = 0, 0
    for i in range(pieces):
        columns = pl.ds(pl.multiple_of(at + i * TILE, TILE), TILE)
        for j, weight in enumerate((own_weight, other_weight)):
            pltpu.make_async_copy(weight.at[:, columns], weights.at[i, j], sems.at[i, j]).wait()
        total = jnp.dot(attended[:, :half], weights[i, 0], preferred_element_type=jnp.float32)
        total += jnp.dot(attended[:, half:], weights[i, 1], preferred_element_type=jnp.float32)
        outs[out][:, filled : filled + TILE] = total.astype(outs[out].dtype)
        filled += TILE
        if filled == outs[out].shape[1]:
            out, filled = out + 1, 0


def project(operands, weights, other_side, first, widths, dtype, merging=False):
    half = HEADS * HD // 2
    shapes = [jax.ShapeDtypeStruct((BLOCK, width), dtype) for width in widths]
    if merging:
        shapes = [jax.ShapeDtypeStruct((BLOCK, 2 * half), jnp.bfloat16)] + shapes
    pieces = sum(widths) // TILE
    vmem = pl.BlockSpec(memory_space=pltpu.VMEM)
    return pl.pallas_call(
        functools.partial(project_kernel, other_side, first, merging),
        out_shape=shapes,
        in_specs=[vmem] * len(operands)
        + [pl.BlockSpec(memory_space=pltpu.HBM)] * 2,
        out_specs=[vmem] * len(shapes),
        scratch_shapes=[
            pltpu.VMEM((pieces, 2, half, TILE), jnp.bfloat16),
            pltpu.SemaphoreType.DMA((pieces, 2)),
        ],
        compiler_params=pltpu.CompilerParams(vmem_limit_bytes=32 * MIB),
        cost_estimate=pl.CostEstimate(flops=1, bytes_accessed=1, transcendentals=0),
        name="project",
    )(*operands, *weights)


def finish_kernel(kept, received, *rest):
    rest[-1][...] = (kept[...] + received[...].astype(jnp.float32)).astype(jnp.bfloat16)


def finish(kept, received, first, out):
    columns, start = received.shape[1], first // TILE
    tile = pl.BlockSpec((BLOCK, TILE), lambda j: (0, start + j))
    in_specs = [tile, pl.BlockSpec((BLOCK, TILE), lambda j: (0, j))]
    operands = [kept, received]
    if out is not None:
        in_specs.append(pl.BlockSpec(memory_space=pl.ANY))
        operands.append(out)
    return pl.pallas_call(
        finish_kernel,
        out_shape=jax.ShapeDtypeStruct(kept.shape, jnp.bfloat16),
        grid=(columns // TILE,),
        in_specs=in_specs,
        out_specs=tile,
        input_output_aliases={} if out is None else {2: 0},
        compiler_params=pltpu.CompilerParams(vmem_limit_bytes=32 * MIB),
        cost_estimate=pl.CostEstimate(
            flops=BLOCK * columns, bytes_accessed=8 * BLOCK * columns, transcendentals=0
        ),
        name="finish",
    )(*operands)


def body(queries, key_heads, value_heads, doc_lengths, out_weight):
    s = lax.axis_index("seq")
    t = lax.axis_index("tensor")
    hi, core = t // 2, t % 2

    query_pos = s * BLOCK + jnp.arange(BLOCK, dtype=jnp.int32)
    cosine, sine = rope_tables(query_pos)
    own_key = lax.dynamic_index_in_dim(key_heads, hi, 1, keepdims=False).astype(jnp.float32)
    own_key = rope(own_key, cosine, sine).astype(jnp.bfloat16)
    own_value = lax.dynamic_index_in_dim(value_heads, hi, 1, keepdims=False)
    block = jnp.concatenate([own_key, own_value], axis=1)

    q_own = turn(queries, cosine, sine)
    q_other = permute(q_own, other_core)
    near = [permute(block, along_rows(step)) for step in (1, 2)]
    far = permute(block, far_block)
    *near, far = lax.optimization_barrier((*near, far))
    half = lax.dynamic_slice_in_dim(block, core * (BLOCK // 2), BLOCK // 2, 0)
    group_1 = jnp.concatenate([half, *near], axis=0)
    near = jnp.concatenate(near, axis=0)
    group_1, near, q_other, out_weight = lax.optimization_barrier(
        (group_1, near, q_other, out_weight)
    )
    other_weight = permute(out_weight, other_core)
    shifts = (1, -1, 2)
    group_2 = permute(near, two_rows_on)
    columns_1 = [permute(group_1, in_row(shift)) for shift in shifts]

    q_all = jnp.concatenate([q_own, q_other], axis=1)
    doc_ends = jnp.cumsum(doc_lengths)
    low = jnp.max(jnp.where(doc_ends[:, None] <= query_pos[None], doc_ends[:, None], 0), axis=0)
    low = jnp.broadcast_to(low, (8, HEADS, BLOCK)).reshape(8, LANES)
    step = functools.partial(attend, q_all, low)

    state = step([half, near], [("half", 0), (1, 0), (2, 0)])
    rows_2 = lambda shift: [(3, shift), (4, shift)]
    group_2, state = lax.optimization_barrier((group_2, state))
    columns_2 = [permute(group_2, in_row(shift)) for shift in shifts]
    for shift, keys in zip(shifts, columns_1):
        refs, kinds = [keys], [("half", shift), (1, shift), (2, shift)]
        if shift == 1:
            refs, kinds = [group_2] + refs, rows_2(0) + kinds
        if shift == 2:
            refs, kinds = refs + [far], kinds + [("far", 0)]
        state = step(refs, kinds, state)
    state, other_weight = lax.optimization_barrier((state, other_weight))
    weights = (out_weight, other_weight)
    state = step(columns_2[:1], rows_2(1), state)
    state = step(columns_2[1:2], rows_2(-1), state)
    state = step(columns_2[2:], rows_2(2), state)

    theirs = permute(state, other_core)
    attended, partial = project((state, theirs), weights, True, 0, (512,), jnp.bfloat16, True)
    received = [permute(partial, other_hi)]
    for partial in project((attended,), weights, True, 512, (512,) * 3, jnp.bfloat16):
        received.append(permute(partial, other_hi))
    (kept,) = project((attended,), weights, False, 0, (OUT_COLUMNS,), jnp.float32)
    out, first = None, 0
    for piece in received:
        out = finish(kept, piece, first, out)
        first += piece.shape[1]
    return out


def solution(mesh):
    return jax.shard_map(
        body,
        mesh=mesh,
        in_specs=(
            P("seq", "tensor"),
            P("seq", None, None),
            P("seq", None, None),
            P(),
            P("tensor", None),
        ),
        out_specs=P("seq", "tensor"),
        check_vma=False,
    )
```

```python
import functools
import math

import jax
import jax.numpy as jnp
from jax import lax
from jax.experimental import pallas as pl
from jax.experimental.pallas import tpu as pltpu
from jax.sharding import PartitionSpec as P

HQ = 16
KVH = 2
HD = 128
SEQ = 64
TENSOR = 4
ROW = 4
THETA = 500000.0
EMPTY = -1e30
MASKED = -1e32
LOG2E = math.log2(math.e)
BLOCK = 256
ROW_TOKENS = ROW * BLOCK
HEADS = 8
LANES = HEADS * BLOCK
STATE = HD + 8
TILE = 512
NOWHERE = -(1 << 24)
OUT_COLUMNS = 2048
MIB = 1024 * 1024


def device_perm(move):
    pairs = []
    for s in range(SEQ):
        for hi in range(2):
            for core in range(2):
                to = move(s, hi, core)
                if to is not None:
                    pairs.append((s * TENSOR + hi * 2 + core, to[0] * TENSOR + to[1] * 2 + to[2]))
    return pairs


def permute(x, move):
    return lax.ppermute(x, ("seq", "tensor"), device_perm(move))


def in_row(shift):
    return lambda s, hi, core: (s - s % ROW + (s + shift) % ROW, hi, core)


def other_core(s, hi, core):
    return s, hi, 1 - core


def other_hi(s, hi, core):
    return s, 1 - hi, core


def far_block(s, hi, core):
    if core == 0 and s % ROW == ROW - 1 and s + 33 < SEQ:
        return s + 33, hi, core
    return None


def along_rows(step):
    def move(s, hi, core):
        if core == 0:
            return (s + step * ROW, hi, core) if s + step * ROW < SEQ else None
        return (s + (9 - step) * ROW) % SEQ, hi, core

    return move


def two_rows_on(s, hi, core):
    if core == 0:
        return (s + 2 * ROW, hi, core) if s + 2 * ROW < SEQ else None
    return (s - 2 * ROW) % SEQ, hi, core


def rope_tables(positions):
    half = HD // 2
    exponents = jnp.arange(half, dtype=jnp.float32) * (2.0 / HD)
    inverse = jnp.power(jnp.float32(THETA), -exponents)
    angles = positions.astype(jnp.float32)[:, None] * inverse[None, :]
    return jnp.cos(angles), jnp.sin(angles)


def rope(values, cosine, sine):
    half = HD // 2
    first, second = values[..., :half], values[..., half:]
    return jnp.concatenate(
        [first * cosine - second * sine, second * cosine + first * sine], axis=-1
    )


def place():
    s, t = lax.axis_index("seq"), lax.axis_index("tensor")
    return s, t >> 1, t & 1, s >> 2, s & 3


def part_at(kind, shift):
    s, _, core, row, col = place()
    at = (col + ROW - shift) & 3
    if kind == "far":
        there = (core == 0) & (col == 0) & (s >= 33)
        return jnp.where(there, (s - 33) * BLOCK, NOWHERE), BLOCK
    if kind == "half":
        base = (row * ROW + at) * BLOCK + core * (BLOCK // 2)
        return jnp.where(at > col, NOWHERE, base), BLOCK // 2
    return (jnp.where(core == 0, row - kind, row - 9 + kind) * ROW + at) * BLOCK, BLOCK


def attend_kernel(kinds, fresh, q_ref, low_ref, *rest):
    state = rest[-1]
    kept, refs = (None, rest[:-1]) if fresh else (rest[-2], rest[:-2])
    scale = HD**-0.5 * LOG2E
    first_query = place()[0] * BLOCK
    low_first = jnp.min(low_ref[0:1, 0:HD])
    parts, bases, none = [], [], True
    at, i = 0, 0
    for kind, shift in kinds:
        base, size = part_at(kind, shift)
        parts.append(refs[i].at[at : at + size])
        at += size
        if at == refs[i].shape[0]:
            at, i = 0, i + 1
        bases.append(base)
        none = (low_first >= base + size) & none

    def step():
        q = q_ref[...]
        low = low_ref[0:1, :]
        scores = []
        for part, base, kind in zip(parts, bases, kinds):
            s = jnp.dot(part[:, :HD], q, preferred_element_type=jnp.float32)
            at = lax.broadcasted_iota(jnp.int32, s.shape, 0)
            live = at >= low - base
            if kind == ("half", 0):
                query = lax.broadcasted_iota(jnp.int32, (1, LANES), 1) % BLOCK + first_query
                live = live & (at <= query - base)
            scores.append(jnp.where(live, s, MASKED))
        s = jnp.concatenate(scores, axis=0) if len(scores) > 1 else scores[0]
        values = [part[:, HD:].T for part in parts]
        values = jnp.concatenate(values, axis=1) if len(values) > 1 else values[0]
        values = jnp.concatenate([values, jnp.ones((16, values.shape[1]), jnp.bfloat16)], axis=0)
        peak = jnp.max(s, axis=0, keepdims=True) * scale
        old = jnp.full_like(peak, EMPTY) if fresh else kept[HD : HD + 1, :]
        new = jnp.maximum(old, peak)
        weights = jnp.exp2(s * scale - new).astype(jnp.bfloat16)
        summed = jnp.dot(values, weights, preferred_element_type=jnp.float32)
        denom = summed[HD : HD + 1]
        summed = summed[:HD]
        if not fresh:
            alpha = jnp.exp2(old - new)
            summed = summed + kept[:HD, :] * alpha
            denom = denom + kept[HD + 1 : HD + 2, :] * alpha
        state[:HD, :] = summed
        state[HD:, :] = jnp.concatenate([new, denom, jnp.zeros((6, LANES), jnp.float32)], axis=0)

    if fresh:
        step()
    else:

        @pl.when(none)
        def _():
            state[...] = kept[...]

        @pl.when(jnp.logical_not(none))
        def _():
            step()


def attend(q_all, low, refs, kinds, state=None):
    operands = list(refs) + ([] if state is None else [state])
    return pl.pallas_call(
        functools.partial(attend_kernel, kinds, state is None),
        out_shape=jax.ShapeDtypeStruct((STATE, LANES), jnp.float32),
        in_specs=[pl.BlockSpec(memory_space=pltpu.VMEM)] * (2 + len(operands)),
        out_specs=pl.BlockSpec(memory_space=pltpu.VMEM),
        input_output_aliases={} if state is None else {1 + len(operands): 0},
        compiler_params=pltpu.CompilerParams(vmem_limit_bytes=32 * MIB),
        cost_estimate=pl.CostEstimate(flops=1, bytes_accessed=1, transcendentals=0),
        name="attend",
    )(q_all, low, *operands)


def turn_kernel(queries, cosine, sine, out):
    half = HD // 2
    for h in range(queries.shape[1] // HD):
        x = queries[:, h * HD : (h + 1) * HD].astype(jnp.float32)
        turned = rope(x, cosine[...], sine[...]).astype(jnp.bfloat16)
        out[:, h * BLOCK : (h + 1) * BLOCK] = turned.T


def turn(queries, cosine, sine):
    return pl.pallas_call(
        turn_kernel,
        out_shape=jax.ShapeDtypeStruct((HD, queries.shape[1] // HD * BLOCK), jnp.bfloat16),
        in_specs=[pl.BlockSpec(memory_space=pltpu.VMEM)] * 3,
        out_specs=pl.BlockSpec(memory_space=pltpu.VMEM),
        compiler_params=pltpu.CompilerParams(vmem_limit_bytes=16 * MIB),
        cost_estimate=pl.CostEstimate(flops=1, bytes_accessed=1, transcendentals=0),
        name="turn",
    )(queries, cosine, sine)


def merged(mine, theirs, out):
    for h in range(HEADS):
        a = slice(h * BLOCK, (h + 1) * BLOCK)
        g = (h + HEADS // 2) % HEADS
        b = slice(g * BLOCK, (g + 1) * BLOCK)
        peak_a, peak_b = mine[HD : HD + 1, a], theirs[HD : HD + 1, b]
        peak = jnp.maximum(peak_a, peak_b)
        scale_a, scale_b = jnp.exp2(peak_a - peak), jnp.exp2(peak_b - peak)
        denom = mine[HD + 1 : HD + 2, a] * scale_a + theirs[HD + 1 : HD + 2, b] * scale_b
        summed = mine[:HD, a] * scale_a + theirs[:HD, b] * scale_b
        out[:, h * HD : (h + 1) * HD] = (summed / denom).T.astype(jnp.bfloat16)


def project_kernel(other_side, first, merging, *rest):
    half = HEADS * HD // 2
    _, hi, core, _, _ = place()
    weights, sems = rest[-2:]
    if merging:
        mine, theirs, own_weight, other_weight, attended = rest[:5]
        outs = rest[5:-2]
    else:
        attended, own_weight, other_weight = rest[:3]
        outs = rest[3:-2]
    at = (2 * (1 - hi if other_side else hi) + core) * OUT_COLUMNS + first
    pieces = weights.shape[0]
    for i in range(pieces):
        columns = pl.ds(pl.multiple_of(at + i * TILE, TILE), TILE)
        for j, weight in enumerate((own_weight, other_weight)):
            pltpu.make_async_copy(weight.at[:, columns], weights.at[i, j], sems.at[i, j]).start()
    if merging:
        merged(mine, theirs, attended)
    out, filled = 0, 0
    for i in range(pieces):
        columns = pl.ds(pl.multiple_of(at + i * TILE, TILE), TILE)
        for j, weight in enumerate((own_weight, other_weight)):
            pltpu.make_async_copy(weight.at[:, columns], weights.at[i, j], sems.at[i, j]).wait()
        total = jnp.dot(attended[:, :half], weights[i, 0], preferred_element_type=jnp.float32)
        total += jnp.dot(attended[:, half:], weights[i, 1], preferred_element_type=jnp.float32)
        outs[out][:, filled : filled + TILE] = total.astype(outs[out].dtype)
        filled += TILE
        if filled == outs[out].shape[1]:
            out, filled = out + 1, 0


def project(operands, weights, other_side, first, widths, dtype, merging=False):
    half = HEADS * HD // 2
    shapes = [jax.ShapeDtypeStruct((BLOCK, width), dtype) for width in widths]
    if merging:
        shapes = [jax.ShapeDtypeStruct((BLOCK, 2 * half), jnp.bfloat16)] + shapes
    pieces = sum(widths) // TILE
    vmem = pl.BlockSpec(memory_space=pltpu.VMEM)
    return pl.pallas_call(
        functools.partial(project_kernel, other_side, first, merging),
        out_shape=shapes,
        in_specs=[vmem] * len(operands)
        + [pl.BlockSpec(memory_space=pltpu.HBM)] * 2,
        out_specs=[vmem] * len(shapes),
        scratch_shapes=[
            pltpu.VMEM((pieces, 2, half, TILE), jnp.bfloat16),
            pltpu.SemaphoreType.DMA((pieces, 2)),
        ],
        compiler_params=pltpu.CompilerParams(vmem_limit_bytes=32 * MIB),
        cost_estimate=pl.CostEstimate(flops=1, bytes_accessed=1, transcendentals=0),
        name="project",
    )(*operands, *weights)


def finish_kernel(kept, received, *rest):
    rest[-1][...] = (kept[...] + received[...].astype(jnp.float32)).astype(jnp.bfloat16)


def finish(kept, received, first, out):
    columns, start = received.shape[1], first // TILE
    tile = pl.BlockSpec((BLOCK, TILE), lambda j: (0, start + j))
    in_specs = [tile, pl.BlockSpec((BLOCK, TILE), lambda j: (0, j))]
    operands = [kept, received]
    if out is not None:
        in_specs.append(pl.BlockSpec(memory_space=pl.ANY))
        operands.append(out)
    return pl.pallas_call(
        finish_kernel,
        out_shape=jax.ShapeDtypeStruct(kept.shape, jnp.bfloat16),
        grid=(columns // TILE,),
        in_specs=in_specs,
        out_specs=tile,
        input_output_aliases={} if out is None else {2: 0},
        compiler_params=pltpu.CompilerParams(vmem_limit_bytes=32 * MIB),
        cost_estimate=pl.CostEstimate(
            flops=BLOCK * columns, bytes_accessed=8 * BLOCK * columns, transcendentals=0
        ),
        name="finish",
    )(*operands)


def body(queries, key_heads, value_heads, doc_lengths, out_weight):
    s = lax.axis_index("seq")
    t = lax.axis_index("tensor")
    hi, core = t // 2, t % 2

    query_pos = s * BLOCK + jnp.arange(BLOCK, dtype=jnp.int32)
    cosine, sine = rope_tables(query_pos)
    own_key = lax.dynamic_index_in_dim(key_heads, hi, 1, keepdims=False).astype(jnp.float32)
    own_key = rope(own_key, cosine, sine).astype(jnp.bfloat16)
    own_value = lax.dynamic_index_in_dim(value_heads, hi, 1, keepdims=False)
    block = jnp.concatenate([own_key, own_value], axis=1)

    q_own = turn(queries, cosine, sine)
    q_other = permute(q_own, other_core)
    near = [permute(block, along_rows(step)) for step in (1, 2)]
    far = permute(block, far_block)
    *near, far = lax.optimization_barrier((*near, far))
    half = lax.dynamic_slice_in_dim(block, core * (BLOCK // 2), BLOCK // 2, 0)
    group_1 = jnp.concatenate([half, *near], axis=0)
    near = jnp.concatenate(near, axis=0)
    group_1, near, q_other, out_weight = lax.optimization_barrier(
        (group_1, near, q_other, out_weight)
    )
    other_weight = permute(out_weight, other_core)
    shifts = (1, -1, 2)
    group_2 = permute(near, two_rows_on)
    columns_1 = [permute(group_1, in_row(shift)) for shift in shifts]

    q_all = jnp.concatenate([q_own, q_other], axis=1)
    doc_ends = jnp.cumsum(doc_lengths)
    low = jnp.max(jnp.where(doc_ends[:, None] <= query_pos[None], doc_ends[:, None], 0), axis=0)
    low = jnp.broadcast_to(low, (8, HEADS, BLOCK)).reshape(8, LANES)
    step = functools.partial(attend, q_all, low)

    state = step([half, near], [("half", 0), (1, 0), (2, 0)])
    rows_2 = lambda shift: [(3, shift), (4, shift)]
    group_2, state = lax.optimization_barrier((group_2, state))
    columns_2 = [permute(group_2, in_row(shift)) for shift in shifts]
    state = step([group_2], rows_2(0), state)
    for shift, keys in zip(shifts, columns_1):
        refs, kinds = [keys], [("half", shift), (1, shift), (2, shift)]
        if shift == 2:
            refs, kinds = refs + [far], kinds + [("far", 0)]
        state = step(refs, kinds, state)
    state, other_weight = lax.optimization_barrier((state, other_weight))
    weights = (out_weight, other_weight)
    state = step(columns_2[:1], rows_2(1), state)
    state = step(columns_2[1:2], rows_2(-1), state)
    state = step(columns_2[2:], rows_2(2), state)

    theirs = permute(state, other_core)
    attended, partial = project((state, theirs), weights, True, 0, (512,), jnp.bfloat16, True)
    received = [permute(partial, other_hi)]
    for partial in project((attended,), weights, True, 512, (512,) * 3, jnp.bfloat16):
        received.append(permute(partial, other_hi))
    (kept,) = project((attended,), weights, False, 0, (OUT_COLUMNS,), jnp.float32)
    out, first = None, 0
    for piece in received:
        out = finish(kept, piece, first, out)
        first += piece.shape[1]
    return out


def solution(mesh):
    return jax.shard_map(
        body,
        mesh=mesh,
        in_specs=(
            P("seq", "tensor"),
            P("seq", None, None),
            P("seq", None, None),
            P(),
            P("tensor", None),
        ),
        out_specs=P("seq", "tensor"),
        check_vma=False,
    )
```
